512 devices in a mesh: virt: 32 (over y_lo, z), ao: 16 (over y_hi, x, core).
Axes of the slice: x: 4, y: 4 (y_hi: 2, y_lo: 2; y = y_hi * 2 + y_lo), z: 16, core: 2. Of those that a mesh axis runs over, the one named last changes fastest.
Arguments:
- density: bfloat16 [640, 640, 128], P('virt', 'ao'), may hold values from -6 to 6
- virt_coeff: bfloat16 [640, 1024], P('virt'), may hold values from -0.25 to 0.25
- block_coeff: bfloat16 [128, 1024], P('ao'), may hold values from -0.5 to 0.5
- ao_order: int32 [1024], replicated, may hold values from 0 to 1023, each once
Outputs:
- density_ao: bfloat16 [1024, 1024, 1024], P('ao', 'virt')
The draws below stay inside these ranges and needn't reach their ends.
Inputs may be any that keep to these rules, and one draw needn't show every extreme that they name: `ao_order`: each basis function appears exactly once.
All inputs are finite; a program needn't handle non-finite values.
Results may differ from the reference program's by a relative error of at most 0.0057.
Values may be sent and summed in bfloat16 or wider, within the bound.
A program may use at most 64 MiB of HBM per device.

```python
import jax
import jax.numpy as jnp
from jax import lax

V = 640
NAO = 1024
CB = 128


def shard_levels(key, dims, shards, least, largest):
    level, own = 1.0, jax.random.fold_in(key, 6)
    for dim, parts in shards:
        heights = jnp.exp(jax.random.uniform(jax.random.fold_in(own, dim), (parts,), jnp.float32, least / len(shards), largest / len(shards)))
        level = level * jnp.repeat(heights, dims[dim] // parts).reshape([-1 if axis == dim else 1 for axis in range(len(dims))])
    return level


def normal_values(stream_key, dims, scale, reach, shards=(), dtype=jnp.bfloat16):
    drawn = scale * jax.random.normal(stream_key, dims, jnp.float32)
    if shards:
        drawn = drawn * shard_levels(stream_key, dims, shards, -0.22, 0.18)
    return jnp.clip(drawn, -reach, reach).astype(dtype)


def setup_inputs(seed: int = 0) -> dict:
    key_of = jax.random.split(jax.random.key(seed), 5)
    density = normal_values(key_of[0], (V, V, CB), 1.0, 6.0, ((0, 32), (1, 16)))
    virt_coeff = normal_values(key_of[1], (V, NAO), V ** -0.5, 0.25, ((0, 32),))
    block_coeff = normal_values(key_of[2], (CB, NAO), CB ** -0.5, 0.5, ((0, 16),))
    ao_order = jax.random.permutation(key_of[3], NAO).astype(jnp.int32)
    return dict(density=density, virt_coeff=virt_coeff, block_coeff=block_coeff, ao_order=ao_order)


sigma_block = 64


def reference(density, virt_coeff, block_coeff, ao_order):
    coef_panel = jnp.take(block_coeff, ao_order, axis=1).astype(jnp.float32)
    blocks = coef_panel.reshape(CB, NAO // sigma_block, sigma_block).transpose(1, 0, 2)
    dense = density.astype(jnp.float32)
    coeffs = virt_coeff.astype(jnp.float32)

    def one_block(section):
        quarter = jnp.einsum("abc,cs->abs", dense, section).astype(jnp.bfloat16)
        halfway = jnp.einsum("abs,bn->asn", quarter.astype(jnp.float32), coeffs).astype(jnp.bfloat16)
        return jnp.einsum("asn,am->snm", halfway.astype(jnp.float32), coeffs).astype(jnp.bfloat16)

    return lax.map(one_block, blocks).reshape(NAO, NAO, NAO)
```

```python
import jax
import jax.numpy as jnp
from jax import lax
from jax.experimental import pallas as pl
from jax.experimental.pallas import tpu as pltpu
from jax.sharding import PartitionSpec as P

MESH = pl.DeviceIdType.MESH
BF = jnp.bfloat16
F32 = jnp.float32
TN = (((0,), (0,)), ((), ()))
NT = (((1,), (1,)), ((), ()))


def exchange(
    order_ref, d_ref, c_ref, b_ref, h_ref, cp_ref,
    dl, cl, bl, hot, pt, df, dp, cf, t1, s, r, rf, g, ta, hf,
    dss, dsr, css, csr, cps, cpr, ccs, ccr, bs, br, zs, zr, ps, pr, qs, qr, ks, kr, ls, lr,
):
    v, j = lax.axis_index("virt"), lax.axis_index("ao")
    y_lo, z = v // 16, v % 16
    core, x, y_hi = j % 2, (j // 2) % 4, j // 8
    y = 2 * y_hi + y_lo
    jc = j // 2
    lanes = pl.ds(pl.multiple_of(jc * 128, 128), 128)
    other = (v, j + 1 - 2 * core)

    def plane(d, sign):
        yy = (y + sign * (d // 4) + 4) % 4
        xx = (x + sign * (d % 4) + 4) % 4
        return yy, xx, (yy % 2) * 16 + z, (yy // 2) * 8 + xx * 2 + core

    def remote(src, dst, send, recv, dev):
        return pltpu.make_async_remote_copy(
            src_ref=src, dst_ref=dst, send_sem=send, recv_sem=recv, device_id=dev, device_id_type=MESH
        )

    barrier = pltpu.get_barrier_semaphore()

    @pl.loop(1, 16)
    def _(t):
        pl.semaphore_signal(barrier, inc=1, device_id=(v, (j + t) % 16), device_id_type=MESH)
        pl.semaphore_signal(barrier, inc=1, device_id=(y_lo * 16 + (z + t) % 16, j), device_id_type=MESH)

    @pl.loop(1, 16)
    def _(t):
        yy, xx, vv, jj = plane(t, 1)

        @pl.when(yy % 2 != y_lo)
        def _():
            pl.semaphore_signal(barrier, inc=1, device_id=(vv, jj), device_id_type=MESH)

    pl.semaphore_wait(barrier, 38)

    def c_z(t):
        return remote(c_ref.at[:, lanes], cl.at[core, y, x, z // 2], css.at[t], csr.at[z // 2],
                      (y_lo * 16 + (z + t) % 16, j))

    @pl.when(z % 2 == core)
    def _():
        @pl.loop(1, 16)
        def _(t):
            c_z(t).start()

        cl[core, y, x, z // 2] = c_ref[:, lanes]

    def d_a(t, u):
        jj = (j + t) % 16
        src = d_ref.at[jj] if u == 0 else d_ref.at[16 + jj // 4]
        return remote(src, dl.at[u, j], dss.at[u, t], dsr.at[u, t], (v, jj))

    @pl.loop(1, 16)
    def _(t):
        d_a(t, 0).start()
        d_a(t, 1).start()

    dl[0, j] = d_ref[j]
    dl[1, j] = d_ref[16 + j // 4]

    @pl.loop(0, 8)
    def _(zz):
        @pl.when(2 * zz + core != z)
        def _():
            remote(c_ref.at[:, lanes], cl.at[core, y, x, zz], css.at[0], csr.at[zz], other).wait_recv()

    def c_p(d, slot_y, slot_x, dev):
        blk = cl.at[core, slot_y, slot_x]
        return remote(blk, blk, cps.at[d], cpr.at[d], dev)

    def c_c(d, k, slot_y, slot_x):
        blk = cl.at[k, slot_y, slot_x]
        return remote(blk, blk, ccs.at[d], ccr.at[d], other)

    @pl.loop(1, 16)
    def _(d):
        yy, xx, vv, jj = plane(d, 1)
        c_p(d, y, x, (vv, jj)).start()

    c_c(0, core, y, x).start()

    def b_a(t):
        return remote(b_ref, bl.at[j], bs.at[t], br.at[t], (v, (j + t) % 16))

    @pl.loop(1, 16)
    def _(t):
        b_a(t).start()

    bl[j] = b_ref[...]

    column = lax.broadcasted_iota(jnp.int32, (1, 1024), 1)

    @pl.loop(0, 64)
    def _(k):
        hot[pl.ds(k, 1), :] = jnp.where(column == order_ref[j * 64 + k], 1.0, 0.0).astype(F32)

    @pl.loop(1, 16)
    def _(t):
        frm = (j - t + 16) % 16
        for u in range(2):
            remote(d_ref.at[0], dl.at[u, frm], dss.at[u, t], dsr.at[u, t], other).wait_recv()

    for u in range(2):
        for jj in range(16):
            df[u, pl.ds(jj * 40, 40), :] = dl[u, jj].astype(F32)
        for q in range(40):
            dp[u, pl.ds(q * 16, 16), :] = df[u, pl.ds((q // 20) * 320 + q % 20, 16, stride=20), :].astype(BF)

    @pl.loop(1, 16)
    def _(d):
        yy, xx, vv, jj = plane(d, -1)
        c_p(d, yy, xx, other).wait_recv()
        c_c(d, core, yy, xx).start()

    @pl.loop(0, 16)
    def _(d):
        yy, xx, vv, jj = plane(d, -1)
        c_c(d, 1 - core, yy, xx).wait_recv()

    @pl.loop(0, 8)
    def _(q):
        xx, yh = q % 4, q // 4
        for yl in range(2):
            for zz in range(16):
                cf[yl * 16 + zz, pl.ds(0, 20), :] = cl[zz % 2, 2 * yh + yl, xx, zz // 2].astype(F32)
        flat = cf.reshape(32 * 24, 128)
        for k in range(40):
            cp_ref[pl.ds(k * 16, 16), pl.ds(pl.multiple_of(q * 128, 128), 128)] = flat[
                pl.ds((k // 20) * 384 + k % 20, 16, stride=24), :
            ].astype(BF)

    @pl.loop(0, 8)
    def _(q):
        yl, z4 = q // 4, (q % 4) * 4
        cols = cp_ref[:, pl.ds(pl.multiple_of(q * 128, 128), 128)]
        for u in range(2):
            tt = lax.dot_general(dp[u], cols, TN, preferred_element_type=F32)
            tt = tt.T.astype(BF)
            for e in range(4):
                if u == 0:
                    s[z4 + e, pl.ds(pl.multiple_of(yl * 32, 32), 32), :] = tt[e * 32:(e + 1) * 32]
                else:
                    t1[yl * 2, z4 + e] = tt[e * 32:e * 32 + 16]
                    t1[yl * 2 + 1, z4 + e] = tt[e * 32 + 16:e * 32 + 32]

    for zz in range(16):
        s[zz, pl.ds(64, 16), :] = t1[j % 4, zz]

    def t_z(t):
        zz = (z + t) % 16
        return remote(s.at[zz], r.at[z], zs.at[t], zr.at[t], (y_lo * 16 + zz, j))

    @pl.loop(0, 15)
    def _(w):
        t_z((16 + (w // 2 + 1) * (1 - 2 * (w % 2))) % 16).start()

    r[z] = s[z]

    @pl.loop(1, 16)
    def _(t):
        remote(b_ref, bl.at[(j - t + 16) % 16], bs.at[t], br.at[t], other).wait_recv()

    pt[...] = lax.dot_general(
        hot[...].astype(BF), bl[...].reshape(128, 1024), NT, preferred_element_type=F32
    ).astype(BF)

    @pl.loop(1, 16)
    def _(t):
        remote(s.at[0], r.at[(z - t + 16) % 16], zs.at[t], zr.at[t], other).wait_recv()

    for zz in range(16):
        rf[pl.ds(zz * 80, 80), :] = r[zz].astype(F32)
    for k in range(80):
        g[k] = rf[pl.ds(k, 16, stride=80), :].astype(BF)

    def rows(yl, jj, shared):
        base = yl * 20 + (16 + jj // 4 if shared else jj)
        return pl.ds(pl.multiple_of(base * 16, 16), 16)

    def t_p(d, dy_lo, dev):
        return remote(g.at[pl.ds(dy_lo * 32, 32)], ta.at[pl.ds(0, 32), rows(y_lo, j, False), :], ps.at[d], pr.at[d], dev)

    def t_q(d, dev):
        return remote(g.at[pl.ds(64, 16)], ta.at[pl.ds((j % 2) * 16, 16), rows(y_lo, j, True), :], qs.at[d], qr.at[d], dev)

    def t_k(d, sv, sj):
        blk = ta.at[pl.ds(0, 32), rows(sv // 16, sj, False), :]
        return remote(blk, blk, ks.at[d], kr.at[d], other)

    def t_l(d, sv, sj):
        blk = ta.at[pl.ds((sj % 2) * 16, 16), rows(sv // 16, sj, True), :]
        return remote(blk, blk, ls.at[d], lr.at[d], other)

    def shared_to(yl, jj):
        return (jj % 4) // 2 == yl

    @pl.loop(1, 16)
    def _(d):
        yy, xx, vv, jj = plane(d, 1)
        t_p(d, yy % 2, (vv, jj)).start()

        @pl.when(shared_to(yy % 2, j))
        def _():
            t_q(d, (vv, jj)).start()

    ta[:, rows(y_lo, j, False), :] = g[pl.ds(y_lo * 32, 32)]
    t_k(0, v, j).start()

    @pl.when(shared_to(y_lo, j))
    def _():
        ta[pl.ds((j % 2) * 16, 16), rows(y_lo, j, True), :] = g[pl.ds(64, 16)]
        t_l(0, v, j).start()

    @pl.loop(1, 16)
    def _(d):
        yy, xx, vv, jj = plane(d, -1)
        remote(g.at[pl.ds(0, 32)], ta.at[pl.ds(0, 32), rows(yy % 2, jj, False), :], ps.at[d], pr.at[d], other).wait_recv()
        t_k(d, vv, jj).start()

        @pl.when(shared_to(y_lo, jj))
        def _():
            remote(g.at[pl.ds(64, 16)], ta.at[pl.ds((jj % 2) * 16, 16), rows(yy % 2, jj, True), :],
                   qs.at[d], qr.at[d], other).wait_recv()
            t_l(d, vv, jj).start()

    @pl.loop(0, 16)
    def _(d):
        yy, xx, vv, jj = plane(d, -1)
        peer = jj + 1 - 2 * core
        t_k(d, vv, peer).wait_recv()

        @pl.when(shared_to(y_lo, peer))
        def _():
            t_l(d, vv, peer).wait_recv()

    @pl.loop(0, 32)
    def _(n):
        part = lax.dot_general(pt[...], ta[n], NT, preferred_element_type=F32)
        for k in range(5):
            hf[k, pl.ds(n, 64, stride=32), :] = part[:, k * 128:(k + 1) * 128]

    @pl.loop(0, 16)
    def _(k):
        part = pl.ds(pl.multiple_of(k * 128, 128), 128)
        for q in range(5):
            h_ref[part, q * 128:(q + 1) * 128] = hf[q, part, :].astype(BF)

    @pl.when(z % 2 == core)
    def _():
        @pl.loop(1, 16)
        def _(t):
            c_z(t).wait_send()

    @pl.loop(1, 16)
    def _(t):
        d_a(t, 0).wait_send()
        d_a(t, 1).wait_send()
        c_p(t, y, x, other).wait_send()
        b_a(t).wait_send()
        t_z(t).wait_send()
        yy, xx, vv, jj = plane(t, 1)
        t_p(t, yy % 2, (vv, jj)).wait_send()

        @pl.when(shared_to(yy % 2, j))
        def _():
            t_q(t, (vv, jj)).wait_send()

    @pl.loop(0, 16)
    def _(d):
        yy, xx, vv, jj = plane(d, -1)
        c_c(d, core, yy, xx).wait_send()
        t_k(d, vv, jj).wait_send()

        @pl.when(shared_to(y_lo, jj))
        def _():
            t_l(d, vv, jj).wait_send()


def shards(density, virt_coeff, block_coeff, ao_order):
    vmem = pl.BlockSpec(memory_space=pltpu.VMEM)
    dma = pltpu.SemaphoreType.DMA
    half, coeff = pl.pallas_call(
        exchange,
        out_shape=(jax.ShapeDtypeStruct((2048, 640), BF), jax.ShapeDtypeStruct((640, 1024), BF)),
        in_specs=[pl.BlockSpec(memory_space=pltpu.SMEM), vmem, vmem, vmem],
        out_specs=(vmem, vmem),
        scratch_shapes=[
            pltpu.VMEM((2, 16, 40, 128), BF),
            pltpu.VMEM((2, 4, 4, 8, 20, 128), BF),
            pltpu.VMEM((16, 8, 1024), BF),
            pltpu.VMEM((64, 1024), F32),
            pltpu.VMEM((64, 128), BF),
            pltpu.VMEM((2, 640, 128), F32),
            pltpu.VMEM((2, 640, 128), BF),
            pltpu.VMEM((32, 24, 128), F32),
            pltpu.VMEM((4, 16, 16, 128), BF),
            pltpu.VMEM((16, 80, 128), BF),
            pltpu.VMEM((16, 80, 128), BF),
            pltpu.VMEM((1280, 128), F32),
            pltpu.VMEM((80, 16, 128), BF),
            pltpu.VMEM((32, 640, 128), BF),
            pltpu.VMEM((5, 2048, 128), F32),
            dma((2, 16)), dma((2, 16)),
            dma((16,)), dma((8,)),
            dma((16,)), dma((16,)),
            dma((16,)), dma((16,)),
            dma((16,)), dma((16,)),
            dma((16,)), dma((16,)),
            dma((16,)), dma((16,)),
            dma((16,)), dma((16,)),
            dma((16,)), dma((16,)),
            dma((16,)), dma((16,)),
        ],
        compiler_params=pltpu.CompilerParams(
            collective_id=0, has_side_effects=True, vmem_limit_bytes=48 * 1024 * 1024
        ),
    )(ao_order, density, virt_coeff, block_coeff)
    out = jnp.dot(half, coeff, preferred_element_type=F32).astype(BF)
    return out.reshape(64, 32, 1024)


def solution(mesh):
    return jax.shard_map(
        shards,
        mesh=mesh,
        in_specs=(P("virt", "ao", None), P("virt", None), P("ao", None), P()),
        out_specs=P("ao", "virt", None),
        check_vma=False,
    )
```

```python
import jax
import jax.numpy as jnp
from jax import lax
from jax.experimental import pallas as pl
from jax.experimental.pallas import tpu as pltpu
from jax.sharding import PartitionSpec as P

MESH = pl.DeviceIdType.MESH
BF = jnp.bfloat16
F32 = jnp.float32
TN = (((0,), (0,)), ((), ()))
NT = (((1,), (1,)), ((), ()))
STEPS = 4
BLOCKS = [(y % 2, (y // 2) * 8 + x * 2 + c) for c in range(2) for x in range(4) for y in range(4)]
BLOCKS += [(y % 2, 16 + (y // 2) * 2 + h) for h in range(2) for y in range(4)]


def exchange(
    order_hbm, d_ref, c_ref, b_ref, o_ref,
    order, dl, cl, bl, hot, pt, df, dp, cf, cp, s, sh, r, rh, rf, g, gh, ta, hf, hb, ob,
    order_sem, ob_sem, ds, dr, bs, br, zcs, zcr, ycs, ycr, xcs, xcr, fcs, fcr, kcs, kcr,
    zs, zr, ys, yr, xs, xr, fs, fr, ks, kr, zhs, zhr, yhs, yhr, xhs, xhr, fhs, fhr, khs, khr,
):
    v, j = lax.axis_index("virt"), lax.axis_index("ao")
    y_lo, z = v // 16, v % 16
    core, x, y_hi = j % 2, (j // 2) % 4, j // 8
    y = 2 * y_hi + y_lo
    share = j % 4
    right, left, far = (x + 1) % 4, (x + 3) % 4, (x + 2) % 4
    lanes = pl.ds(pl.multiple_of((j // 2) * 128, 128), 128)

    def dev(yy, xx):
        return (yy % 2) * 16 + z, (yy // 2) * 8 + xx * 2 + core

    other = (v, j + 1 - 2 * core)
    to_right, to_left = dev(y, right), dev(y, left)

    def remote(src, dst, send, recv, device):
        return pltpu.make_async_remote_copy(
            src_ref=src, dst_ref=dst, send_sem=send, recv_sem=recv, device_id=device, device_id_type=MESH
        )

    def arrived(ref, sem):
        remote(ref, ref, sem, sem, other).wait_recv()

    def left_for(ref, sem):
        remote(ref, ref, sem, sem, other).wait_send()

    order_copy = pltpu.make_async_copy(order_hbm, order, order_sem)
    order_copy.start()

    barrier = pltpu.get_barrier_semaphore()
    for dy in (1, 3):
        pl.semaphore_signal(barrier, inc=1, device_id=dev((y + dy) % 4, x), device_id_type=MESH)

    @pl.loop(1, 16)
    def _(t):
        pl.semaphore_signal(barrier, inc=1, device_id=(y_lo * 16 + (z + t) % 16, j), device_id_type=MESH)
        pl.semaphore_signal(barrier, inc=1, device_id=(v, (j + t) % 16), device_id_type=MESH)

    pl.semaphore_wait(barrier, 32)

    @pl.when(z % 2 == core)
    def _():
        @pl.loop(1, 16)
        def _(t):
            remote(c_ref.at[:, lanes], cl.at[core, x, y, z // 2], zcs.at[t], zcr, (y_lo * 16 + (z + t) % 16, j)).start()

        pltpu.make_async_copy(c_ref.at[:, lanes], cl.at[core, x, y, z // 2], zcr).start()

    @pl.loop(1, 16)
    def _(t):
        jj = (j + t) % 16
        remote(d_ref.at[jj], dl.at[0, j], ds, dr, (v, jj)).start()
        remote(d_ref.at[16 + jj // 4], dl.at[1, j], ds, dr, (v, jj)).start()

    pltpu.make_async_copy(d_ref.at[j], dl.at[0, j], dr).start()
    pltpu.make_async_copy(d_ref.at[16 + j // 4], dl.at[1, j], dr).start()

    order_copy.wait()
    column = lax.broadcasted_iota(jnp.int32, (1, 1024), 1)

    @pl.loop(0, 64)
    def _(k):
        hot[pl.ds(k, 1), :] = jnp.where(column == order[j * 64 + k], 1.0, 0.0).astype(F32)

    mine = cl.at[core, x, y]
    arrived(mine, zcr)
    for dy in (1, 3, 2):
        remote(mine, mine, ycs, ycr, dev((y + dy) % 4, x)).start()

    arrived(dl, dr)
    for u in range(2):
        for jj in range(16):
            df[u, pl.ds(jj * 40, 40), :] = dl[u, jj].astype(F32)
        for q, (yl, i) in enumerate(BLOCKS):
            dp[pl.ds(q * 16, 16), pl.ds(u * 128, 128)] = df[u, pl.ds(yl * 320 + i, 16, stride=20), :].astype(BF)

    arrived(cl.at[core, x, pl.ds(0, 3)], ycr)
    column_blocks = cl.at[core, x]
    remote(column_blocks, column_blocks, xcs.at[0], xcr.at[0], to_right).start()
    remote(column_blocks, column_blocks, xcs.at[1], xcr.at[1], to_left).start()

    def coeff_to_core(e, xx):
        blk = cl.at[core, xx]
        remote(blk, blk, kcs.at[e], kcr.at[e], other).start()

    def make_t(e, xx):
        arrived(cl.at[1 - core, xx], kcr.at[e])

        for yh in range(2):
            for yl in range(2):
                for zz in range(16):
                    cf[yl * 16 + zz, pl.ds(0, 20), :] = cl[zz % 2, xx, 2 * yh + yl, zz // 2].astype(F32)
            flat = cf.reshape(32 * 24, 128)
            lane = pl.ds(pl.multiple_of((yh * 4 + xx) * 128, 128), 128)
            for q, (yl, i) in enumerate(BLOCKS):
                cp[pl.ds(q * 16, 16), lane] = flat[pl.ds(yl * 384 + i, 16, stride=24), :].astype(BF)
            tt = lax.dot_general(cp[:, lane], dp[...], TN, preferred_element_type=F32).astype(BF)
            for q in range(4):
                for k in range(STEPS):
                    rows = tt[q * 32 + k * 8:q * 32 + k * 8 + 8]
                    s[k, xx * 4 + q, pl.ds(yh * 8, 8), :] = rows[:, :128]
                    sh[k, xx * 4 + q, pl.ds(yh * 8, 8), :] = rows[:, 128:]

    coeff_to_core(0, x)
    make_t(0, x)
    blk = cl.at[core, left]
    arrived(blk, xcr.at[0])
    remote(cl.at[core, left, pl.ds(0, 2)], cl.at[core, left, pl.ds(0, 2)], fcs.at[0], fcr.at[0], to_right).start()
    coeff_to_core(1, left)
    blk = cl.at[core, right]
    arrived(blk, xcr.at[1])
    remote(cl.at[core, right, pl.ds(2, 2)], cl.at[core, right, pl.ds(2, 2)], fcs.at[1], fcr.at[1], to_left).start()
    coeff_to_core(2, right)
    make_t(1, left)
    arrived(cl.at[core, far, pl.ds(0, 2)], fcr.at[0])
    arrived(cl.at[core, far, pl.ds(2, 2)], fcr.at[1])
    coeff_to_core(3, far)
    make_t(2, right)
    make_t(3, far)

    for k in range(STEPS):
        @pl.loop(0, 15)
        def _(w):
            zz = (z + 16 + (w // 2 + 1) * (1 - 2 * (w % 2))) % 16
            remote(s.at[k, zz], r.at[k, z], zs.at[k], zr.at[k], (y_lo * 16 + zz, j)).start()

        r[k, z] = s[k, z]

        @pl.when(share == k)
        def _():
            @pl.loop(0, 15)
            def _(w):
                zz = (z + 16 + (w // 2 + 1) * (1 - 2 * (w % 2))) % 16
                remote(sh.at[k, zz], rh.at[z], zhs, zhr, (y_lo * 16 + zz, j)).start()

            rh[z] = sh[k, z]

    @pl.loop(1, 16)
    def _(t):
        remote(b_ref, bl.at[j], bs, br, (v, (j + t) % 16)).start()

    pltpu.make_async_copy(b_ref, bl.at[j], br).start()

    def at(block, count=1):
        return pl.ds(pl.multiple_of(block * 16, 16), count * 16)

    def piece(k):
        return pl.ds(k * 8, 8)

    def turn(src, dst):
        for zz in range(16):
            rf[pl.ds(zz * 16, 16), :] = src[zz].astype(F32)
        for i in range(16):
            dst[i // 8, i % 8] = rf[pl.ds(i, 16, stride=16), :].astype(BF)

    own = core * 16 + x * 4
    pool = 32 + (x // 2) * 4

    def along_y(k):
        arrived(r.at[k, pl.ds(0, 15)], zr.at[k])
        turn(r.at[k], g.at[k])
        to = ta.at[piece(k), at(own + y), :]
        for dy in (1, 3, 2):
            half = y_lo if dy == 2 else 1 - y_lo
            remote(g.at[k, half], to, ys.at[k], yr.at[k], dev((y + dy) % 4, x)).start()
        ta[piece(k), at(own + y), :] = g[k, y_lo]

        @pl.when(share == k)
        def _():
            arrived(rh.at[pl.ds(0, 15)], zhr)
            turn(rh, gh)
            to_pool = ta.at[piece(k), at(pool + y), :]
            for dy in (1, 3, 2):
                half = y_lo if dy == 2 else 1 - y_lo
                remote(gh.at[half], to_pool, yhs, yhr, dev((y + dy) % 4, x)).start()
            ta[piece(k), at(pool + y), :] = gh[y_lo]

    def main(k, xx, first=0, count=4):
        return ta.at[piece(k), at(core * 16 + xx * 4 + first, count), :]

    def pooled(k, xx, first=0, count=4):
        return ta.at[piece(k), at(32 + (xx // 2) * 4 + first, count), :]

    def to_core(k, xx):
        blk = main(k, xx)
        remote(blk, blk, ks.at[k], kr.at[k], other).start()

    def along_x(k):
        arrived(main(k, x, 0, 3), yr.at[k])
        blk = main(k, x)
        remote(blk, blk, xs.at[k, 0], xr.at[k, 0], to_right).start()
        remote(blk, blk, xs.at[k, 1], xr.at[k, 1], to_left).start()

        @pl.when(share == k)
        def _():
            arrived(pooled(k, x, 0, 3), yhr)
            blk = pooled(k, x)
            remote(blk, blk, xhs.at[0], xhr.at[0], to_right).start()
            remote(blk, blk, xhs.at[1], xhr.at[1], to_left).start()

        to_core(k, x)

    def between(k):
        return jnp.logical_and(core == k % 2, x % 2 != k // 2)

    def pass_on(k):
        arrived(main(k, left), xr.at[k, 0])
        blk = main(k, left, 0, 2)
        remote(blk, blk, fs.at[k, 0], fr.at[k, 0], to_right).start()
        arrived(main(k, right), xr.at[k, 1])
        blk = main(k, right, 2, 2)
        remote(blk, blk, fs.at[k, 1], fr.at[k, 1], to_left).start()

        @pl.when(between(k))
        def _():
            arrived(pooled(k, left), xhr.at[0])
            blk = pooled(k, left, 0, 2)
            remote(blk, blk, fhs.at[0], fhr.at[0], to_right).start()
            arrived(pooled(k, right), xhr.at[1])
            blk = pooled(k, right, 2, 2)
            remote(blk, blk, fhs.at[1], fhr.at[1], to_left).start()

        to_core(k, left)
        to_core(k, right)

    def last(k):
        arrived(main(k, far, 0, 2), fr.at[k, 0])
        arrived(main(k, far, 2, 2), fr.at[k, 1])
        to_core(k, far)

        @pl.when(share == k)
        def _():
            arrived(pooled(k, far, 0, 2), fhr.at[0])
            arrived(pooled(k, far, 2, 2), fhr.at[1])

        @pl.when(core == k % 2)
        def _():
            blk = ta.at[piece(k), at(32, 8), :]
            remote(blk, blk, khs.at[k], khr.at[k], other).start()

    def finish(k):
        arrived(ta.at[piece(k), at((1 - core) * 16, 16), :], kr.at[k])

        @pl.when(core != k % 2)
        def _():
            arrived(ta.at[piece(k), at(32, 8), :], khr.at[k])

        for n in range(8):
            part = lax.dot_general(pt[...], ta[k * 8 + n], NT, preferred_element_type=F32)
            for q in range(5):
                hf[q, pl.ds(n, 64, stride=8), :] = part[:, q * 128:(q + 1) * 128]
        for q in range(5):
            hb[:, pl.ds(q * 128, 128)] = hf[q].astype(BF)

        @pl.loop(0, 4)
        def _(q):
            cols = pl.ds(pl.multiple_of(q * 256, 256), 256)
            out = jnp.dot(hb[...], cp[:, cols], preferred_element_type=F32).astype(BF)
            ob[k // 2, :, pl.ds((k % 2) * 8, 8), cols] = out.reshape(64, 8, 256)

        if k % 2 == 1:
            pltpu.make_async_copy(ob.at[k // 2], o_ref.at[:, pl.ds(k // 2 * 16, 16), :], ob_sem.at[k // 2]).start()

    for t in range(STEPS + 4):
        if 0 <= t - 1 < STEPS:
            along_x(t - 1)
        if t < STEPS:
            along_y(t)
        if 0 <= t - 2 < STEPS:
            pass_on(t - 2)
        if 0 <= t - 3 < STEPS:
            last(t - 3)
        if t == 3:
            arrived(bl, br)
            pt[...] = lax.dot_general(
                hot[...].astype(BF), bl[...].reshape(128, 1024), NT, preferred_element_type=F32
            ).astype(BF)
        if 0 <= t - 4 < STEPS:
            finish(t - 4)

    @pl.when(z % 2 == core)
    def _():
        @pl.loop(1, 16)
        def _(t):
            left_for(c_ref.at[:, lanes], zcs.at[t])

    left_for(dl.at[:, pl.ds(0, 15)], ds)
    left_for(bl.at[pl.ds(0, 15)], bs)
    left_for(cl.at[core, x, pl.ds(0, 3)], ycs)
    for e in range(2):
        left_for(cl.at[core, x], xcs.at[e])
        left_for(cl.at[core, x, pl.ds(0, 2)], fcs.at[e])
    for e in range(4):
        left_for(cl.at[core, x], kcs.at[e])
    left_for(rh.at[pl.ds(0, 15)], zhs)
    left_for(main(0, x, 0, 3), yhs)
    for e in range(2):
        left_for(main(0, x), xhs.at[e])
        left_for(main(0, x, 0, 2), fhs.at[e])
    for k in range(STEPS):
        left_for(s.at[k, pl.ds(0, 15)], zs.at[k])
        left_for(main(k, x, 0, 3), ys.at[k])
        for e in range(2):
            left_for(main(k, x), xs.at[k, e])
            left_for(main(k, x, 0, 2), fs.at[k, e])
        left_for(ta.at[piece(k), at(core * 16, 16), :], ks.at[k])

        @pl.when(core == k % 2)
        def _():
            left_for(ta.at[piece(k), at(32, 8), :], khs.at[k])

    for e in range(2):
        pltpu.make_async_copy(ob.at[e], o_ref.at[:, pl.ds(e * 16, 16), :], ob_sem.at[e]).wait()


def shards(density, virt_coeff, block_coeff, ao_order):
    hbm = pl.BlockSpec(memory_space=pltpu.HBM)
    dma = pltpu.SemaphoreType.DMA
    one, two, four = dma, dma((2,)), dma((4,))
    return pl.pallas_call(
        exchange,
        out_shape=jax.ShapeDtypeStruct((64, 32, 1024), BF),
        in_specs=[hbm] * 4,
        out_specs=hbm,
        scratch_shapes=[
            pltpu.SMEM((1024,), jnp.int32),
            pltpu.VMEM((2, 16, 40, 128), BF),
            pltpu.VMEM((2, 4, 4, 8, 20, 128), BF),
            pltpu.VMEM((16, 8, 1024), BF),
            pltpu.VMEM((64, 1024), F32),
            pltpu.VMEM((64, 128), BF),
            pltpu.VMEM((2, 640, 128), F32),
            pltpu.VMEM((640, 256), BF),
            pltpu.VMEM((32, 24, 128), F32),
            pltpu.VMEM((640, 1024), BF),
            pltpu.VMEM((STEPS, 16, 16, 128), BF),
            pltpu.VMEM((STEPS, 16, 16, 128), BF),
            pltpu.VMEM((STEPS, 16, 16, 128), BF),
            pltpu.VMEM((16, 16, 128), BF),
            pltpu.VMEM((256, 128), F32),
            pltpu.VMEM((STEPS, 2, 8, 16, 128), BF),
            pltpu.VMEM((2, 8, 16, 128), BF),
            pltpu.VMEM((32, 640, 128), BF),
            pltpu.VMEM((5, 512, 128), F32),
            pltpu.VMEM((512, 640), BF),
            pltpu.VMEM((2, 64, 16, 1024), BF),
            one, two,
            one, one,
            one, one,
            dma((16,)), one, one, one, two, two, two, two, four, four,
            four, four, four, four, dma((4, 2)), dma((4, 2)), dma((4, 2)), dma((4, 2)), four, four,
            one, one, one, one, two, two, two, two, four, four,
        ],
        compiler_params=pltpu.CompilerParams(
            collective_id=0, has_side_effects=True, vmem_limit_bytes=48 * 1024 * 1024
        ),
    )(ao_order, density, virt_coeff, block_coeff)


def solution(mesh):
    return jax.shard_map(
        shards,
        mesh=mesh,
        in_specs=(P("virt", "ao", None), P("virt", None), P("ao", None), P()),
        out_specs=P("ao", "virt", None),
        check_vma=False,
    )
```

```python
import jax
import jax.numpy as jnp
from jax import lax
from jax.experimental import pallas as pl
from jax.experimental.pallas import tpu as pltpu
from jax.sharding import PartitionSpec as P

MESH = pl.DeviceIdType.MESH
BF = jnp.bfloat16
F32 = jnp.float32
TN = (((0,), (0,)), ((), ()))
NT = (((1,), (1,)), ((), ()))
STEPS = 4
BLOCKS = [(y % 2, (y // 2) * 8 + x * 2 + c) for c in range(2) for x in range(4) for y in range(4)]
BLOCKS += [(y % 2, 16 + (y // 2) * 2 + h) for h in range(2) for y in range(4)]


def exchange(
    order_hbm, d_ref, c_ref, b_ref, o_ref,
    order, dl, dm, cl, bl, hot, kp, df, dp, cf, cp, s, sh, r, rh, rf, g, gh, ta, hb, ob,
    order_sem, ob_sem, ds, dr, dms, dmr, dks, dkr, bs, br, zcs, zcr, ycs, ycr, xcs, xcr, fcs, fcr, kcs, kcr,
    zs, zr, ys, yr, xs, xr, fs, fr, ks, kr, zhs, zhr, yhs, yhr, xhs, xhr, fhs, fhr, khs, khr,
):
    v, j = lax.axis_index("virt"), lax.axis_index("ao")
    y_lo, z = v // 16, v % 16
    core, x, y_hi = j % 2, (j // 2) % 4, j // 8
    y = 2 * y_hi + y_lo
    share = j % 4
    right, left, far = (x + 1) % 4, (x + 3) % 4, (x + 2) % 4
    lanes = pl.ds(pl.multiple_of((j // 2) * 128, 128), 128)

    def dev(yy, xx):
        return (yy % 2) * 16 + z, (yy // 2) * 8 + xx * 2 + core

    other = (v, j + 1 - 2 * core)
    to_right, to_left = dev(y, right), dev(y, left)

    def remote(src, dst, send, recv, device):
        return pltpu.make_async_remote_copy(
            src_ref=src, dst_ref=dst, send_sem=send, recv_sem=recv, device_id=device, device_id_type=MESH
        )

    def arrived(ref, sem):
        remote(ref, ref, sem, sem, other).wait_recv()

    def left_for(ref, sem):
        remote(ref, ref, sem, sem, other).wait_send()

    order_copy = pltpu.make_async_copy(order_hbm, order, order_sem)
    order_copy.start()

    barrier = pltpu.get_barrier_semaphore()
    for dy in (1, 3):
        pl.semaphore_signal(barrier, inc=1, device_id=dev((y + dy) % 4, x), device_id_type=MESH)

    @pl.loop(1, 16)
    def _(t):
        pl.semaphore_signal(barrier, inc=1, device_id=(y_lo * 16 + (z + t) % 16, j), device_id_type=MESH)
        pl.semaphore_signal(barrier, inc=1, device_id=(v, (j + t) % 16), device_id_type=MESH)

    pl.semaphore_wait(barrier, 32)

    @pl.when(z % 2 == core)
    def _():
        @pl.loop(1, 16)
        def _(t):
            remote(c_ref.at[:, lanes], cl.at[core, x, y, z // 2], zcs.at[t], zcr, (y_lo * 16 + (z + t) % 16, j)).start()

        pltpu.make_async_copy(c_ref.at[:, lanes], cl.at[core, x, y, z // 2], zcr).start()

    @pl.loop(1, 16)
    def _(t):
        jj = (j + t) % 16
        remote(d_ref.at[jj], dl.at[j], ds, dr, (v, jj)).start()

    @pl.loop(1, 8)
    def _(t):
        jj = (j + 2 * t) % 16
        remote(d_ref.at[16 + jj // 4], dm.at[core, j // 2], dms, dmr, (v, jj)).start()

    pltpu.make_async_copy(d_ref.at[j], dl.at[j], dr).start()
    pltpu.make_async_copy(d_ref.at[16 + j // 4], dm.at[core, j // 2], dmr).start()

    order_copy.wait()
    column = lax.broadcasted_iota(jnp.int32, (1, 1024), 1)

    @pl.loop(0, 64)
    def _(k):
        hot[pl.ds(k, 1), :] = jnp.where(column == order[j * 64 + k], 1.0, 0.0).astype(F32)

    mine = cl.at[core, x, y]
    arrived(mine, zcr)
    for dy in (1, 3, 2):
        remote(mine, mine, ycs, ycr, dev((y + dy) % 4, x)).start()

    arrived(dm.at[core], dmr)
    remote(dm.at[core], dm.at[core], dks, dkr, other).start()

    def coeff(xx, first=0, count=4):
        return cl.at[core, xx, pl.ds(first, count)]

    def both_ways(blocks, send, recv):
        for half in range(2):
            for way, device in enumerate((to_right, to_left)):
                first = 2 * (half ^ way)
                blk = blocks(first, 2)
                remote(blk, blk, send.at[way, half], recv.at[way, half], device).start()

    arrived(coeff(x, 0, 3), ycr)
    both_ways(lambda first, count: coeff(x, first, count), xcs, xcr)

    def coeff_to_core(e, xx):
        blk = cl.at[core, xx]
        remote(blk, blk, kcs.at[e], kcr.at[e], other).start()

    def make_t(e, xx):
        arrived(cl.at[1 - core, xx], kcr.at[e])

        for yh in range(2):
            for yl in range(2):
                for zz in range(16):
                    cf[yl * 16 + zz, pl.ds(0, 20), :] = cl[zz % 2, xx, 2 * yh + yl, zz // 2].astype(F32)
            flat = cf.reshape(32 * 24, 128)
            lane = pl.ds(pl.multiple_of((yh * 4 + xx) * 128, 128), 128)
            for q, (yl, i) in enumerate(BLOCKS):
                cp[pl.ds(q * 16, 16), lane] = flat[pl.ds(yl * 384 + i, 16, stride=24), :].astype(BF)
            tt = lax.dot_general(cp[:, lane], dp[...], TN, preferred_element_type=F32).astype(BF)
            for q in range(4):
                for k in range(STEPS):
                    rows = tt[q * 32 + k * 8:q * 32 + k * 8 + 8]
                    s[k, xx * 4 + q, pl.ds(yh * 8, 8), :] = rows[:, :128]
                    sh[k, xx * 4 + q, pl.ds(yh * 8, 8), :] = rows[:, 128:]

    coeff_to_core(0, x)

    arrived(dl, dr)
    arrived(dm.at[1 - core], dkr)
    for u in range(2):
        for jj in range(16):
            df[u, pl.ds(jj * 40, 40), :] = (dm[jj % 2, jj // 2] if u else dl[jj]).astype(F32)
        for q, (yl, i) in enumerate(BLOCKS):
            dp[pl.ds(q * 16, 16), pl.ds(u * 128, 128)] = df[u, pl.ds(yl * 320 + i, 16, stride=20), :].astype(BF)

    make_t(0, x)
    for way, (frm, device) in enumerate(((left, to_right), (right, to_left))):
        blk = coeff(frm, 2 * way, 2)
        arrived(blk, xcr.at[way, 0])
        remote(blk, blk, fcs.at[way], fcr.at[way], device).start()
    for way, frm in enumerate((left, right)):
        arrived(coeff(frm, 2 - 2 * way, 2), xcr.at[way, 1])
        coeff_to_core(1 + way, frm)
    make_t(1, left)
    arrived(coeff(far, 0, 2), fcr.at[0])
    arrived(coeff(far, 2, 2), fcr.at[1])
    coeff_to_core(3, far)
    make_t(2, right)
    make_t(3, far)

    for k in range(STEPS):
        @pl.loop(0, 15)
        def _(w):
            zz = (z + 16 + (w // 2 + 1) * (1 - 2 * (w % 2))) % 16
            remote(s.at[k, zz], r.at[k, z], zs.at[k], zr.at[k], (y_lo * 16 + zz, j)).start()

        r[k, z] = s[k, z]

        @pl.when(share == k)
        def _():
            @pl.loop(0, 15)
            def _(w):
                zz = (z + 16 + (w // 2 + 1) * (1 - 2 * (w % 2))) % 16
                remote(sh.at[k, zz], rh.at[z], zhs, zhr, (y_lo * 16 + zz, j)).start()

            rh[z] = sh[k, z]

    @pl.loop(1, 16)
    def _(t):
        remote(b_ref, bl.at[j], bs, br, (v, (j + t) % 16)).start()

    pltpu.make_async_copy(b_ref, bl.at[j], br).start()

    def at(block, count=1):
        return pl.ds(pl.multiple_of(block * 16, 16), count * 16)

    def piece(k):
        return pl.ds(k * 8, 8)

    def turn(src, dst):
        for zz in range(16):
            rf[pl.ds(zz * 16, 16), :] = src[zz].astype(F32)
        for i in range(16):
            dst[i // 8, i % 8] = rf[pl.ds(i, 16, stride=16), :].astype(BF)

    own = core * 16 + x * 4
    pool = 32 + (x // 2) * 4

    def along_y(k):
        arrived(r.at[k, pl.ds(0, 15)], zr.at[k])
        turn(r.at[k], g.at[k])
        to = ta.at[piece(k), at(own + y), :]
        for dy in (1, 3, 2):
            half = y_lo if dy == 2 else 1 - y_lo
            remote(g.at[k, half], to, ys.at[k], yr.at[k], dev((y + dy) % 4, x)).start()
        ta[piece(k), at(own + y), :] = g[k, y_lo]

        @pl.when(share == k)
        def _():
            arrived(rh.at[pl.ds(0, 15)], zhr)
            turn(rh, gh)
            to_pool = ta.at[piece(k), at(pool + y), :]
            for dy in (1, 3, 2):
                half = y_lo if dy == 2 else 1 - y_lo
                remote(gh.at[half], to_pool, yhs, yhr, dev((y + dy) % 4, x)).start()
            ta[piece(k), at(pool + y), :] = gh[y_lo]

    def main(k, xx, first=0, count=4):
        return ta.at[piece(k), at(core * 16 + xx * 4 + first, count), :]

    def pooled(k, xx, first=0, count=4):
        return ta.at[piece(k), at(32 + (xx // 2) * 4 + first, count), :]

    def to_core(k, xx):
        blk = main(k, xx)
        remote(blk, blk, ks.at[k], kr.at[k], other).start()

    def along_x(k):
        arrived(main(k, x, 0, 3), yr.at[k])
        both_ways(lambda first, count: main(k, x, first, count), xs.at[k], xr.at[k])

        @pl.when(share == k)
        def _():
            arrived(pooled(k, x, 0, 3), yhr)
            both_ways(lambda first, count: pooled(k, x, first, count), xhs, xhr)

        to_core(k, x)

    def between(k):
        return jnp.logical_and(core == k % 2, x % 2 != k // 2)

    def pass_on(k):
        for way, (frm, device) in enumerate(((left, to_right), (right, to_left))):
            blk = main(k, frm, 2 * way, 2)
            arrived(blk, xr.at[k, way, 0])
            remote(blk, blk, fs.at[k, way], fr.at[k, way], device).start()

        @pl.when(between(k))
        def _():
            for way, (frm, device) in enumerate(((left, to_right), (right, to_left))):
                blk = pooled(k, frm, 2 * way, 2)
                arrived(blk, xhr.at[way, 0])
                remote(blk, blk, fhs.at[way], fhr.at[way], device).start()

    def sides(k):
        for way, frm in enumerate((left, right)):
            arrived(main(k, frm, 2 - 2 * way, 2), xr.at[k, way, 1])
            to_core(k, frm)

        @pl.when(between(k))
        def _():
            for way, frm in enumerate((left, right)):
                arrived(pooled(k, frm, 2 - 2 * way, 2), xhr.at[way, 1])

    def last(k):
        arrived(main(k, far, 0, 2), fr.at[k, 0])
        arrived(main(k, far, 2, 2), fr.at[k, 1])
        to_core(k, far)

        @pl.when(share == k)
        def _():
            arrived(pooled(k, far, 0, 2), fhr.at[0])
            arrived(pooled(k, far, 2, 2), fhr.at[1])

        @pl.when(core == k % 2)
        def _():
            blk = ta.at[piece(k), at(32, 8), :]
            remote(blk, blk, khs.at[k], khr.at[k], other).start()

    def finish(k):
        arrived(ta.at[piece(k), at((1 - core) * 16, 16), :], kr.at[k])

        @pl.when(core != k % 2)
        def _():
            arrived(ta.at[piece(k), at(32, 8), :], khr.at[k])

        for first, count in ((0, 256), (256, 256), (512, 128)):
            terms = jnp.concatenate([ta[k * 8 + n, pl.ds(first, count), :] for n in range(8)], axis=1)
            hb[:, pl.ds(first, count)] = lax.dot_general(kp[...], terms, NT, preferred_element_type=F32).astype(BF)

        @pl.loop(0, 4)
        def _(q):
            cols = pl.ds(pl.multiple_of(q * 256, 256), 256)
            out = jnp.dot(hb[...], cp[:, cols], preferred_element_type=F32)
            ob[k // 2, :, pl.ds((k % 2) * 8, 8), cols] = out.reshape(64, 8, 256).astype(BF)

        if k % 2 == 1:
            pltpu.make_async_copy(ob.at[k // 2], o_ref.at[:, pl.ds(k // 2 * 16, 16), :], ob_sem.at[k // 2]).start()

    along_y(0)

    arrived(bl, br)
    panel = lax.dot_general(hot[...].astype(BF), bl[...].reshape(128, 1024), NT, preferred_element_type=F32).astype(BF)
    spread = lax.broadcasted_iota(jnp.int32, (512, 64), 0) // 8 == lax.broadcasted_iota(jnp.int32, (512, 64), 1)
    panel = jnp.dot(jnp.where(spread, 1.0, 0.0).astype(BF), panel, preferred_element_type=F32)
    place = lax.broadcasted_iota(jnp.int32, (512, 128), 0) % 8
    for n in range(8):
        kp[:, pl.ds(n * 128, 128)] = jnp.where(place == n, panel, 0.0).astype(BF)

    for k in range(STEPS):
        along_x(k)
        if k + 1 < STEPS:
            along_y(k + 1)
        if k >= 2:
            finish(k - 2)
        if k >= 1:
            last(k - 1)
        pass_on(k)
        sides(k)
    finish(STEPS - 2)
    last(STEPS - 1)
    finish(STEPS - 1)

    @pl.when(z % 2 == core)
    def _():
        @pl.loop(1, 16)
        def _(t):
            left_for(c_ref.at[:, lanes], zcs.at[t])

    left_for(dl.at[pl.ds(0, 15)], ds)
    left_for(dl.at[pl.ds(0, 7)], dms)
    left_for(dm.at[core], dks)
    left_for(bl.at[pl.ds(0, 15)], bs)
    left_for(cl.at[core, x, pl.ds(0, 3)], ycs)
    for e in range(2):
        for half in range(2):
            left_for(coeff(x, 0, 2), xcs.at[e, half])
        left_for(coeff(x, 0, 2), fcs.at[e])
    for e in range(4):
        left_for(cl.at[core, x], kcs.at[e])
    left_for(rh.at[pl.ds(0, 15)], zhs)
    left_for(main(0, x, 0, 3), yhs)
    for e in range(2):
        for half in range(2):
            left_for(main(0, x, 0, 2), xhs.at[e, half])
        left_for(main(0, x, 0, 2), fhs.at[e])
    for k in range(STEPS):
        left_for(s.at[k, pl.ds(0, 15)], zs.at[k])
        left_for(main(k, x, 0, 3), ys.at[k])
        for e in range(2):
            for half in range(2):
                left_for(main(k, x, 0, 2), xs.at[k, e, half])
            left_for(main(k, x, 0, 2), fs.at[k, e])
        left_for(ta.at[piece(k), at(core * 16, 16), :], ks.at[k])

        @pl.when(core == k % 2)
        def _():
            left_for(ta.at[piece(k), at(32, 8), :], khs.at[k])

    for e in range(2):
        pltpu.make_async_copy(ob.at[e], o_ref.at[:, pl.ds(e * 16, 16), :], ob_sem.at[e]).wait()


def shards(density, virt_coeff, block_coeff, ao_order):
    hbm = pl.BlockSpec(memory_space=pltpu.HBM)
    dma = pltpu.SemaphoreType.DMA
    one, two, four = dma, dma((2,)), dma((4,))
    return pl.pallas_call(
        exchange,
        out_shape=jax.ShapeDtypeStruct((64, 32, 1024), BF),
        in_specs=[hbm] * 4,
        out_specs=hbm,
        scratch_shapes=[
            pltpu.SMEM((1024,), jnp.int32),
            pltpu.VMEM((16, 40, 128), BF),
            pltpu.VMEM((2, 8, 40, 128), BF),
            pltpu.VMEM((2, 4, 4, 8, 20, 128), BF),
            pltpu.VMEM((16, 8, 1024), BF),
            pltpu.VMEM((64, 1024), F32),
            pltpu.VMEM((512, 1024), BF),
            pltpu.VMEM((2, 640, 128), F32),
            pltpu.VMEM((640, 256), BF),
            pltpu.VMEM((32, 24, 128), F32),
            pltpu.VMEM((640, 1024), BF),
            pltpu.VMEM((STEPS, 16, 16, 128), BF),
            pltpu.VMEM((STEPS, 16, 16, 128), BF),
            pltpu.VMEM((STEPS, 16, 16, 128), BF),
            pltpu.VMEM((16, 16, 128), BF),
            pltpu.VMEM((256, 128), F32),
            pltpu.VMEM((STEPS, 2, 8, 16, 128), BF),
            pltpu.VMEM((2, 8, 16, 128), BF),
            pltpu.VMEM((32, 640, 128), BF),
            pltpu.VMEM((512, 640), BF),
            pltpu.VMEM((2, 64, 16, 1024), BF),
            one, two,
            one, one, one, one, one, one,
            one, one,
            dma((16,)), one, one, one, dma((2, 2)), dma((2, 2)), two, two, four, four,
            four, four, four, four, dma((4, 2, 2)), dma((4, 2, 2)), dma((4, 2)), dma((4, 2)), four, four,
            one, one, one, one, dma((2, 2)), dma((2, 2)), two, two, four, four,
        ],
        compiler_params=pltpu.CompilerParams(
            collective_id=0, has_side_effects=True, vmem_limit_bytes=60 * 1024 * 1024
        ),
    )(ao_order, density, virt_coeff, block_coeff)


def solution(mesh):
    return jax.shard_map(
        shards,
        mesh=mesh,
        in_specs=(P("virt", "ao", None), P("virt", None), P("ao", None), P()),
        out_specs=P("ao", "virt", None),
        check_vma=False,
    )
```

```python
import jax
import jax.numpy as jnp
from jax import lax
from jax.experimental import pallas as pl
from jax.experimental.pallas import tpu as pltpu
from jax.sharding import PartitionSpec as P

MESH = pl.DeviceIdType.MESH
BF = jnp.bfloat16
F32 = jnp.float32
TN = (((0,), (0,)), ((), ()))
NT = (((1,), (1,)), ((), ()))
STEPS = 4
BLOCKS = [(y % 2, (y // 2) * 8 + x * 2 + c) for c in range(2) for x in range(4) for y in range(4)]
BLOCKS += [(y % 2, 16 + (y // 2) * 2 + h) for h in range(2) for y in range(4)]


def exchange(
    order_hbm, d_ref, c_ref, b_ref, o_ref,
    order, dl, dm, cl, bl, hot, pt, kp, df, dp, cf, cp, s, r, rf, g, gh, tm, tq, hb, ho, hq,
    order_sem, ds, dr, dms, dmr, dks, dkr, bs, br, bks, bkr, zcs, zcr, ycs, ycr, xcs, xcr, fcs, fcr, kcs, kcr,
    zs, zr, ys, yr, xs, xr, fs, fr, hs, hr, yhs, yhr, xhs, xhr, fhs, fhr, qs, qr,
):
    v, j = lax.axis_index("virt"), lax.axis_index("ao")
    y_lo, z = v // 16, v % 16
    core, x, y_hi = j % 2, (j // 2) % 4, j // 8
    y = 2 * y_hi + y_lo
    share = j % 4
    right, left, far = (x + 1) % 4, (x + 3) % 4, (x + 2) % 4
    lanes = pl.ds(pl.multiple_of((j // 2) * 128, 128), 128)

    def dev(yy, xx):
        return (yy % 2) * 16 + z, (yy // 2) * 8 + xx * 2 + core

    other = (v, j + 1 - 2 * core)
    to_right, to_left = dev(y, right), dev(y, left)

    def remote(src, dst, send, recv, device):
        return pltpu.make_async_remote_copy(
            src_ref=src, dst_ref=dst, send_sem=send, recv_sem=recv, device_id=device, device_id_type=MESH
        )

    def arrived(ref, sem):
        remote(ref, ref, sem, sem, other).wait_recv()

    def left_for(ref, sem):
        remote(ref, ref, sem, sem, other).wait_send()

    order_copy = pltpu.make_async_copy(order_hbm, order, order_sem)
    order_copy.start()

    barrier = pltpu.get_barrier_semaphore()
    for dy in (1, 3):
        pl.semaphore_signal(barrier, inc=1, device_id=dev((y + dy) % 4, x), device_id_type=MESH)

    @pl.loop(1, 16)
    def _(t):
        pl.semaphore_signal(barrier, inc=1, device_id=(y_lo * 16 + (z + t) % 16, j), device_id_type=MESH)
        pl.semaphore_signal(barrier, inc=1, device_id=(v, (j + t) % 16), device_id_type=MESH)

    pl.semaphore_wait(barrier, 32)

    @pl.when(z % 2 == core)
    def _():
        @pl.loop(1, 16)
        def _(t):
            remote(c_ref.at[:, lanes], cl.at[core, x, y, z // 2], zcs.at[t], zcr, (y_lo * 16 + (z + t) % 16, j)).start()

        pltpu.make_async_copy(c_ref.at[:, lanes], cl.at[core, x, y, z // 2], zcr).start()

    @pl.loop(1, 16)
    def _(t):
        jj = (j + t) % 16
        remote(d_ref.at[jj], dl.at[j], ds, dr, (v, jj)).start()

    @pl.loop(1, 8)
    def _(t):
        jj = (j + 2 * t) % 16
        remote(d_ref.at[16 + jj // 4], dm.at[core, j // 2], dms, dmr, (v, jj)).start()

    pltpu.make_async_copy(d_ref.at[j], dl.at[j], dr).start()
    pltpu.make_async_copy(d_ref.at[16 + j // 4], dm.at[core, j // 2], dmr).start()

    order_copy.wait()
    column = lax.broadcasted_iota(jnp.int32, (1, 1024), 1)

    @pl.loop(0, 128)
    def _(k):
        hot[pl.ds(k, 1), :] = jnp.where(column == order[(j // 2) * 128 + k], 1.0, 0.0).astype(F32)

    mine = cl.at[core, x, y]
    arrived(mine, zcr)
    for dy in (1, 3, 2):
        remote(mine, mine, ycs, ycr, dev((y + dy) % 4, x)).start()

    arrived(dm.at[core], dmr)
    remote(dm.at[core], dm.at[core], dks, dkr, other).start()

    def coeff(xx, first=0, count=4):
        return cl.at[core, xx, pl.ds(first, count)]

    def both_ways(blocks, send, recv):
        for half in range(2):
            for way, device in enumerate((to_right, to_left)):
                first = 2 * (half ^ way)
                blk = blocks(first, 2)
                remote(blk, blk, send.at[way, half], recv.at[way, half], device).start()

    arrived(coeff(x, 0, 3), ycr)
    both_ways(lambda first, count: coeff(x, first, count), xcs, xcr)

    def coeff_to_core(e, xx):
        blk = cl.at[core, xx]
        remote(blk, blk, kcs.at[e], kcr.at[e], other).start()

    def make_t(e, xx):
        arrived(cl.at[1 - core, xx], kcr.at[e])

        for yh in range(2):
            for yl in range(2):
                for zz in range(16):
                    cf[yl * 16 + zz, pl.ds(0, 20), :] = cl[zz % 2, xx, 2 * yh + yl, zz // 2].astype(F32)
            flat = cf.reshape(32 * 24, 128)
            lane = pl.ds(pl.multiple_of((yh * 4 + xx) * 128, 128), 128)
            for q, (yl, i) in enumerate(BLOCKS):
                cp[pl.ds(q * 16, 16), lane] = flat[pl.ds(yl * 384 + i, 16, stride=24), :].astype(BF)
            tt = lax.dot_general(cp[:, lane], dp[...], TN, preferred_element_type=F32).astype(BF)
            for q in range(4):
                for k in range(STEPS):
                    rows = tt[q * 32 + k * 8:q * 32 + k * 8 + 8]
                    s[k, xx * 4 + q, pl.ds(yh * 8, 8), :] = rows[:, :128]
                    s[k, xx * 4 + q, pl.ds(16 + yh * 8, 8), :] = rows[:, 128:]

    coeff_to_core(0, x)

    arrived(dl, dr)
    arrived(dm.at[1 - core], dkr)
    for u in range(2):
        for jj in range(16):
            df[u, pl.ds(jj * 40, 40), :] = (dm[jj % 2, jj // 2] if u else dl[jj]).astype(F32)
        for q, (yl, i) in enumerate(BLOCKS):
            dp[pl.ds(q * 16, 16), pl.ds(u * 128, 128)] = df[u, pl.ds(yl * 320 + i, 16, stride=20), :].astype(BF)

    make_t(0, x)
    for way, (frm, device) in enumerate(((left, to_right), (right, to_left))):
        blk = coeff(frm, 2 * way, 2)
        arrived(blk, xcr.at[way, 0])
        remote(blk, blk, fcs.at[way], fcr.at[way], device).start()
    for way, frm in enumerate((left, right)):
        arrived(coeff(frm, 2 - 2 * way, 2), xcr.at[way, 1])
        coeff_to_core(1 + way, frm)
    make_t(1, left)
    arrived(coeff(far, 0, 2), fcr.at[0])
    arrived(coeff(far, 2, 2), fcr.at[1])
    coeff_to_core(3, far)
    make_t(2, right)
    make_t(3, far)

    for k in range(STEPS):
        def along_z(part):
            @pl.loop(0, 15)
            def _(w):
                zz = (z + 16 + (w // 2 + 1) * (1 - 2 * (w % 2))) % 16
                remote(s.at[k, zz, part], r.at[k, z, part], zs.at[k], zr.at[k], (y_lo * 16 + zz, j)).start()

        @pl.when(share == k)
        def _():
            along_z(pl.ds(0, 32))

        @pl.when(share != k)
        def _():
            along_z(pl.ds(0, 16))

        r[k, z] = s[k, z]

    @pl.loop(1, 8)
    def _(t):
        remote(b_ref, bl.at[core, j // 2], bs, br, (v, (j + 2 * t) % 16)).start()

    pltpu.make_async_copy(b_ref, bl.at[core, j // 2], br).start()

    def at(block, count=1):
        return pl.ds(pl.multiple_of(block * 16, 16), count * 16)

    def piece(k):
        return pl.ds(k * 8, 8)

    def turn(k, first, dst):
        for zz in range(16):
            rf[pl.ds(zz * 16, 16), :] = r[k, zz, pl.ds(first, 16), :].astype(F32)
        for i in range(16):
            dst[i // 8, i % 8] = rf[pl.ds(i, 16, stride=16), :].astype(BF)

    def main(k, xx, first=0, count=4):
        return tm.at[piece(k), at(xx * 4 + first, count), :]

    def pooled(k, xx, first=0, count=4):
        return tq.at[piece(k), at((xx // 2) * 4 + first, count), :]

    def along_y(k):
        @pl.when(share != k)
        def _():
            arrived(r.at[k, pl.ds(0, 15), pl.ds(0, 16)], zr.at[k])

        @pl.when(share == k)
        def _():
            arrived(r.at[k, pl.ds(0, 15)], zr.at[k])

        turn(k, 0, g.at[k])
        for dy in (1, 3, 2):
            half = y_lo if dy == 2 else 1 - y_lo
            remote(g.at[k, half], main(k, x, y, 1), ys.at[k], yr.at[k], dev((y + dy) % 4, x)).start()
        tm[piece(k), at(x * 4 + y), :] = g[k, y_lo]

        @pl.when(share == k)
        def _():
            turn(k, 16, gh)
            for dy in (1, 3, 2):
                half = y_lo if dy == 2 else 1 - y_lo
                remote(gh.at[half], pooled(k, x, y, 1), yhs, yhr, dev((y + dy) % 4, x)).start()
            tq[piece(k), at((x // 2) * 4 + y), :] = gh[y_lo]

    def along_x(k):
        arrived(main(k, x, 0, 3), yr.at[k])
        both_ways(lambda first, count: main(k, x, first, count), xs.at[k], xr.at[k])

        @pl.when(share == k)
        def _():
            arrived(pooled(k, x, 0, 3), yhr)
            both_ways(lambda first, count: pooled(k, x, first, count), xhs, xhr)

    def between(k):
        return jnp.logical_and(core == k % 2, x % 2 != k // 2)

    def pass_on(k):
        for way, (frm, device) in enumerate(((left, to_right), (right, to_left))):
            blk = main(k, frm, 2 * way, 2)
            arrived(blk, xr.at[k, way, 0])
            remote(blk, blk, fs.at[k, way], fr.at[k, way], device).start()

        @pl.when(between(k))
        def _():
            for way, (frm, device) in enumerate(((left, to_right), (right, to_left))):
                blk = pooled(k, frm, 2 * way, 2)
                arrived(blk, xhr.at[way, 0])
                remote(blk, blk, fhs.at[way], fhr.at[way], device).start()

    def sides(k):
        for way, frm in enumerate((left, right)):
            arrived(main(k, frm, 2 - 2 * way, 2), xr.at[k, way, 1])

        @pl.when(between(k))
        def _():
            for way, frm in enumerate((left, right)):
                arrived(pooled(k, frm, 2 - 2 * way, 2), xhr.at[way, 1])

    mine_at = pl.ds(pl.multiple_of(core * 256, 256), 256)
    theirs_at = pl.ds(pl.multiple_of((1 - core) * 256, 256), 256)
    pool_at = pl.ds(512, 128)

    def to_s(k):
        arrived(main(k, far, 0, 2), fr.at[k, 0])
        arrived(main(k, far, 2, 2), fr.at[k, 1])
        terms = jnp.concatenate([tm[k * 8 + n] for n in range(8)], axis=1)
        ho[k] = lax.dot_general(kp[1 - core], terms, NT, preferred_element_type=F32).astype(BF)
        remote(ho.at[k], hb.at[k, :, mine_at], hs.at[k], hr.at[k], other).start()

        @pl.when(core == k % 2)
        def _():
            @pl.when(share == k)
            def _():
                arrived(pooled(k, far, 0, 2), fhr.at[0])
                arrived(pooled(k, far, 2, 2), fhr.at[1])

            terms = jnp.concatenate([tq[k * 8 + n] for n in range(8)], axis=1)
            hq[k] = lax.dot_general(kp[1 - core], terms, NT, preferred_element_type=F32).astype(BF)
            remote(hq.at[k], hb.at[k, :, pool_at], qs.at[k], qr.at[k], other).start()
            hb[k, :, pool_at] = lax.dot_general(kp[core], terms, NT, preferred_element_type=F32).astype(BF)

        terms = jnp.concatenate([tm[k * 8 + n] for n in range(8)], axis=1)
        hb[k, :, mine_at] = lax.dot_general(kp[core], terms, NT, preferred_element_type=F32).astype(BF)

    def to_m(k):
        arrived(hb.at[k, :, theirs_at], hr.at[k])

        @pl.when(core != k % 2)
        def _():
            arrived(hb.at[k, :, pool_at], qr.at[k])

        @pl.loop(0, 4)
        def _(q):
            cols = pl.ds(pl.multiple_of(q * 256, 256), 256)
            out = jnp.dot(hb[k], cp[:, cols], preferred_element_type=F32)
            o_ref[:, pl.ds(k * 8, 8), cols] = out.reshape(64, 8, 256).astype(BF)

    along_y(0)

    arrived(bl.at[core], br)
    remote(bl.at[core], bl.at[core], bks, bkr, other).start()
    arrived(bl.at[1 - core], bkr)
    block = jnp.concatenate([bl[q % 2, q // 2].astype(F32) for q in range(16)], axis=0).astype(BF)
    pt[...] = lax.dot_general(hot[...].astype(BF), block, NT, preferred_element_type=F32).astype(BF)
    spread = lax.broadcasted_iota(jnp.int32, (512, 64), 0) // 8 == lax.broadcasted_iota(jnp.int32, (512, 64), 1)
    place = lax.broadcasted_iota(jnp.int32, (512, 128), 0) % 8
    for e in range(2):
        panel = jnp.dot(jnp.where(spread, 1.0, 0.0).astype(BF), pt[e * 64:(e + 1) * 64], preferred_element_type=F32)
        for n in range(8):
            kp[e, :, pl.ds(n * 128, 128)] = jnp.where(place == n, panel, 0.0).astype(BF)

    for k in range(STEPS):
        along_x(k)
        if k + 1 < STEPS:
            along_y(k + 1)
        if k >= 2:
            to_m(k - 2)
        if k >= 1:
            to_s(k - 1)
        pass_on(k)
        sides(k)
    to_m(STEPS - 2)
    to_s(STEPS - 1)
    to_m(STEPS - 1)

    @pl.when(z % 2 == core)
    def _():
        @pl.loop(1, 16)
        def _(t):
            left_for(c_ref.at[:, lanes], zcs.at[t])

    left_for(dl.at[pl.ds(0, 15)], ds)
    left_for(dl.at[pl.ds(0, 7)], dms)
    left_for(dm.at[core], dks)
    left_for(bl.at[core, pl.ds(0, 7)], bs)
    left_for(bl.at[core], bks)
    left_for(cl.at[core, x, pl.ds(0, 3)], ycs)
    for e in range(2):
        for half in range(2):
            left_for(coeff(x, 0, 2), xcs.at[e, half])
        left_for(coeff(x, 0, 2), fcs.at[e])
    for e in range(4):
        left_for(cl.at[core, x], kcs.at[e])
    left_for(main(0, x, 0, 3), yhs)
    for e in range(2):
        for half in range(2):
            left_for(main(0, x, 0, 2), xhs.at[e, half])
        left_for(main(0, x, 0, 2), fhs.at[e])
    for k in range(STEPS):
        @pl.when(share != k)
        def _():
            left_for(s.at[k, pl.ds(0, 15), pl.ds(0, 16)], zs.at[k])

        @pl.when(share == k)
        def _():
            left_for(s.at[k, pl.ds(0, 15)], zs.at[k])

        left_for(main(k, x, 0, 3), ys.at[k])
        for e in range(2):
            for half in range(2):
                left_for(main(k, x, 0, 2), xs.at[k, e, half])
            left_for(main(k, x, 0, 2), fs.at[k, e])
        left_for(ho.at[k], hs.at[k])

        @pl.when(core == k % 2)
        def _():
            left_for(hq.at[k], qs.at[k])


def shards(density, virt_coeff, block_coeff, ao_order):
    hbm = pl.BlockSpec(memory_space=pltpu.HBM)
    dma = pltpu.SemaphoreType.DMA
    one, two, four = dma, dma((2,)), dma((4,))
    return pl.pallas_call(
        exchange,
        out_shape=pltpu.VMEM((64, 32, 1024), BF),
        in_specs=[hbm] * 4,
        out_specs=pl.BlockSpec(memory_space=pltpu.VMEM),
        scratch_shapes=[
            pltpu.SMEM((1024,), jnp.int32),
            pltpu.VMEM((16, 40, 128), BF),
            pltpu.VMEM((2, 8, 40, 128), BF),
            pltpu.VMEM((2, 4, 4, 8, 20, 128), BF),
            pltpu.VMEM((2, 8, 8, 1024), BF),
            pltpu.VMEM((128, 1024), F32),
            pltpu.VMEM((128, 128), BF),
            pltpu.VMEM((2, 512, 1024), BF),
            pltpu.VMEM((2, 640, 128), F32),
            pltpu.VMEM((640, 256), BF),
            pltpu.VMEM((32, 24, 128), F32),
            pltpu.VMEM((640, 1024), BF),
            pltpu.VMEM((STEPS, 16, 32, 128), BF),
            pltpu.VMEM((STEPS, 16, 32, 128), BF),
            pltpu.VMEM((256, 128), F32),
            pltpu.VMEM((STEPS, 2, 8, 16, 128), BF),
            pltpu.VMEM((2, 8, 16, 128), BF),
            pltpu.VMEM((32, 256, 128), BF),
            pltpu.VMEM((32, 128, 128), BF),
            pltpu.VMEM((STEPS, 512, 640), BF),
            pltpu.VMEM((STEPS, 512, 256), BF),
            pltpu.VMEM((STEPS, 512, 128), BF),
            one,
            one, one, one, one, one, one,
            one, one, one, one,
            dma((16,)), one, one, one, dma((2, 2)), dma((2, 2)), two, two, four, four,
            four, four, four, four, dma((4, 2, 2)), dma((4, 2, 2)), dma((4, 2)), dma((4, 2)), four, four,
            one, one, dma((2, 2)), dma((2, 2)), two, two, four, four,
        ],
        compiler_params=pltpu.CompilerParams(
            collective_id=0, has_side_effects=True, vmem_limit_bytes=56 * 1024 * 1024
        ),
    )(ao_order, density, virt_coeff, block_coeff)


def solution(mesh):
    return jax.shard_map(
        shards,
        mesh=mesh,
        in_specs=(P("virt", "ao", None), P("virt", None), P("ao", None), P()),
        out_specs=P("ao", "virt", None),
        check_vma=False,
    )
```

```python
import jax
import jax.numpy as jnp
from jax import lax
from jax.experimental import pallas as pl
from jax.experimental.pallas import tpu as pltpu
from jax.sharding import PartitionSpec as P

MESH = pl.DeviceIdType.MESH
BF = jnp.bfloat16
F32 = jnp.float32
TN = (((0,), (0,)), ((), ()))
NT = (((1,), (1,)), ((), ()))
STEPS = 4
BLOCKS = [(y % 2, (y // 2) * 8 + x * 2 + c) for c in range(2) for x in range(4) for y in range(4)]
BLOCKS += [(y % 2, 16 + (y // 2) * 2 + h) for h in range(2) for y in range(4)]


def exchange(
    order_hbm, d_ref, c_ref, b_ref, o_ref,
    order, dl, cl, bl, hot, pt, kp, df, dp, cf, cp, s, r, rf, g, gh, tm, tq, hb, ho, hq,
    order_sem, ds, dr, des, der, dks, dkr, bs, br, bks, bkr, zcs, zcr, ycs, ycr, xcs, xcr, fcs, fcr, kcs, kcr,
    zs, zr, ys, yr, xs, xr, fs, fr, hs, hr, yhs, yhr, xhs, xhr, fhs, fhr, qs, qr,
):
    v, j = lax.axis_index("virt"), lax.axis_index("ao")
    y_lo, z = v // 16, v % 16
    core, x, y_hi = j % 2, (j // 2) % 4, j // 8
    y = 2 * y_hi + y_lo
    share = j % 4
    right, left, far = (x + 1) % 4, (x + 3) % 4, (x + 2) % 4
    chip = j // 2

    def lanes_of(yh, e):
        return pl.ds(pl.multiple_of(yh * 512 + core * 256 + e * 128, 128), 128)

    lanes = lanes_of(x // 2, x % 2)

    def dev(yy, xx):
        return (yy % 2) * 16 + z, (yy // 2) * 8 + xx * 2 + core

    other = (v, j + 1 - 2 * core)
    to_right, to_left = dev(y, right), dev(y, left)

    def remote(src, dst, send, recv, device):
        return pltpu.make_async_remote_copy(
            src_ref=src, dst_ref=dst, send_sem=send, recv_sem=recv, device_id=device, device_id_type=MESH
        )

    def arrived(ref, sem):
        remote(ref, ref, sem, sem, other).wait_recv()

    def left_for(ref, sem):
        remote(ref, ref, sem, sem, other).wait_send()

    order_copy = pltpu.make_async_copy(order_hbm, order, order_sem)
    order_copy.start()

    barrier = pltpu.get_barrier_semaphore()
    for dy in (1, 3):
        pl.semaphore_signal(barrier, inc=1, device_id=dev((y + dy) % 4, x), device_id_type=MESH)

    pl.semaphore_signal(barrier, inc=1, device_id=other, device_id_type=MESH)

    @pl.loop(1, 8)
    def _(t):
        pl.semaphore_signal(barrier, inc=1, device_id=(v, (j + 2 * t) % 16), device_id_type=MESH)

    @pl.loop(1, 16)
    def _(t):
        zv = y_lo * 16 + (z + t) % 16
        pl.semaphore_signal(barrier, inc=1, device_id=(zv, j), device_id_type=MESH)

        @pl.when(z // 8 != core)
        def _():
            pl.semaphore_signal(barrier, inc=1, device_id=(zv, j + 1 - 2 * core), device_id_type=MESH)

    pl.semaphore_wait(barrier, 32 + (z // 8 + core) % 2)

    @pl.loop(1, 16)
    def _(t):
        remote(c_ref.at[:, lanes], cl.at[x, y_lo, z], zcs.at[t], zcr, (y_lo * 16 + (z + t) % 16, j)).start()

    pltpu.make_async_copy(c_ref.at[:, lanes], cl.at[x, y_lo, z], zcr).start()

    @pl.loop(1, 8)
    def _(t):
        jj = (j + 2 * t) % 16
        remote(d_ref.at[pl.ds(jj // 2 * 2, 2)], dl.at[pl.ds(0, 2), core, chip], ds, dr, (v, jj)).start()
        remote(d_ref.at[16 + jj // 4], dl.at[2, core, chip], des, der, (v, jj)).start()

    pltpu.make_async_copy(d_ref.at[pl.ds(chip * 2, 2)], dl.at[pl.ds(0, 2), core, chip], dr).start()
    pltpu.make_async_copy(d_ref.at[16 + j // 4], dl.at[2, core, chip], der).start()

    order_copy.wait()
    column = lax.broadcasted_iota(jnp.int32, (1, 1024), 1)

    @pl.loop(0, 128)
    def _(k):
        hot[pl.ds(k, 1), :] = jnp.where(column == order[chip * 128 + k], 1.0, 0.0).astype(F32)

    arrived(cl.at[x, y_lo], zcr)
    for e, dy in enumerate((3, 1)):
        blk = cl.at[x, y_lo, pl.ds(e * 8, 8)]
        remote(blk, blk, ycs.at[e], ycr, dev((y + dy) % 4, x)).start()

    arrived(dl.at[pl.ds(0, 2), core], dr)
    arrived(dl.at[2, core], der)
    remote(dl.at[:, core], dl.at[:, core], dks, dkr, other).start()

    def both_ways(blocks, send, recv):
        for half in range(2):
            for way, device in enumerate((to_right, to_left)):
                blk = blocks(half ^ way)
                remote(blk, blk, send.at[way, half], recv.at[way, half], device).start()

    arrived(cl.at[x, 1 - y_lo], ycr)
    both_ways(lambda part: cl.at[x, part], xcs, xcr)

    arrived(dl.at[:, 1 - core], dkr)
    for u in range(3):
        for jj in range(16):
            df[u, pl.ds(jj * 40, 40), :] = dl[u, jj % 2, jj // 2].astype(F32)
        for q, (yl, i) in enumerate(BLOCKS):
            dp[pl.ds(q * 16, 16), pl.ds(u * 128, 128)] = df[u, pl.ds(yl * 320 + i, 16, stride=20), :].astype(BF)

    def relay(xx):
        for yl in range(2):
            for zz in range(16):
                cf[yl * 16 + zz, pl.ds(0, 20), :] = cl[xx, yl, zz].astype(F32)
        flat = cf.reshape(32 * 24, 128)
        to = lanes_of(xx // 2, xx % 2)
        for q, (yl, i) in enumerate(BLOCKS):
            cp[pl.ds(q * 16, 16), to] = flat[pl.ds(yl * 384 + i, 16, stride=24), :].astype(BF)

    relay(x)
    for way, (frm, device) in enumerate(((left, to_right), (right, to_left))):
        blk = cl.at[frm, way]
        arrived(blk, xcr.at[way, 0])
        remote(blk, blk, fcs.at[way], fcr.at[way], device).start()
    for way, frm in enumerate((left, right)):
        arrived(cl.at[frm, 1 - way], xcr.at[way, 1])
        relay(frm)
    for way in range(2):
        arrived(cl.at[far, way], fcr.at[way])
    relay(far)

    for yh in range(2):
        for e in range(2):
            tt = lax.dot_general(cp[:, lanes_of(yh, e)], dp[...], TN, preferred_element_type=F32).astype(BF)
            for q in range(4):
                for k in range(STEPS):
                    rows = tt[q * 32 + k * 8:q * 32 + k * 8 + 8]
                    s[0, k, e * 4 + q, pl.ds(yh * 8, 8), :] = rows[:, :128]
                    s[1, k, e * 4 + q, pl.ds(yh * 8, 8), :] = rows[:, 128:256]
                    s[k % 2, k, e * 4 + q, pl.ds(16 + yh * 8, 8), :] = rows[:, 256:]

    def whole(k, c):
        return jnp.logical_and(c == k % 2, x % 2 == k // 2)

    for k in range(STEPS):
        for c in range(2):
            def along_z(part):
                @pl.loop(0, 8)
                def _(w):
                    zl = (z + w) % 8
                    zz = core * 8 + zl
                    itself = jnp.logical_and(zz == z, c == core)

                    @pl.when(itself)
                    def _():
                        pltpu.make_async_copy(s.at[c, k, zl, part], r.at[k, z, part], zr.at[k]).start()

                    @pl.when(jnp.logical_not(itself))
                    def _():
                        remote(s.at[c, k, zl, part], r.at[k, z, part], zs.at[k, c], zr.at[k],
                               (y_lo * 16 + zz, chip * 2 + c)).start()

            @pl.when(whole(k, c))
            def _():
                along_z(pl.ds(0, 32))

            @pl.when(jnp.logical_not(whole(k, c)))
            def _():
                along_z(pl.ds(0, 16))

    for e in range(2):
        half = cp.at[:, pl.ds(pl.multiple_of(e * 512 + core * 256, 256), 256)]
        remote(half, half, kcs.at[e], kcr.at[e], other).start()

    @pl.loop(1, 8)
    def _(t):
        remote(b_ref, bl.at[core, chip], bs, br, (v, (j + 2 * t) % 16)).start()

    pltpu.make_async_copy(b_ref, bl.at[core, chip], br).start()

    def at(block, count=1):
        return pl.ds(pl.multiple_of(block * 16, 16), count * 16)

    def piece(k):
        return pl.ds(k * 8, 8)

    def turn(k, first, dst):
        for zz in range(16):
            rf[pl.ds(zz * 16, 16), :] = r[k, zz, pl.ds(first, 16), :].astype(F32)
        for i in range(16):
            dst[i // 8, i % 8] = rf[pl.ds(i, 16, stride=16), :].astype(BF)

    def main(k, xx, first=0, count=4):
        return tm.at[piece(k), at(xx * 4 + first, count), :]

    def pooled(k, xx, first=0, count=4):
        return tq.at[piece(k), at((xx // 2) * 4 + first, count), :]

    def along_y(k):
        @pl.when(share != k)
        def _():
            arrived(r.at[k, :, pl.ds(0, 16)], zr.at[k])

        @pl.when(share == k)
        def _():
            arrived(r.at[k], zr.at[k])

        turn(k, 0, g.at[k])
        for dy in (1, 3, 2):
            half = y_lo if dy == 2 else 1 - y_lo
            remote(g.at[k, half], main(k, x, y, 1), ys.at[k], yr.at[k], dev((y + dy) % 4, x)).start()
        tm[piece(k), at(x * 4 + y), :] = g[k, y_lo]

        @pl.when(share == k)
        def _():
            turn(k, 16, gh)
            for dy in (1, 3, 2):
                half = y_lo if dy == 2 else 1 - y_lo
                remote(gh.at[half], pooled(k, x, y, 1), yhs, yhr, dev((y + dy) % 4, x)).start()
            tq[piece(k), at((x // 2) * 4 + y), :] = gh[y_lo]

    def along_x(k):
        arrived(main(k, x, 0, 3), yr.at[k])
        both_ways(lambda part: main(k, x, 2 * part, 2), xs.at[k], xr.at[k])

        @pl.when(share == k)
        def _():
            arrived(pooled(k, x, 0, 3), yhr)
            both_ways(lambda part: pooled(k, x, 2 * part, 2), xhs, xhr)

    def between(k):
        return jnp.logical_and(core == k % 2, x % 2 != k // 2)

    def pass_on(k):
        for way, (frm, device) in enumerate(((left, to_right), (right, to_left))):
            blk = main(k, frm, 2 * way, 2)
            arrived(blk, xr.at[k, way, 0])
            remote(blk, blk, fs.at[k, way], fr.at[k, way], device).start()

        @pl.when(between(k))
        def _():
            for way, (frm, device) in enumerate(((left, to_right), (right, to_left))):
                blk = pooled(k, frm, 2 * way, 2)
                arrived(blk, xhr.at[way, 0])
                remote(blk, blk, fhs.at[way], fhr.at[way], device).start()

    def sides(k):
        for way, frm in enumerate((left, right)):
            arrived(main(k, frm, 2 - 2 * way, 2), xr.at[k, way, 1])

        @pl.when(between(k))
        def _():
            for way, frm in enumerate((left, right)):
                arrived(pooled(k, frm, 2 - 2 * way, 2), xhr.at[way, 1])

    mine_at = pl.ds(pl.multiple_of(core * 256, 256), 256)
    theirs_at = pl.ds(pl.multiple_of((1 - core) * 256, 256), 256)
    pool_at = pl.ds(512, 128)

    def to_s(k):
        arrived(main(k, far, 0, 2), fr.at[k, 0])
        arrived(main(k, far, 2, 2), fr.at[k, 1])
        terms = jnp.concatenate([tm[k * 8 + n] for n in range(8)], axis=1)
        ho[k] = lax.dot_general(kp[1 - core], terms, NT, preferred_element_type=F32).astype(BF)
        remote(ho.at[k], hb.at[k, :, mine_at], hs.at[k], hr.at[k], other).start()

        @pl.when(core == k % 2)
        def _():
            @pl.when(share == k)
            def _():
                arrived(pooled(k, far, 0, 2), fhr.at[0])
                arrived(pooled(k, far, 2, 2), fhr.at[1])

            terms = jnp.concatenate([tq[k * 8 + n] for n in range(8)], axis=1)
            hq[k] = lax.dot_general(kp[1 - core], terms, NT, preferred_element_type=F32).astype(BF)
            remote(hq.at[k], hb.at[k, :, pool_at], qs.at[k], qr.at[k], other).start()
            hb[k, :, pool_at] = lax.dot_general(kp[core], terms, NT, preferred_element_type=F32).astype(BF)

        terms = jnp.concatenate([tm[k * 8 + n] for n in range(8)], axis=1)
        hb[k, :, mine_at] = lax.dot_general(kp[core], terms, NT, preferred_element_type=F32).astype(BF)

    def to_m(k):
        arrived(hb.at[k, :, theirs_at], hr.at[k])

        @pl.when(core != k % 2)
        def _():
            arrived(hb.at[k, :, pool_at], qr.at[k])

        @pl.loop(0, 4)
        def _(q):
            cols = pl.ds(pl.multiple_of(q * 256, 256), 256)
            out = jnp.dot(hb[k], cp[:, cols], preferred_element_type=F32)
            o_ref[:, pl.ds(k * 8, 8), cols] = out.reshape(64, 8, 256).astype(BF)

    along_y(0)

    arrived(bl.at[core], br)
    remote(bl.at[core], bl.at[core], bks, bkr, other).start()
    arrived(bl.at[1 - core], bkr)
    block = jnp.concatenate([bl[q % 2, q // 2].astype(F32) for q in range(16)], axis=0).astype(BF)
    pt[...] = lax.dot_general(hot[...].astype(BF), block, NT, preferred_element_type=F32).astype(BF)
    spread = lax.broadcasted_iota(jnp.int32, (512, 64), 0) // 8 == lax.broadcasted_iota(jnp.int32, (512, 64), 1)
    place = lax.broadcasted_iota(jnp.int32, (512, 128), 0) % 8
    for e in range(2):
        panel = jnp.dot(jnp.where(spread, 1.0, 0.0).astype(BF), pt[e * 64:(e + 1) * 64], preferred_element_type=F32)
        for n in range(8):
            kp[e, :, pl.ds(n * 128, 128)] = jnp.where(place == n, panel, 0.0).astype(BF)

    for k in range(STEPS):
        along_x(k)
        if k == 1:
            for e in range(2):
                arrived(cp.at[:, pl.ds(pl.multiple_of(e * 512 + (1 - core) * 256, 256), 256)], kcr.at[e])
        if k + 1 < STEPS:
            along_y(k + 1)
        if k >= 2:
            to_m(k - 2)
        if k >= 1:
            to_s(k - 1)
        pass_on(k)
        sides(k)
    to_m(STEPS - 2)
    to_s(STEPS - 1)
    to_m(STEPS - 1)

    @pl.loop(1, 16)
    def _(t):
        left_for(c_ref.at[:, lanes], zcs.at[t])

    left_for(dl.at[pl.ds(0, 2), core, pl.ds(0, 7)], ds)
    left_for(dl.at[2, core, pl.ds(0, 7)], des)
    left_for(dl.at[:, core], dks)
    left_for(bl.at[core, pl.ds(0, 7)], bs)
    left_for(bl.at[core], bks)
    for e in range(2):
        left_for(cl.at[x, y_lo, pl.ds(0, 8)], ycs.at[e])
        for half in range(2):
            left_for(cl.at[x, 0], xcs.at[e, half])
        left_for(cl.at[x, 0], fcs.at[e])
        left_for(cp.at[:, pl.ds(e * 256, 256)], kcs.at[e])
    left_for(main(0, x, 0, 3), yhs)
    for e in range(2):
        for half in range(2):
            left_for(main(0, x, 0, 2), xhs.at[e, half])
        left_for(main(0, x, 0, 2), fhs.at[e])
    for k in range(STEPS):
        for c in range(2):
            itself = jnp.logical_and(z // 8 == core, c == core)
            for count, few in ((7, itself), (8, jnp.logical_not(itself))):
                @pl.when(jnp.logical_and(few, whole(k, c)))
                def _():
                    left_for(s.at[c, k, pl.ds(0, count)], zs.at[k, c])

                @pl.when(jnp.logical_and(few, jnp.logical_not(whole(k, c))))
                def _():
                    left_for(s.at[c, k, pl.ds(0, count), pl.ds(0, 16)], zs.at[k, c])

        left_for(main(k, x, 0, 3), ys.at[k])
        for e in range(2):
            for half in range(2):
                left_for(main(k, x, 0, 2), xs.at[k, e, half])
            left_for(main(k, x, 0, 2), fs.at[k, e])
        left_for(ho.at[k], hs.at[k])

        @pl.when(core == k % 2)
        def _():
            left_for(hq.at[k], qs.at[k])


def shards(density, virt_coeff, block_coeff, ao_order):
    hbm = pl.BlockSpec(memory_space=pltpu.HBM)
    dma = pltpu.SemaphoreType.DMA
    one, two, four = dma, dma((2,)), dma((4,))
    return pl.pallas_call(
        exchange,
        out_shape=pltpu.VMEM((64, 32, 1024), BF),
        in_specs=[hbm] * 4,
        out_specs=pl.BlockSpec(memory_space=pltpu.VMEM),
        scratch_shapes=[
            pltpu.SMEM((1024,), jnp.int32),
            pltpu.VMEM((3, 2, 8, 40, 128), BF),
            pltpu.VMEM((4, 2, 16, 20, 128), BF),
            pltpu.VMEM((2, 8, 8, 1024), BF),
            pltpu.VMEM((128, 1024), F32),
            pltpu.VMEM((128, 128), BF),
            pltpu.VMEM((2, 512, 1024), BF),
            pltpu.VMEM((3, 640, 128), F32),
            pltpu.VMEM((640, 384), BF),
            pltpu.VMEM((32, 24, 128), F32),
            pltpu.VMEM((640, 1024), BF),
            pltpu.VMEM((2, STEPS, 8, 32, 128), BF),
            pltpu.VMEM((STEPS, 16, 32, 128), BF),
            pltpu.VMEM((256, 128), F32),
            pltpu.VMEM((STEPS, 2, 8, 16, 128), BF),
            pltpu.VMEM((2, 8, 16, 128), BF),
            pltpu.VMEM((32, 256, 128), BF),
            pltpu.VMEM((32, 128, 128), BF),
            pltpu.VMEM((STEPS, 512, 640), BF),
            pltpu.VMEM((STEPS, 512, 256), BF),
            pltpu.VMEM((STEPS, 512, 128), BF),
            one,
            one, one, one, one, one, one,
            one, one, one, one,
            dma((16,)), one, two, one, dma((2, 2)), dma((2, 2)), two, two, two, two,
            dma((4, 2)), four, four, four, dma((4, 2, 2)), dma((4, 2, 2)), dma((4, 2)), dma((4, 2)), four, four,
            one, one, dma((2, 2)), dma((2, 2)), two, two, four, four,
        ],
        compiler_params=pltpu.CompilerParams(
            collective_id=0, has_side_effects=True, vmem_limit_bytes=56 * 1024 * 1024
        ),
    )(ao_order, density, virt_coeff, block_coeff)


def solution(mesh):
    return jax.shard_map(
        shards,
        mesh=mesh,
        in_specs=(P("virt", "ao", None), P("virt", None), P("ao", None), P()),
        out_specs=P("ao", "virt", None),
        check_vma=False,
    )
```

```python
import jax
import jax.numpy as jnp
from jax import lax
from jax.experimental import pallas as pl
from jax.experimental.pallas import tpu as pltpu
from jax.sharding import PartitionSpec as P

MESH = pl.DeviceIdType.MESH
BF = jnp.bfloat16
F32 = jnp.float32
TN = (((0,), (0,)), ((), ()))
NT = (((1,), (1,)), ((), ()))
STEPS = 4
BLOCKS = [(y % 2, (y // 2) * 8 + x * 2 + c) for c in range(2) for x in range(4) for y in range(4)]
BLOCKS += [(y % 2, 16 + (y // 2) * 2 + h) for h in range(2) for y in range(4)]


def exchange(
    order_hbm, d_ref, c_ref, b_ref, o_ref,
    order, dl, cl, bl, hot, pt, kp, df, dp, cf, cp, tt, s, r, rf, g, gh, tm, tq, hb, ho, hq,
    order_sem, ds, dr, des, der, dks, dkr, bs, br, bks, bkr, zcs, zcr, ycs, ycr, xcs, xcr, fcs, fcr, kcs, kcr,
    zs, zr, ys, yr, xs, xr, fs, fr, hs, hr, yhs, yhr, xhs, xhr, fhs, fhr, qs, qr,
):
    v, j = lax.axis_index("virt"), lax.axis_index("ao")
    y_lo, z = v // 16, v % 16
    core, x, y_hi = j % 2, (j // 2) % 4, j // 8
    y = 2 * y_hi + y_lo
    share = j % 4
    right, left, far = (x + 1) % 4, (x + 3) % 4, (x + 2) % 4
    chip = j // 2

    def lanes_of(yh, e):
        return pl.ds(pl.multiple_of(yh * 512 + core * 256 + e * 128, 128), 128)

    lanes = lanes_of(x // 2, x % 2)

    def dev(yy, xx):
        return (yy % 2) * 16 + z, (yy // 2) * 8 + xx * 2 + core

    other = (v, j + 1 - 2 * core)
    to_right, to_left = dev(y, right), dev(y, left)

    def remote(src, dst, send, recv, device):
        return pltpu.make_async_remote_copy(
            src_ref=src, dst_ref=dst, send_sem=send, recv_sem=recv, device_id=device, device_id_type=MESH
        )

    def arrived(ref, sem):
        remote(ref, ref, sem, sem, other).wait_recv()

    def left_for(ref, sem):
        remote(ref, ref, sem, sem, other).wait_send()

    order_copy = pltpu.make_async_copy(order_hbm, order, order_sem)
    order_copy.start()

    barrier = pltpu.get_barrier_semaphore()
    for dy in (1, 3):
        pl.semaphore_signal(barrier, inc=1, device_id=dev((y + dy) % 4, x), device_id_type=MESH)

    pl.semaphore_signal(barrier, inc=1, device_id=other, device_id_type=MESH)

    @pl.loop(1, 8)
    def _(t):
        pl.semaphore_signal(barrier, inc=1, device_id=(v, (j + 2 * t) % 16), device_id_type=MESH)

    @pl.loop(1, 16)
    def _(t):
        zv = y_lo * 16 + (z + t) % 16
        pl.semaphore_signal(barrier, inc=1, device_id=(zv, j), device_id_type=MESH)

        @pl.when(z // 8 != core)
        def _():
            pl.semaphore_signal(barrier, inc=1, device_id=(zv, j + 1 - 2 * core), device_id_type=MESH)

    pl.semaphore_wait(barrier, 32 + (z // 8 + core) % 2)

    @pl.loop(1, 16)
    def _(t):
        remote(c_ref.at[:, lanes], cl.at[x, y_lo, z], zcs.at[t], zcr, (y_lo * 16 + (z + t) % 16, j)).start()

    pltpu.make_async_copy(c_ref.at[:, lanes], cl.at[x, y_lo, z], zcr).start()

    @pl.loop(1, 8)
    def _(t):
        jj = (j + 2 * t) % 16
        remote(d_ref.at[pl.ds(jj // 2 * 2, 2)], dl.at[pl.ds(0, 2), core, chip], ds, dr, (v, jj)).start()
        remote(d_ref.at[16 + jj // 4], dl.at[2, core, chip], des, der, (v, jj)).start()

    pltpu.make_async_copy(d_ref.at[pl.ds(chip * 2, 2)], dl.at[pl.ds(0, 2), core, chip], dr).start()
    pltpu.make_async_copy(d_ref.at[16 + j // 4], dl.at[2, core, chip], der).start()

    order_copy.wait()
    column = lax.broadcasted_iota(jnp.int32, (1, 1024), 1)

    @pl.loop(0, 128)
    def _(k):
        hot[pl.ds(k, 1), :] = jnp.where(column == order[chip * 128 + k], 1.0, 0.0).astype(F32)

    def coeff_x(part, yl):
        blk = cl.at[x, yl]
        remote(blk, blk, xcs.at[0, part], xcr.at[0, part], to_right).start()
        remote(blk, blk, xcs.at[1, part], xcr.at[1, part], to_left).start()

    def coeff_on(part, yl):
        for way, (frm, device) in enumerate(((left, to_right), (right, to_left))):
            arrived(cl.at[frm, yl], xcr.at[way, part])
            blk = cl.at[frm, yl, pl.ds(way * 8, 8)]
            remote(blk, blk, fcs.at[way, part], fcr.at[way, part], device).start()

    arrived(cl.at[x, y_lo], zcr)
    for e, dy in enumerate((3, 1)):
        blk = cl.at[x, y_lo, pl.ds(e * 8, 8)]
        remote(blk, blk, ycs.at[e], ycr, dev((y + dy) % 4, x)).start()
    coeff_x(0, y_lo)

    arrived(dl.at[pl.ds(0, 2), core], dr)
    arrived(dl.at[2, core], der)
    remote(dl.at[:, core], dl.at[:, core], dks, dkr, other).start()

    arrived(cl.at[x, 1 - y_lo], ycr)
    coeff_x(1, 1 - y_lo)
    coeff_on(0, y_lo)

    arrived(dl.at[:, 1 - core], dkr)
    for u in range(3):
        for jj in range(16):
            df[u, pl.ds(jj * 40, 40), :] = dl[u, jj % 2, jj // 2].astype(F32)
        for q, (yl, i) in enumerate(BLOCKS):
            dp[pl.ds(q * 16, 16), pl.ds(u * 128, 128)] = df[u, pl.ds(yl * 320 + i, 16, stride=20), :].astype(BF)

    coeff_on(1, 1 - y_lo)

    @pl.loop(1, 8)
    def _(t):
        remote(b_ref, bl.at[core, chip], bs, br, (v, (j + 2 * t) % 16)).start()

    pltpu.make_async_copy(b_ref, bl.at[core, chip], br).start()

    def both_ways(blocks, send, recv):
        for half in range(2):
            for way, device in enumerate((to_right, to_left)):
                blk = blocks(half ^ way)
                remote(blk, blk, send.at[way, half], recv.at[way, half], device).start()

    def relay(xx):
        for yl in range(2):
            for zz in range(16):
                cf[yl * 16 + zz, pl.ds(0, 20), :] = cl[xx, yl, zz].astype(F32)
        flat = cf.reshape(32 * 24, 128)
        to = lanes_of(xx // 2, xx % 2)
        for q, (yl, i) in enumerate(BLOCKS):
            cp[pl.ds(q * 16, 16), to] = flat[pl.ds(yl * 384 + i, 16, stride=24), :].astype(BF)
        tt[xx] = lax.dot_general(cp[:, to], dp[...], TN, preferred_element_type=F32).astype(BF)

    relay(x)
    relay(left)
    relay(right)
    for way in range(2):
        arrived(cl.at[far, y_lo, pl.ds(way * 8, 8)], fcr.at[way, 0])
        arrived(cl.at[far, 1 - y_lo, pl.ds(way * 8, 8)], fcr.at[way, 1])
    relay(far)

    def regroup(k):
        for yh in range(2):
            for e in range(2):
                for q in range(4):
                    rows = tt[2 * yh + e, q * 32 + k * 8:q * 32 + k * 8 + 8, :]
                    s[0, k, e * 4 + q, pl.ds(yh * 8, 8), :] = rows[:, :128]
                    s[1, k, e * 4 + q, pl.ds(yh * 8, 8), :] = rows[:, 128:256]
                    s[k % 2, k, e * 4 + q, pl.ds(16 + yh * 8, 8), :] = rows[:, 256:]

    def whole(k, c):
        return jnp.logical_and(c == k % 2, x % 2 == k // 2)

    def to_planes(k):
        for c in range(2):
            def along_z(part):
                @pl.loop(0, 8)
                def _(w):
                    zl = (z + w) % 8
                    zz = core * 8 + zl
                    itself = jnp.logical_and(zz == z, c == core)

                    @pl.when(itself)
                    def _():
                        pltpu.make_async_copy(s.at[c, k, zl, part], r.at[k, z, part], zr.at[k]).start()

                    @pl.when(jnp.logical_not(itself))
                    def _():
                        remote(s.at[c, k, zl, part], r.at[k, z, part], zs.at[k, c], zr.at[k],
                               (y_lo * 16 + zz, chip * 2 + c)).start()

            @pl.when(whole(k, c))
            def _():
                along_z(pl.ds(0, 32))

            @pl.when(jnp.logical_not(whole(k, c)))
            def _():
                along_z(pl.ds(0, 16))

    def at(block, count=1):
        return pl.ds(pl.multiple_of(block * 16, 16), count * 16)

    def piece(k):
        return pl.ds(k * 8, 8)

    def turn(k, first, dst):
        for zz in range(16):
            rf[pl.ds(zz * 16, 16), :] = r[k, zz, pl.ds(first, 16), :].astype(F32)
        for i in range(16):
            dst[i // 8, i % 8] = rf[pl.ds(i, 16, stride=16), :].astype(BF)

    def main(k, xx, first=0, count=4):
        return tm.at[piece(k), at(xx * 4 + first, count), :]

    def pooled(k, xx, first=0, count=4):
        return tq.at[piece(k), at((xx // 2) * 4 + first, count), :]

    def along_y(k):
        @pl.when(share != k)
        def _():
            arrived(r.at[k, :, pl.ds(0, 16)], zr.at[k])

        @pl.when(share == k)
        def _():
            arrived(r.at[k], zr.at[k])

        turn(k, 0, g.at[k])
        for dy in (1, 3, 2):
            half = y_lo if dy == 2 else 1 - y_lo
            remote(g.at[k, half], main(k, x, y, 1), ys.at[k], yr.at[k], dev((y + dy) % 4, x)).start()
        tm[piece(k), at(x * 4 + y), :] = g[k, y_lo]

        @pl.when(share == k)
        def _():
            turn(k, 16, gh)
            for dy in (1, 3, 2):
                half = y_lo if dy == 2 else 1 - y_lo
                remote(gh.at[half], pooled(k, x, y, 1), yhs, yhr, dev((y + dy) % 4, x)).start()
            tq[piece(k), at((x // 2) * 4 + y), :] = gh[y_lo]

    def along_x(k):
        arrived(main(k, x, 0, 3), yr.at[k])
        both_ways(lambda part: main(k, x, 2 * part, 2), xs.at[k], xr.at[k])

        @pl.when(share == k)
        def _():
            arrived(pooled(k, x, 0, 3), yhr)
            both_ways(lambda part: pooled(k, x, 2 * part, 2), xhs, xhr)

    def between(k):
        return jnp.logical_and(core == k % 2, x % 2 != k // 2)

    def pass_on(k):
        for way, (frm, device) in enumerate(((left, to_right), (right, to_left))):
            blk = main(k, frm, 2 * way, 2)
            arrived(blk, xr.at[k, way, 0])
            remote(blk, blk, fs.at[k, way], fr.at[k, way], device).start()

        @pl.when(between(k))
        def _():
            for way, (frm, device) in enumerate(((left, to_right), (right, to_left))):
                blk = pooled(k, frm, 2 * way, 2)
                arrived(blk, xhr.at[way, 0])
                remote(blk, blk, fhs.at[way], fhr.at[way], device).start()

    def sides(k):
        for way, frm in enumerate((left, right)):
            arrived(main(k, frm, 2 - 2 * way, 2), xr.at[k, way, 1])

        @pl.when(between(k))
        def _():
            for way, frm in enumerate((left, right)):
                arrived(pooled(k, frm, 2 - 2 * way, 2), xhr.at[way, 1])

    mine_at = pl.ds(pl.multiple_of(core * 256, 256), 256)
    theirs_at = pl.ds(pl.multiple_of((1 - core) * 256, 256), 256)
    pool_at = pl.ds(512, 128)

    def to_s(k):
        arrived(main(k, far, 0, 2), fr.at[k, 0])
        arrived(main(k, far, 2, 2), fr.at[k, 1])
        terms = jnp.concatenate([tm[k * 8 + n] for n in range(8)], axis=1)
        ho[k] = lax.dot_general(kp[1 - core], terms, NT, preferred_element_type=F32).astype(BF)
        remote(ho.at[k], hb.at[k, :, mine_at], hs.at[k], hr.at[k], other).start()

        @pl.when(core == k % 2)
        def _():
            @pl.when(share == k)
            def _():
                arrived(pooled(k, far, 0, 2), fhr.at[0])
                arrived(pooled(k, far, 2, 2), fhr.at[1])

            terms = jnp.concatenate([tq[k * 8 + n] for n in range(8)], axis=1)
            hq[k] = lax.dot_general(kp[1 - core], terms, NT, preferred_element_type=F32).astype(BF)
            remote(hq.at[k], hb.at[k, :, pool_at], qs.at[k], qr.at[k], other).start()
            hb[k, :, pool_at] = lax.dot_general(kp[core], terms, NT, preferred_element_type=F32).astype(BF)

        terms = jnp.concatenate([tm[k * 8 + n] for n in range(8)], axis=1)
        hb[k, :, mine_at] = lax.dot_general(kp[core], terms, NT, preferred_element_type=F32).astype(BF)

    def to_m(k):
        arrived(hb.at[k, :, theirs_at], hr.at[k])

        @pl.when(core != k % 2)
        def _():
            arrived(hb.at[k, :, pool_at], qr.at[k])

        @pl.loop(0, 4)
        def _(q):
            cols = pl.ds(pl.multiple_of(q * 256, 256), 256)
            out = jnp.dot(hb[k], cp[:, cols], preferred_element_type=F32)
            o_ref[:, pl.ds(k * 8, 8), cols] = out.reshape(64, 8, 256).astype(BF)

    for k in range(3):
        regroup(k)
        to_planes(k)
    along_y(0)
    regroup(3)
    to_planes(3)

    arrived(bl.at[core], br)
    remote(bl.at[core], bl.at[core], bks, bkr, other).start()
    arrived(bl.at[1 - core], bkr)
    block = jnp.concatenate([bl[q % 2, q // 2].astype(F32) for q in range(16)], axis=0).astype(BF)
    pt[...] = lax.dot_general(hot[...].astype(BF), block, NT, preferred_element_type=F32).astype(BF)
    spread = lax.broadcasted_iota(jnp.int32, (512, 64), 0) // 8 == lax.broadcasted_iota(jnp.int32, (512, 64), 1)
    place = lax.broadcasted_iota(jnp.int32, (512, 128), 0) % 8
    for e in range(2):
        panel = jnp.dot(jnp.where(spread, 1.0, 0.0).astype(BF), pt[e * 64:(e + 1) * 64], preferred_element_type=F32)
        for n in range(8):
            kp[e, :, pl.ds(n * 128, 128)] = jnp.where(place == n, panel, 0.0).astype(BF)

    for k in range(STEPS):
        along_x(k)
        if k == 0:
            for e in range(2):
                half = cp.at[:, pl.ds(pl.multiple_of(e * 512 + core * 256, 256), 256)]
                remote(half, half, kcs.at[e], kcr.at[e], other).start()
        if k == 2:
            for e in range(2):
                arrived(cp.at[:, pl.ds(pl.multiple_of(e * 512 + (1 - core) * 256, 256), 256)], kcr.at[e])
        if k + 1 < STEPS:
            along_y(k + 1)
        if k >= 2:
            to_m(k - 2)
        if k >= 1:
            to_s(k - 1)
        pass_on(k)
        sides(k)
    to_m(STEPS - 2)
    to_s(STEPS - 1)
    to_m(STEPS - 1)

    @pl.loop(1, 16)
    def _(t):
        left_for(c_ref.at[:, lanes], zcs.at[t])

    left_for(dl.at[pl.ds(0, 2), core, pl.ds(0, 7)], ds)
    left_for(dl.at[2, core, pl.ds(0, 7)], des)
    left_for(dl.at[:, core], dks)
    left_for(bl.at[core, pl.ds(0, 7)], bs)
    left_for(bl.at[core], bks)
    for e in range(2):
        left_for(cl.at[x, y_lo, pl.ds(0, 8)], ycs.at[e])
        for half in range(2):
            left_for(cl.at[x, 0], xcs.at[e, half])
            left_for(cl.at[x, 0, pl.ds(0, 8)], fcs.at[e, half])
        left_for(cp.at[:, pl.ds(e * 256, 256)], kcs.at[e])
    left_for(main(0, x, 0, 3), yhs)
    for e in range(2):
        for half in range(2):
            left_for(main(0, x, 0, 2), xhs.at[e, half])
        left_for(main(0, x, 0, 2), fhs.at[e])
    for k in range(STEPS):
        for c in range(2):
            itself = jnp.logical_and(z // 8 == core, c == core)
            for count, few in ((7, itself), (8, jnp.logical_not(itself))):
                @pl.when(jnp.logical_and(few, whole(k, c)))
                def _():
                    left_for(s.at[c, k, pl.ds(0, count)], zs.at[k, c])

                @pl.when(jnp.logical_and(few, jnp.logical_not(whole(k, c))))
                def _():
                    left_for(s.at[c, k, pl.ds(0, count), pl.ds(0, 16)], zs.at[k, c])

        left_for(main(k, x, 0, 3), ys.at[k])
        for e in range(2):
            for half in range(2):
                left_for(main(k, x, 0, 2), xs.at[k, e, half])
            left_for(main(k, x, 0, 2), fs.at[k, e])
        left_for(ho.at[k], hs.at[k])

        @pl.when(core == k % 2)
        def _():
            left_for(hq.at[k], qs.at[k])


def shards(density, virt_coeff, block_coeff, ao_order):
    hbm = pl.BlockSpec(memory_space=pltpu.HBM)
    dma = pltpu.SemaphoreType.DMA
    one, two, four = dma, dma((2,)), dma((4,))
    return pl.pallas_call(
        exchange,
        out_shape=pltpu.VMEM((64, 32, 1024), BF),
        in_specs=[hbm] * 4,
        out_specs=pl.BlockSpec(memory_space=pltpu.VMEM),
        scratch_shapes=[
            pltpu.SMEM((1024,), jnp.int32),
            pltpu.VMEM((3, 2, 8, 40, 128), BF),
            pltpu.VMEM((4, 2, 16, 20, 128), BF),
            pltpu.VMEM((2, 8, 8, 1024), BF),
            pltpu.VMEM((128, 1024), F32),
            pltpu.VMEM((128, 128), BF),
            pltpu.VMEM((2, 512, 1024), BF),
            pltpu.VMEM((3, 640, 128), F32),
            pltpu.VMEM((640, 384), BF),
            pltpu.VMEM((32, 24, 128), F32),
            pltpu.VMEM((640, 1024), BF),
            pltpu.VMEM((4, 128, 384), BF),
            pltpu.VMEM((2, STEPS, 8, 32, 128), BF),
            pltpu.VMEM((STEPS, 16, 32, 128), BF),
            pltpu.VMEM((256, 128), F32),
            pltpu.VMEM((STEPS, 2, 8, 16, 128), BF),
            pltpu.VMEM((2, 8, 16, 128), BF),
            pltpu.VMEM((32, 256, 128), BF),
            pltpu.VMEM((32, 128, 128), BF),
            pltpu.VMEM((STEPS, 512, 640), BF),
            pltpu.VMEM((STEPS, 512, 256), BF),
            pltpu.VMEM((STEPS, 512, 128), BF),
            one,
            one, one, one, one, one, one,
            one, one, one, one,
            dma((16,)), one, two, one, dma((2, 2)), dma((2, 2)), dma((2, 2)), dma((2, 2)), two, two,
            dma((4, 2)), four, four, four, dma((4, 2, 2)), dma((4, 2, 2)), dma((4, 2)), dma((4, 2)), four, four,
            one, one, dma((2, 2)), dma((2, 2)), two, two, four, four,
        ],
        compiler_params=pltpu.CompilerParams(
            collective_id=0, has_side_effects=True, vmem_limit_bytes=56 * 1024 * 1024
        ),
    )(ao_order, density, virt_coeff, block_coeff)


def solution(mesh):
    return jax.shard_map(
        shards,
        mesh=mesh,
        in_specs=(P("virt", "ao", None), P("virt", None), P("ao", None), P()),
        out_specs=P("ao", "virt", None),
        check_vma=False,
    )
```

```python
import jax
import jax.numpy as jnp
from jax import lax
from jax.experimental import pallas as pl
from jax.experimental.pallas import tpu as pltpu
from jax.sharding import PartitionSpec as P

MESH = pl.DeviceIdType.MESH
BF = jnp.bfloat16
F32 = jnp.float32
TN = (((0,), (0,)), ((), ()))
NT = (((1,), (1,)), ((), ()))
STEPS = 4
BLOCKS = [(y % 2, (y // 2) * 8 + x * 2 + c) for c in range(2) for x in range(4) for y in range(4)]
BLOCKS += [(y % 2, 16 + (y // 2) * 2 + h) for h in range(2) for y in range(4)]


def exchange(
    order_hbm, d_ref, c_ref, b_ref, o_ref,
    order, dl, cl, bl, hot, pt, kp, df, dp, cf, cp, tt, s, r, rf, g, gh, gx, tm, tq, hb, ho, hq,
    order_sem, ds, dr, des, der, dks, dkr, bs, br, bks, bkr, zcs, zcr, ycs, ycr, xcs, xcr, fcs, fcr, kcs, kcr,
    zs, zr, ys, yr, xs, xr, fs, fr, hs, hr, yhs, yhr, xhs, xhr, fhs, fhr, qs, qr,
):
    v, j = lax.axis_index("virt"), lax.axis_index("ao")
    y_lo, z = v // 16, v % 16
    core, x, y_hi = j % 2, (j // 2) % 4, j // 8
    y = 2 * y_hi + y_lo
    share = j % 4
    right, left, far = (x + 1) % 4, (x + 3) % 4, (x + 2) % 4
    chip = j // 2

    def lanes_of(yh, e):
        return pl.ds(pl.multiple_of(yh * 512 + core * 256 + e * 128, 128), 128)

    lanes = lanes_of(x // 2, x % 2)

    def dev(yy, xx):
        return (yy % 2) * 16 + z, (yy // 2) * 8 + xx * 2 + core

    other = (v, j + 1 - 2 * core)
    to_right, to_left = dev(y, right), dev(y, left)

    def remote(src, dst, send, recv, device):
        return pltpu.make_async_remote_copy(
            src_ref=src, dst_ref=dst, send_sem=send, recv_sem=recv, device_id=device, device_id_type=MESH
        )

    def arrived(ref, sem):
        remote(ref, ref, sem, sem, other).wait_recv()

    def left_for(ref, sem):
        remote(ref, ref, sem, sem, other).wait_send()

    order_copy = pltpu.make_async_copy(order_hbm, order, order_sem)
    order_copy.start()

    barrier = pltpu.get_barrier_semaphore()

    def to_and_fro(w):
        return (w + 1) // 2 * (1 - 2 * (w % 2))

    @pl.loop(0, 15)
    def _(w):
        zv = y_lo * 16 + (z + 8 + to_and_fro(w)) % 16
        pl.semaphore_signal(barrier, inc=1, device_id=(zv, j), device_id_type=MESH)

        @pl.when(z // 8 != core)
        def _():
            pl.semaphore_signal(barrier, inc=1, device_id=(zv, j + 1 - 2 * core), device_id_type=MESH)

    for dy in (1, 3):
        pl.semaphore_signal(barrier, inc=1, device_id=dev((y + dy) % 4, x), device_id_type=MESH)

    pl.semaphore_signal(barrier, inc=1, device_id=other, device_id_type=MESH)

    @pl.loop(1, 8)
    def _(t):
        pl.semaphore_signal(barrier, inc=1, device_id=(v, (j + 2 * t) % 16), device_id_type=MESH)

    pl.semaphore_wait(barrier, 32 + (z // 8 + core) % 2)

    @pl.loop(0, 15)
    def _(w):
        zv = y_lo * 16 + (z + 8 + to_and_fro(w)) % 16
        remote(c_ref.at[:, lanes], cl.at[x, y_lo, z], zcs.at[w], zcr, (zv, j)).start()

    pltpu.make_async_copy(c_ref.at[:, lanes], cl.at[x, y_lo, z], zcr).start()

    @pl.loop(1, 8)
    def _(t):
        jj = (j + 2 * t) % 16
        remote(d_ref.at[pl.ds(jj // 2 * 2, 2)], dl.at[pl.ds(0, 2), core, chip], ds, dr, (v, jj)).start()
        remote(d_ref.at[16 + jj // 4], dl.at[2, core, chip], des, der, (v, jj)).start()

    pltpu.make_async_copy(d_ref.at[pl.ds(chip * 2, 2)], dl.at[pl.ds(0, 2), core, chip], dr).start()
    pltpu.make_async_copy(d_ref.at[16 + j // 4], dl.at[2, core, chip], der).start()

    order_copy.wait()
    column = lax.broadcasted_iota(jnp.int32, (1, 1024), 1)

    @pl.loop(0, 128)
    def _(k):
        hot[pl.ds(k, 1), :] = jnp.where(column == order[chip * 128 + k], 1.0, 0.0).astype(F32)

    def coeff_x(part, yl):
        blk = cl.at[x, yl]
        remote(blk, blk, xcs.at[0, part], xcr.at[0, part], to_right).start()
        remote(blk, blk, xcs.at[1, part], xcr.at[1, part], to_left).start()

    def coeff_on(part, yl):
        for way, (frm, device) in enumerate(((left, to_right), (right, to_left))):
            arrived(cl.at[frm, yl], xcr.at[way, part])
            blk = cl.at[frm, yl, pl.ds(way * 8, 8)]
            remote(blk, blk, fcs.at[way, part], fcr.at[way, part], device).start()

    arrived(cl.at[x, y_lo], zcr)
    for e, dy in enumerate((3, 1)):
        blk = cl.at[x, y_lo, pl.ds(e * 8, 8)]
        remote(blk, blk, ycs.at[e], ycr, dev((y + dy) % 4, x)).start()
    coeff_x(0, y_lo)

    arrived(dl.at[pl.ds(0, 2), core], dr)
    arrived(dl.at[2, core], der)
    remote(dl.at[:, core], dl.at[:, core], dks, dkr, other).start()

    arrived(cl.at[x, 1 - y_lo], ycr)
    coeff_x(1, 1 - y_lo)
    coeff_on(0, y_lo)

    arrived(dl.at[:, 1 - core], dkr)
    for u in range(3):
        for jj in range(16):
            df[u, pl.ds(jj * 40, 40), :] = dl[u, jj % 2, jj // 2].astype(F32)
        for q, (yl, i) in enumerate(BLOCKS):
            dp[pl.ds(q * 16, 16), pl.ds(u * 128, 128)] = df[u, pl.ds(yl * 320 + i, 16, stride=20), :].astype(BF)

    coeff_on(1, 1 - y_lo)

    @pl.loop(1, 8)
    def _(t):
        remote(b_ref, bl.at[core, chip], bs, br, (v, (j + 2 * t) % 16)).start()

    pltpu.make_async_copy(b_ref, bl.at[core, chip], br).start()

    def both_ways(blocks, send, recv):
        for half in range(2):
            for way, device in enumerate((to_right, to_left)):
                blk = blocks(half ^ way)
                remote(blk, blk, send.at[way, half], recv.at[way, half], device).start()

    def relay(xx):
        for yl in range(2):
            for zz in range(16):
                cf[yl * 16 + zz, pl.ds(0, 20), :] = cl[xx, yl, zz].astype(F32)
        flat = cf.reshape(32 * 24, 128)
        to = lanes_of(xx // 2, xx % 2)
        for q, (yl, i) in enumerate(BLOCKS):
            cp[pl.ds(q * 16, 16), to] = flat[pl.ds(yl * 384 + i, 16, stride=24), :].astype(BF)
        tt[xx] = lax.dot_general(cp[:, to], dp[...], TN, preferred_element_type=F32).astype(BF)

    relay(x)
    relay(left)
    relay(right)
    for way in range(2):
        arrived(cl.at[far, y_lo, pl.ds(way * 8, 8)], fcr.at[way, 0])
        arrived(cl.at[far, 1 - y_lo, pl.ds(way * 8, 8)], fcr.at[way, 1])
    relay(far)

    def regroup(k):
        for yh in range(2):
            for e in range(2):
                for q in range(4):
                    rows = tt[2 * yh + e, q * 32 + k * 8:q * 32 + k * 8 + 8, :]
                    s[0, k, e * 4 + q, pl.ds(yh * 8, 8), :] = rows[:, :128]
                    s[1, k, e * 4 + q, pl.ds(yh * 8, 8), :] = rows[:, 128:256]
                    s[k % 2, k, e * 4 + q, pl.ds(16 + yh * 8, 8), :] = rows[:, 256:]

    def whole(k, c):
        return jnp.logical_and(c == k % 2, x % 2 == k // 2)

    start = 8 + 4 * (1 - (z // 8 + core) % 2)

    def to_planes(k):
        for c in range(2):
            def along_z(part):
                @pl.loop(0, 8)
                def _(w):
                    zl = (z + start + to_and_fro(w)) % 8
                    zz = core * 8 + zl
                    itself = jnp.logical_and(zz == z, c == core)

                    @pl.when(itself)
                    def _():
                        pltpu.make_async_copy(s.at[c, k, zl, part], r.at[k, z, part], zr.at[k]).start()

                    @pl.when(jnp.logical_not(itself))
                    def _():
                        remote(s.at[c, k, zl, part], r.at[k, z, part], zs.at[k, c], zr.at[k],
                               (y_lo * 16 + zz, chip * 2 + c)).start()

            @pl.when(whole(k, c))
            def _():
                along_z(pl.ds(0, 32))

            @pl.when(jnp.logical_not(whole(k, c)))
            def _():
                along_z(pl.ds(0, 16))

    def at(block, count=1):
        return pl.ds(pl.multiple_of(block * 16, 16), count * 16)

    def piece(k):
        return pl.ds(k * 8, 8)

    def turn(k, first, dst):
        for zz in range(16):
            rf[pl.ds(zz * 16, 16), :] = r[k, zz, pl.ds(first, 16), :].astype(F32)
        for i in range(16):
            dst[i // 8, i % 8] = rf[pl.ds(i, 16, stride=16), :].astype(BF)

    def main(k, xx, first=0, count=4):
        return tm.at[piece(k), at(xx * 4 + first, count), :]

    def pooled(k, xx):
        return gx.at[k // 2, :, :, xx // 2]

    def along_y(k):
        @pl.when(share != k)
        def _():
            arrived(r.at[k, :, pl.ds(0, 16)], zr.at[k])

        @pl.when(share == k)
        def _():
            arrived(r.at[k], zr.at[k])

        turn(k, 0, g.at[k])
        for dy in (1, 3, 2):
            half = y_lo if dy == 2 else 1 - y_lo
            remote(g.at[k, half], main(k, x, y, 1), ys.at[k], yr.at[k], dev((y + dy) % 4, x)).start()
        tm[piece(k), at(x * 4 + y), :] = g[k, y_lo]

        @pl.when(share == k)
        def _():
            turn(k, 16, gh)
            gx[k // 2, :, :, x // 2] = gh[...]
            for way, device in enumerate((to_right, to_left)):
                remote(pooled(k, x), pooled(k, x), xhs.at[way], xhr.at[way], device).start()

    def along_x(k):
        arrived(main(k, x, 0, 3), yr.at[k])
        both_ways(lambda part: main(k, x, 2 * part, 2), xs.at[k], xr.at[k])

        @pl.when(jnp.logical_and(core == k % 2, x % 2 != k // 2))
        def _():
            for way, (frm, device) in enumerate(((left, to_right), (right, to_left))):
                arrived(pooled(k, frm), xhr.at[way])
                blk = gx.at[k // 2, way, :, frm // 2]
                remote(blk, blk, fhs.at[way], fhr.at[way], device).start()

    def pass_on(k):
        for way, (frm, device) in enumerate(((left, to_right), (right, to_left))):
            blk = main(k, frm, 2 * way, 2)
            arrived(blk, xr.at[k, way, 0])
            remote(blk, blk, fs.at[k, way], fr.at[k, way], device).start()

        @pl.when(core == k % 2)
        def _():
            @pl.when(share == k)
            def _():
                for way in range(2):
                    arrived(gx.at[k // 2, way, :, far // 2], fhr.at[way])

            for dy in (1, 3, 2):
                half = y_lo if dy == 2 else 1 - y_lo
                remote(gx.at[k // 2, half], tq.at[piece(k), :, y], yhs.at[k // 2], yhr.at[k // 2], dev((y + dy) % 4, x)).start()
            tq[piece(k), :, y] = gx[k // 2, y_lo]

    def sides(k):
        for way, frm in enumerate((left, right)):
            arrived(main(k, frm, 2 - 2 * way, 2), xr.at[k, way, 1])

    mine_at = pl.ds(pl.multiple_of(core * 256, 256), 256)
    theirs_at = pl.ds(pl.multiple_of((1 - core) * 256, 256), 256)
    pool_at = pl.ds(512, 128)

    def to_s(k):
        arrived(main(k, far, 0, 2), fr.at[k, 0])
        arrived(main(k, far, 2, 2), fr.at[k, 1])
        terms = jnp.concatenate([tm[k * 8 + n] for n in range(8)], axis=1)
        ho[k] = lax.dot_general(kp[1 - core], terms, NT, preferred_element_type=F32).astype(BF)
        remote(ho.at[k], hb.at[k, :, mine_at], hs.at[k], hr.at[k], other).start()

        @pl.when(core == k % 2)
        def _():
            arrived(tq.at[piece(k), :, pl.ds(0, 3)], yhr.at[k // 2])
            terms = jnp.concatenate([tq[k * 8 + n].reshape(128, 128) for n in range(8)], axis=1)
            hq[k] = lax.dot_general(kp[1 - core], terms, NT, preferred_element_type=F32).astype(BF)
            remote(hq.at[k], hb.at[k, :, pool_at], qs.at[k], qr.at[k], other).start()
            hb[k, :, pool_at] = lax.dot_general(kp[core], terms, NT, preferred_element_type=F32).astype(BF)

        terms = jnp.concatenate([tm[k * 8 + n] for n in range(8)], axis=1)
        hb[k, :, mine_at] = lax.dot_general(kp[core], terms, NT, preferred_element_type=F32).astype(BF)

    def to_m(k):
        arrived(hb.at[k, :, theirs_at], hr.at[k])

        @pl.when(core != k % 2)
        def _():
            arrived(hb.at[k, :, pool_at], qr.at[k])

        @pl.loop(0, 4)
        def _(q):
            cols = pl.ds(pl.multiple_of(q * 256, 256), 256)
            out = jnp.dot(hb[k], cp[:, cols], preferred_element_type=F32)
            o_ref[:, pl.ds(k * 8, 8), cols] = out.reshape(64, 8, 256).astype(BF)

    for k in range(3):
        regroup(k)
        to_planes(k)
    along_y(0)
    regroup(3)
    to_planes(3)

    arrived(bl.at[core], br)
    remote(bl.at[core], bl.at[core], bks, bkr, other).start()
    arrived(bl.at[1 - core], bkr)
    block = jnp.concatenate([bl[q % 2, q // 2].astype(F32) for q in range(16)], axis=0).astype(BF)
    pt[...] = lax.dot_general(hot[...].astype(BF), block, NT, preferred_element_type=F32).astype(BF)
    spread = lax.broadcasted_iota(jnp.int32, (512, 64), 0) // 8 == lax.broadcasted_iota(jnp.int32, (512, 64), 1)
    place = lax.broadcasted_iota(jnp.int32, (512, 128), 0) % 8
    for e in range(2):
        panel = jnp.dot(jnp.where(spread, 1.0, 0.0).astype(BF), pt[e * 64:(e + 1) * 64], preferred_element_type=F32)
        for n in range(8):
            kp[e, :, pl.ds(n * 128, 128)] = jnp.where(place == n, panel, 0.0).astype(BF)

    for k in range(STEPS):
        along_x(k)
        if k == 0:
            for e in range(2):
                half = cp.at[:, pl.ds(pl.multiple_of(e * 512 + core * 256, 256), 256)]
                remote(half, half, kcs.at[e], kcr.at[e], other).start()
        if k == 2:
            for e in range(2):
                arrived(cp.at[:, pl.ds(pl.multiple_of(e * 512 + (1 - core) * 256, 256), 256)], kcr.at[e])
        if k + 1 < STEPS:
            along_y(k + 1)
        if k >= 2:
            to_m(k - 2)
        if k >= 1:
            to_s(k - 1)
        pass_on(k)
        sides(k)
    to_m(STEPS - 2)
    to_s(STEPS - 1)
    to_m(STEPS - 1)

    @pl.loop(0, 15)
    def _(w):
        left_for(c_ref.at[:, lanes], zcs.at[w])

    left_for(dl.at[pl.ds(0, 2), core, pl.ds(0, 7)], ds)
    left_for(dl.at[2, core, pl.ds(0, 7)], des)
    left_for(dl.at[:, core], dks)
    left_for(bl.at[core, pl.ds(0, 7)], bs)
    left_for(bl.at[core], bks)
    for e in range(2):
        left_for(cl.at[x, y_lo, pl.ds(0, 8)], ycs.at[e])
        for half in range(2):
            left_for(cl.at[x, 0], xcs.at[e, half])
            left_for(cl.at[x, 0, pl.ds(0, 8)], fcs.at[e, half])
        left_for(cp.at[:, pl.ds(e * 256, 256)], kcs.at[e])
    for e in range(2):
        left_for(tq.at[pl.ds(0, 8), :, pl.ds(0, 3)], yhs.at[e])
        left_for(gx.at[0, :, :, 0], xhs.at[e])
        left_for(gx.at[0, 0, :, 0], fhs.at[e])
    for k in range(STEPS):
        for c in range(2):
            itself = jnp.logical_and(z // 8 == core, c == core)
            for count, few in ((7, itself), (8, jnp.logical_not(itself))):
                @pl.when(jnp.logical_and(few, whole(k, c)))
                def _():
                    left_for(s.at[c, k, pl.ds(0, count)], zs.at[k, c])

                @pl.when(jnp.logical_and(few, jnp.logical_not(whole(k, c))))
                def _():
                    left_for(s.at[c, k, pl.ds(0, count), pl.ds(0, 16)], zs.at[k, c])

        left_for(main(k, x, 0, 3), ys.at[k])
        for e in range(2):
            for half in range(2):
                left_for(main(k, x, 0, 2), xs.at[k, e, half])
            left_for(main(k, x, 0, 2), fs.at[k, e])
        left_for(ho.at[k], hs.at[k])

        @pl.when(core == k % 2)
        def _():
            left_for(hq.at[k], qs.at[k])


def shards(density, virt_coeff, block_coeff, ao_order):
    hbm = pl.BlockSpec(memory_space=pltpu.HBM)
    dma = pltpu.SemaphoreType.DMA
    one, two, four = dma, dma((2,)), dma((4,))
    return pl.pallas_call(
        exchange,
        out_shape=pltpu.VMEM((64, 32, 1024), BF),
        in_specs=[hbm] * 4,
        out_specs=pl.BlockSpec(memory_space=pltpu.VMEM),
        scratch_shapes=[
            pltpu.SMEM((1024,), jnp.int32),
            pltpu.VMEM((3, 2, 8, 40, 128), BF),
            pltpu.VMEM((4, 2, 16, 20, 128), BF),
            pltpu.VMEM((2, 8, 8, 1024), BF),
            pltpu.VMEM((128, 1024), F32),
            pltpu.VMEM((128, 128), BF),
            pltpu.VMEM((2, 512, 1024), BF),
            pltpu.VMEM((3, 640, 128), F32),
            pltpu.VMEM((640, 384), BF),
            pltpu.VMEM((32, 24, 128), F32),
            pltpu.VMEM((640, 1024), BF),
            pltpu.VMEM((4, 128, 384), BF),
            pltpu.VMEM((2, STEPS, 8, 32, 128), BF),
            pltpu.VMEM((STEPS, 16, 32, 128), BF),
            pltpu.VMEM((256, 128), F32),
            pltpu.VMEM((STEPS, 2, 8, 16, 128), BF),
            pltpu.VMEM((2, 8, 16, 128), BF),
            pltpu.VMEM((2, 2, 8, 2, 16, 128), BF),
            pltpu.VMEM((32, 256, 128), BF),
            pltpu.VMEM((32, 2, 4, 16, 128), BF),
            pltpu.VMEM((STEPS, 512, 640), BF),
            pltpu.VMEM((STEPS, 512, 256), BF),
            pltpu.VMEM((STEPS, 512, 128), BF),
            one,
            one, one, one, one, one, one,
            one, one, one, one,
            dma((16,)), one, two, one, dma((2, 2)), dma((2, 2)), dma((2, 2)), dma((2, 2)), two, two,
            dma((4, 2)), four, four, four, dma((4, 2, 2)), dma((4, 2, 2)), dma((4, 2)), dma((4, 2)), four, four,
            two, two, two, two, two, two, four, four,
        ],
        compiler_params=pltpu.CompilerParams(
            collective_id=0, has_side_effects=True, vmem_limit_bytes=56 * 1024 * 1024
        ),
    )(ao_order, density, virt_coeff, block_coeff)


def solution(mesh):
    return jax.shard_map(
        shards,
        mesh=mesh,
        in_specs=(P("virt", "ao", None), P("virt", None), P("ao", None), P()),
        out_specs=P("ao", "virt", None),
        check_vma=False,
    )
```

```python
import jax
import jax.numpy as jnp
from jax import lax
from jax.experimental import pallas as pl
from jax.experimental.pallas import tpu as pltpu
from jax.sharding import PartitionSpec as P

MESH = pl.DeviceIdType.MESH
BF = jnp.bfloat16
F32 = jnp.float32
TN = (((0,), (0,)), ((), ()))
NT = (((1,), (1,)), ((), ()))
STEPS = 4
BLOCKS = [(y % 2, (y // 2) * 8 + x * 2 + c) for c in range(2) for x in range(4) for y in range(4)]
BLOCKS += [(y % 2, 16 + (y // 2) * 2 + h) for h in range(2) for y in range(4)]


def exchange(
    order_hbm, d_ref, c_ref, b_ref, o_ref,
    order, dl, cl, bl, hot, pt, kp, df, dp, cf, cp, tt, s, r, rf, g, gh, gx, tm, tq, hb, ho, hq,
    order_sem, ds, dr, des, der, dks, dkr, bs, br, bks, bkr, zcs, zcr, ycs, ycr, xcs, xcr, fcs, fcr, kcs, kcr,
    zs, zr, ys, yr, xs, xr, fs, fr, hs, hr, yhs, yhr, xhs, xhr, fhs, fhr, qs, qr,
):
    v, j = lax.axis_index("virt"), lax.axis_index("ao")
    y_lo, z = v // 16, v % 16
    core, x, y_hi = j % 2, (j // 2) % 4, j // 8
    y = 2 * y_hi + y_lo
    share = j % 4
    right, left, far = (x + 1) % 4, (x + 3) % 4, (x + 2) % 4
    chip = j // 2

    def lanes_of(yh, e):
        return pl.ds(pl.multiple_of(yh * 512 + core * 256 + e * 128, 128), 128)

    lanes = lanes_of(x // 2, x % 2)

    def dev(yy, xx):
        return (yy % 2) * 16 + z, (yy // 2) * 8 + xx * 2 + core

    other = (v, j + 1 - 2 * core)
    to_right, to_left = dev(y, right), dev(y, left)

    def remote(src, dst, send, recv, device):
        return pltpu.make_async_remote_copy(
            src_ref=src, dst_ref=dst, send_sem=send, recv_sem=recv, device_id=device, device_id_type=MESH
        )

    def arrived(ref, sem):
        remote(ref, ref, sem, sem, other).wait_recv()

    def left_for(ref, sem):
        remote(ref, ref, sem, sem, other).wait_send()

    order_copy = pltpu.make_async_copy(order_hbm, order, order_sem)
    order_copy.start()

    barrier = pltpu.get_barrier_semaphore()

    def to_and_fro(w):
        return (w + 1) // 2 * (1 - 2 * (w % 2))

    @pl.loop(0, 15)
    def _(w):
        zv = y_lo * 16 + (z + 8 + to_and_fro(w)) % 16
        pl.semaphore_signal(barrier, inc=1, device_id=(zv, j), device_id_type=MESH)

        @pl.when(z // 8 != core)
        def _():
            pl.semaphore_signal(barrier, inc=1, device_id=(zv, j + 1 - 2 * core), device_id_type=MESH)

    for dy in (1, 3):
        pl.semaphore_signal(barrier, inc=1, device_id=dev((y + dy) % 4, x), device_id_type=MESH)

    pl.semaphore_signal(barrier, inc=1, device_id=other, device_id_type=MESH)

    @pl.loop(1, 8)
    def _(t):
        pl.semaphore_signal(barrier, inc=1, device_id=(v, (j + 2 * t) % 16), device_id_type=MESH)

    pl.semaphore_wait(barrier, 32 + (z // 8 + core) % 2)

    @pl.loop(0, 15)
    def _(w):
        zv = y_lo * 16 + (z + 8 + to_and_fro(w)) % 16
        remote(c_ref.at[:, lanes], cl.at[x, y_lo, z], zcs.at[w], zcr, (zv, j)).start()

    pltpu.make_async_copy(c_ref.at[:, lanes], cl.at[x, y_lo, z], zcr).start()

    @pl.loop(1, 8)
    def _(t):
        jj = (j + 2 * t) % 16
        remote(d_ref.at[pl.ds(jj // 2 * 2, 2)], dl.at[pl.ds(0, 2), core, chip], ds, dr, (v, jj)).start()
        remote(d_ref.at[16 + jj // 4], dl.at[2, core, chip], des, der, (v, jj)).start()

    pltpu.make_async_copy(d_ref.at[pl.ds(chip * 2, 2)], dl.at[pl.ds(0, 2), core, chip], dr).start()
    pltpu.make_async_copy(d_ref.at[16 + j // 4], dl.at[2, core, chip], der).start()

    order_copy.wait()
    column = lax.broadcasted_iota(jnp.int32, (1, 1024), 1)

    @pl.loop(0, 128)
    def _(k):
        hot[pl.ds(k, 1), :] = jnp.where(column == order[chip * 128 + k], 1.0, 0.0).astype(F32)

    def coeff_x(part, yl):
        blk = cl.at[x, yl]
        remote(blk, blk, xcs.at[0, part], xcr.at[0, part], to_right).start()
        remote(blk, blk, xcs.at[1, part], xcr.at[1, part], to_left).start()

    def coeff_on(part, yl):
        for way, (frm, device) in enumerate(((left, to_right), (right, to_left))):
            arrived(cl.at[frm, yl], xcr.at[way, part])
            blk = cl.at[frm, yl, pl.ds(way * 8, 8)]
            remote(blk, blk, fcs.at[way, part], fcr.at[way, part], device).start()

    arrived(cl.at[x, y_lo], zcr)
    for e, dy in enumerate((3, 1)):
        blk = cl.at[x, y_lo, pl.ds(e * 8, 8)]
        remote(blk, blk, ycs.at[e], ycr, dev((y + dy) % 4, x)).start()
    coeff_x(0, y_lo)

    arrived(dl.at[pl.ds(0, 2), core], dr)
    arrived(dl.at[2, core], der)
    remote(dl.at[:, core], dl.at[:, core], dks, dkr, other).start()

    arrived(cl.at[x, 1 - y_lo], ycr)
    coeff_x(1, 1 - y_lo)
    coeff_on(0, y_lo)

    arrived(dl.at[:, 1 - core], dkr)
    for u in range(3):
        for jj in range(16):
            df[u, pl.ds(jj * 40, 40), :] = dl[u, jj % 2, jj // 2].astype(F32)
        for q, (yl, i) in enumerate(BLOCKS):
            dp[pl.ds(q * 16, 16), pl.ds(u * 128, 128)] = df[u, pl.ds(yl * 320 + i, 16, stride=20), :].astype(BF)

    coeff_on(1, 1 - y_lo)

    @pl.loop(1, 8)
    def _(t):
        remote(b_ref, bl.at[core, chip], bs, br, (v, (j + 2 * t) % 16)).start()

    pltpu.make_async_copy(b_ref, bl.at[core, chip], br).start()

    def both_ways(blocks, send, recv):
        for half in range(2):
            for way, device in enumerate((to_right, to_left)):
                blk = blocks(half ^ way)
                remote(blk, blk, send.at[way, half], recv.at[way, half], device).start()

    def relay(xx):
        for yl in range(2):
            for zz in range(16):
                cf[yl * 16 + zz, pl.ds(0, 20), :] = cl[xx, yl, zz].astype(F32)
        flat = cf.reshape(32 * 24, 128)
        to = lanes_of(xx // 2, xx % 2)
        for q, (yl, i) in enumerate(BLOCKS):
            cp[pl.ds(q * 16, 16), to] = flat[pl.ds(yl * 384 + i, 16, stride=24), :].astype(BF)
        tt[xx] = lax.dot_general(cp[:, to], dp[...], TN, preferred_element_type=F32).astype(BF)

    relay(x)
    relay(left)
    relay(right)
    for way in range(2):
        arrived(cl.at[far, y_lo, pl.ds(way * 8, 8)], fcr.at[way, 0])
        arrived(cl.at[far, 1 - y_lo, pl.ds(way * 8, 8)], fcr.at[way, 1])
    relay(far)

    def regroup(k):
        for yh in range(2):
            for e in range(2):
                for q in range(4):
                    rows = tt[2 * yh + e, q * 32 + k * 8:q * 32 + k * 8 + 8, :]
                    s[0, k, e * 4 + q, pl.ds(yh * 8, 8), :] = rows[:, :128]
                    s[1, k, e * 4 + q, pl.ds(yh * 8, 8), :] = rows[:, 128:256]
                    s[k % 2, k, e * 4 + q, pl.ds(16 + yh * 8, 8), :] = rows[:, 256:]

    def whole(k, c):
        return jnp.logical_and(c == k % 2, x % 2 == k // 2)

    start = 8 + 4 * (1 - (z // 8 + core) % 2)

    def to_planes(k):
        for c in range(2):
            def along_z(part):
                @pl.loop(0, 8)
                def _(w):
                    zl = (z + start + to_and_fro(w)) % 8
                    zz = core * 8 + zl
                    itself = jnp.logical_and(zz == z, c == core)

                    @pl.when(itself)
                    def _():
                        pltpu.make_async_copy(s.at[c, k, zl, part], r.at[k, z, part], zr.at[k]).start()

                    @pl.when(jnp.logical_not(itself))
                    def _():
                        remote(s.at[c, k, zl, part], r.at[k, z, part], zs.at[k, c], zr.at[k],
                               (y_lo * 16 + zz, chip * 2 + c)).start()

            @pl.when(whole(k, c))
            def _():
                along_z(pl.ds(0, 32))

            @pl.when(jnp.logical_not(whole(k, c)))
            def _():
                along_z(pl.ds(0, 16))

    def at(block, count=1):
        return pl.ds(pl.multiple_of(block * 16, 16), count * 16)

    def piece(k):
        return pl.ds(k * 8, 8)

    def turn(k, first, dst):
        for zz in range(16):
            rf[pl.ds(zz * 16, 16), :] = r[k, zz, pl.ds(first, 16), :].astype(F32)
        for i in range(16):
            dst[i // 8, i % 8] = rf[pl.ds(i, 16, stride=16), :].astype(BF)

    def main(k, xx, first=0, count=4):
        return tm.at[piece(k), at(xx * 4 + first, count), :]

    def pooled(k, xx):
        return gx.at[k // 2, :, :, xx // 2]

    def along_y(k):
        @pl.when(share != k)
        def _():
            arrived(r.at[k, :, pl.ds(0, 16)], zr.at[k])

        @pl.when(share == k)
        def _():
            arrived(r.at[k], zr.at[k])

        turn(k, 0, g.at[k])
        for dy in (1, 3, 2):
            half = y_lo if dy == 2 else 1 - y_lo
            remote(g.at[k, half], main(k, x, y, 1), ys.at[k], yr.at[k], dev((y + dy) % 4, x)).start()
        tm[piece(k), at(x * 4 + y), :] = g[k, y_lo]

        @pl.when(share == k)
        def _():
            turn(k, 16, gh)
            gx[k // 2, :, :, x // 2] = gh[...]
            for way, device in enumerate((to_right, to_left)):
                remote(pooled(k, x), pooled(k, x), xhs.at[way], xhr.at[way], device).start()

    def along_x(k):
        arrived(main(k, x, 0, 3), yr.at[k])
        both_ways(lambda part: main(k, x, 2 * part, 2), xs.at[k], xr.at[k])

        @pl.when(jnp.logical_and(core == k % 2, x % 2 != k // 2))
        def _():
            for way, (frm, device) in enumerate(((left, to_right), (right, to_left))):
                arrived(pooled(k, frm), xhr.at[way])
                blk = gx.at[k // 2, way, :, frm // 2]
                remote(blk, blk, fhs.at[way], fhr.at[way], device).start()

    def pass_on(k):
        for way, (frm, device) in enumerate(((left, to_right), (right, to_left))):
            blk = main(k, frm, 2 * way, 2)
            arrived(blk, xr.at[k, way, 0])
            remote(blk, blk, fs.at[k, way], fr.at[k, way], device).start()

        @pl.when(core == k % 2)
        def _():
            @pl.when(share == k)
            def _():
                for way in range(2):
                    arrived(gx.at[k // 2, way, :, far // 2], fhr.at[way])

            for dy in (1, 3, 2):
                half = y_lo if dy == 2 else 1 - y_lo
                remote(gx.at[k // 2, half], tq.at[piece(k), :, y], yhs.at[k // 2], yhr.at[k // 2], dev((y + dy) % 4, x)).start()
            tq[piece(k), :, y] = gx[k // 2, y_lo]

    def sides(k):
        for way, frm in enumerate((left, right)):
            arrived(main(k, frm, 2 - 2 * way, 2), xr.at[k, way, 1])

    mine_at = pl.ds(pl.multiple_of(core * 256, 256), 256)
    theirs_at = pl.ds(pl.multiple_of((1 - core) * 256, 256), 256)
    pool_at = pl.ds(512, 128)

    def to_s(k):
        arrived(main(k, far, 0, 2), fr.at[k, 0])
        arrived(main(k, far, 2, 2), fr.at[k, 1])
        terms = jnp.concatenate([tm[k * 8 + n] for n in range(8)], axis=1)
        ho[k] = lax.dot_general(kp[1 - core], terms, NT, preferred_element_type=F32).astype(BF)
        remote(ho.at[k], hb.at[k, :, mine_at], hs.at[k], hr.at[k], other).start()

        @pl.when(core == k % 2)
        def _():
            arrived(tq.at[piece(k), :, pl.ds(0, 3)], yhr.at[k // 2])
            terms = jnp.concatenate([tq[k * 8 + n].reshape(128, 128) for n in range(8)], axis=1)
            hq[k] = lax.dot_general(kp[1 - core], terms, NT, preferred_element_type=F32).astype(BF)
            remote(hq.at[k], hb.at[k, :, pool_at], qs.at[k], qr.at[k], other).start()
            hb[k, :, pool_at] = lax.dot_general(kp[core], terms, NT, preferred_element_type=F32).astype(BF)

        terms = jnp.concatenate([tm[k * 8 + n] for n in range(8)], axis=1)
        hb[k, :, mine_at] = lax.dot_general(kp[core], terms, NT, preferred_element_type=F32).astype(BF)

    def to_m(k):
        arrived(hb.at[k, :, theirs_at], hr.at[k])

        @pl.when(core != k % 2)
        def _():
            arrived(hb.at[k, :, pool_at], qr.at[k])

        @pl.loop(0, 4)
        def _(q):
            cols = pl.ds(pl.multiple_of(q * 256, 256), 256)
            out = jnp.dot(hb[k], cp[:, cols], preferred_element_type=F32)
            o_ref[:, pl.ds(k * 8, 8), cols] = out.reshape(64, 8, 256).astype(BF)

    arrived(bl.at[core], br)
    remote(bl.at[core], bl.at[core], bks, bkr, other).start()
    for k in range(3):
        regroup(k)
        to_planes(k)

    arrived(bl.at[1 - core], bkr)
    block = jnp.concatenate([bl[q % 2, q // 2].astype(F32) for q in range(16)], axis=0).astype(BF)
    pt[...] = lax.dot_general(hot[...].astype(BF), block, NT, preferred_element_type=F32).astype(BF)
    spread = lax.broadcasted_iota(jnp.int32, (512, 64), 0) // 8 == lax.broadcasted_iota(jnp.int32, (512, 64), 1)
    place = lax.broadcasted_iota(jnp.int32, (512, 128), 0) % 8
    for e in range(2):
        panel = jnp.dot(jnp.where(spread, 1.0, 0.0).astype(BF), pt[e * 64:(e + 1) * 64], preferred_element_type=F32)
        for n in range(8):
            kp[e, :, pl.ds(n * 128, 128)] = jnp.where(place == n, panel, 0.0).astype(BF)

    along_y(0)
    regroup(3)
    to_planes(3)
    along_x(0)

    def coeff_half(e, c):
        return cp.at[:, pl.ds(pl.multiple_of(e * 512 + c * 256, 256), 256)]

    for e in range(2):
        remote(coeff_half(e, core), coeff_half(e, core), kcs.at[e], kcr.at[e], other).start()

    along_y(1)
    along_x(1)
    pass_on(0)
    along_y(2)
    sides(0)
    along_x(2)
    pass_on(1)
    along_y(3)
    sides(1)
    to_s(0)
    along_x(3)
    pass_on(2)
    sides(2)
    for e in range(2):
        arrived(coeff_half(e, 1 - core), kcr.at[e])
    to_m(0)
    to_s(1)
    pass_on(3)
    sides(3)
    to_m(1)
    to_s(2)
    to_s(3)
    to_m(2)
    to_m(3)

    @pl.loop(0, 15)
    def _(w):
        left_for(c_ref.at[:, lanes], zcs.at[w])

    left_for(dl.at[pl.ds(0, 2), core, pl.ds(0, 7)], ds)
    left_for(dl.at[2, core, pl.ds(0, 7)], des)
    left_for(dl.at[:, core], dks)
    left_for(bl.at[core, pl.ds(0, 7)], bs)
    left_for(bl.at[core], bks)
    for e in range(2):
        left_for(cl.at[x, y_lo, pl.ds(0, 8)], ycs.at[e])
        for half in range(2):
            left_for(cl.at[x, 0], xcs.at[e, half])
            left_for(cl.at[x, 0, pl.ds(0, 8)], fcs.at[e, half])
        left_for(cp.at[:, pl.ds(e * 256, 256)], kcs.at[e])
    for e in range(2):
        left_for(tq.at[pl.ds(0, 8), :, pl.ds(0, 3)], yhs.at[e])
        left_for(gx.at[0, :, :, 0], xhs.at[e])
        left_for(gx.at[0, 0, :, 0], fhs.at[e])
    for k in range(STEPS):
        for c in range(2):
            itself = jnp.logical_and(z // 8 == core, c == core)
            for count, few in ((7, itself), (8, jnp.logical_not(itself))):
                @pl.when(jnp.logical_and(few, whole(k, c)))
                def _():
                    left_for(s.at[c, k, pl.ds(0, count)], zs.at[k, c])

                @pl.when(jnp.logical_and(few, jnp.logical_not(whole(k, c))))
                def _():
                    left_for(s.at[c, k, pl.ds(0, count), pl.ds(0, 16)], zs.at[k, c])

        left_for(main(k, x, 0, 3), ys.at[k])
        for e in range(2):
            for half in range(2):
                left_for(main(k, x, 0, 2), xs.at[k, e, half])
            left_for(main(k, x, 0, 2), fs.at[k, e])
        left_for(ho.at[k], hs.at[k])

        @pl.when(core == k % 2)
        def _():
            left_for(hq.at[k], qs.at[k])


def shards(density, virt_coeff, block_coeff, ao_order):
    hbm = pl.BlockSpec(memory_space=pltpu.HBM)
    dma = pltpu.SemaphoreType.DMA
    one, two, four = dma, dma((2,)), dma((4,))
    return pl.pallas_call(
        exchange,
        out_shape=pltpu.VMEM((64, 32, 1024), BF),
        in_specs=[hbm] * 4,
        out_specs=pl.BlockSpec(memory_space=pltpu.VMEM),
        scratch_shapes=[
            pltpu.SMEM((1024,), jnp.int32),
            pltpu.VMEM((3, 2, 8, 40, 128), BF),
            pltpu.VMEM((4, 2, 16, 20, 128), BF),
            pltpu.VMEM((2, 8, 8, 1024), BF),
            pltpu.VMEM((128, 1024), F32),
            pltpu.VMEM((128, 128), BF),
            pltpu.VMEM((2, 512, 1024), BF),
            pltpu.VMEM((3, 640, 128), F32),
            pltpu.VMEM((640, 384), BF),
            pltpu.VMEM((32, 24, 128), F32),
            pltpu.VMEM((640, 1024), BF),
            pltpu.VMEM((4, 128, 384), BF),
            pltpu.VMEM((2, STEPS, 8, 32, 128), BF),
            pltpu.VMEM((STEPS, 16, 32, 128), BF),
            pltpu.VMEM((256, 128), F32),
            pltpu.VMEM((STEPS, 2, 8, 16, 128), BF),
            pltpu.VMEM((2, 8, 16, 128), BF),
            pltpu.VMEM((2, 2, 8, 2, 16, 128), BF),
            pltpu.VMEM((32, 256, 128), BF),
            pltpu.VMEM((32, 2, 4, 16, 128), BF),
            pltpu.VMEM((STEPS, 512, 640), BF),
            pltpu.VMEM((STEPS, 512, 256), BF),
            pltpu.VMEM((STEPS, 512, 128), BF),
            one,
            one, one, one, one, one, one,
            one, one, one, one,
            dma((16,)), one, two, one, dma((2, 2)), dma((2, 2)), dma((2, 2)), dma((2, 2)), two, two,
            dma((4, 2)), four, four, four, dma((4, 2, 2)), dma((4, 2, 2)), dma((4, 2)), dma((4, 2)), four, four,
            two, two, two, two, two, two, four, four,
        ],
        compiler_params=pltpu.CompilerParams(
            collective_id=0, has_side_effects=True, vmem_limit_bytes=56 * 1024 * 1024
        ),
    )(ao_order, density, virt_coeff, block_coeff)


def solution(mesh):
    return jax.shard_map(
        shards,
        mesh=mesh,
        in_specs=(P("virt", "ao", None), P("virt", None), P("ao", None), P()),
        out_specs=P("ao", "virt", None),
        check_vma=False,
    )
```

```python
import jax
import jax.numpy as jnp
from jax import lax
from jax.experimental import pallas as pl
from jax.experimental.pallas import tpu as pltpu
from jax.sharding import PartitionSpec as P

MESH = pl.DeviceIdType.MESH
BF = jnp.bfloat16
F32 = jnp.float32
TN = (((0,), (0,)), ((), ()))
NT = (((1,), (1,)), ((), ()))
STEPS = 4
BLOCKS = [(y % 2, (y // 2) * 8 + x * 2 + c) for c in range(2) for x in range(4) for y in range(4)]
BLOCKS += [(y % 2, 16 + (y // 2) * 2 + h) for h in range(2) for y in range(4)]


def exchange(
    order_hbm, d_ref, c_ref, b_ref, o_ref,
    order, dl, cl, bl, hot, pt, kp, df, dp, cf, cp, tt, s, r, rf, g, gh, gx, tm, tq, hb, ho, hq,
    order_sem, ds, dr, des, der, dks, dkr, bs, br, bks, bkr, zcs, zcr, ycs, ycr, xcs, xcr, fcs, fcr, kcs, kcr,
    zs, zr, ys, yr, xs, xr, fs, fr, hs, hr, yhs, yhr, xhs, xhr, fhs, fhr, qs, qr,
):
    v, j = lax.axis_index("virt"), lax.axis_index("ao")
    y_lo, z = v // 16, v % 16
    core, x, y_hi = j % 2, (j // 2) % 4, j // 8
    y = 2 * y_hi + y_lo
    share = j % 4
    right, left, far = (x + 1) % 4, (x + 3) % 4, (x + 2) % 4
    chip = j // 2

    def lanes_of(yh, e):
        return pl.ds(pl.multiple_of(yh * 512 + core * 256 + e * 128, 128), 128)

    lanes = lanes_of(x % 2, x // 2)

    def dev(yy, xx):
        return (yy % 2) * 16 + z, (yy // 2) * 8 + xx * 2 + core

    other = (v, j + 1 - 2 * core)
    to_right, to_left = dev(y, right), dev(y, left)

    def remote(src, dst, send, recv, device):
        return pltpu.make_async_remote_copy(
            src_ref=src, dst_ref=dst, send_sem=send, recv_sem=recv, device_id=device, device_id_type=MESH
        )

    def arrived(ref, sem):
        remote(ref, ref, sem, sem, other).wait_recv()

    def left_for(ref, sem):
        remote(ref, ref, sem, sem, other).wait_send()

    order_copy = pltpu.make_async_copy(order_hbm, order, order_sem)
    order_copy.start()

    barrier = pltpu.get_barrier_semaphore()

    def to_and_fro(w):
        return (w + 1) // 2 * (1 - 2 * (w % 2))

    @pl.loop(0, 15)
    def _(w):
        zv = y_lo * 16 + (z + 8 + to_and_fro(w)) % 16
        pl.semaphore_signal(barrier, inc=1, device_id=(zv, j), device_id_type=MESH)

        @pl.when(z // 8 != core)
        def _():
            pl.semaphore_signal(barrier, inc=1, device_id=(zv, j + 1 - 2 * core), device_id_type=MESH)

    for dy in (1, 3):
        pl.semaphore_signal(barrier, inc=1, device_id=dev((y + dy) % 4, x), device_id_type=MESH)

    pl.semaphore_signal(barrier, inc=1, device_id=other, device_id_type=MESH)

    @pl.loop(1, 8)
    def _(t):
        pl.semaphore_signal(barrier, inc=1, device_id=(v, (j + 2 * t) % 16), device_id_type=MESH)

    pl.semaphore_wait(barrier, 32 + (z // 8 + core) % 2)

    @pl.loop(0, 15)
    def _(w):
        zv = y_lo * 16 + (z + 8 + to_and_fro(w)) % 16
        remote(c_ref.at[:, lanes], cl.at[x, y_lo, z], zcs.at[w], zcr, (zv, j)).start()

    pltpu.make_async_copy(c_ref.at[:, lanes], cl.at[x, y_lo, z], zcr).start()

    @pl.loop(1, 8)
    def _(t):
        jj = (j + 2 * t) % 16
        remote(d_ref.at[pl.ds(jj // 2 * 2, 2)], dl.at[pl.ds(0, 2), core, chip], ds, dr, (v, jj)).start()
        remote(d_ref.at[16 + jj // 4], dl.at[2, core, chip], des, der, (v, jj)).start()

    pltpu.make_async_copy(d_ref.at[pl.ds(chip * 2, 2)], dl.at[pl.ds(0, 2), core, chip], dr).start()
    pltpu.make_async_copy(d_ref.at[16 + j // 4], dl.at[2, core, chip], der).start()

    order_copy.wait()
    column = lax.broadcasted_iota(jnp.int32, (1, 1024), 1)

    @pl.loop(0, 128)
    def _(k):
        hot[pl.ds(k, 1), :] = jnp.where(column == order[chip * 128 + k], 1.0, 0.0).astype(F32)

    def coeff_x(part, yl):
        blk = cl.at[x, yl]
        remote(blk, blk, xcs.at[0, part], xcr.at[0, part], to_right).start()
        remote(blk, blk, xcs.at[1, part], xcr.at[1, part], to_left).start()

    def coeff_on(part, yl):
        for way, (frm, device) in enumerate(((left, to_right), (right, to_left))):
            arrived(cl.at[frm, yl], xcr.at[way, part])
            blk = cl.at[frm, yl, pl.ds(way * 8, 8)]
            remote(blk, blk, fcs.at[way, part], fcr.at[way, part], device).start()

    arrived(cl.at[x, y_lo], zcr)
    for e, dy in enumerate((3, 1)):
        blk = cl.at[x, y_lo, pl.ds(e * 8, 8)]
        remote(blk, blk, ycs.at[e], ycr, dev((y + dy) % 4, x)).start()
    coeff_x(0, y_lo)

    arrived(dl.at[pl.ds(0, 2), core], dr)
    arrived(dl.at[2, core], der)
    remote(dl.at[:, core], dl.at[:, core], dks, dkr, other).start()

    arrived(cl.at[x, 1 - y_lo], ycr)
    coeff_x(1, 1 - y_lo)
    coeff_on(0, y_lo)

    arrived(dl.at[:, 1 - core], dkr)
    for u in range(3):
        for jj in range(16):
            df[u, pl.ds(jj * 40, 40), :] = dl[u, jj % 2, jj // 2].astype(F32)
        for q, (yl, i) in enumerate(BLOCKS):
            dp[pl.ds(q * 16, 16), pl.ds(u * 128, 128)] = df[u, pl.ds(yl * 320 + i, 16, stride=20), :].astype(BF)

    def both_ways(blocks, send, recv):
        for half in range(2):
            for way, device in enumerate((to_right, to_left)):
                blk = blocks(half ^ way)
                remote(blk, blk, send.at[way, half], recv.at[way, half], device).start()

    def relay(xx):
        for yl in range(2):
            for zz in range(16):
                cf[yl * 16 + zz, pl.ds(0, 20), :] = cl[xx, yl, zz].astype(F32)
        flat = cf.reshape(32 * 24, 128)
        to = lanes_of(xx % 2, xx // 2)
        for q, (yl, i) in enumerate(BLOCKS):
            cp[pl.ds(q * 16, 16), to] = flat[pl.ds(yl * 384 + i, 16, stride=24), :].astype(BF)
        tt[xx] = lax.dot_general(cp[:, to], dp[...], TN, preferred_element_type=F32).astype(BF)

    relay(x)
    coeff_on(1, 1 - y_lo)

    @pl.loop(1, 8)
    def _(t):
        remote(b_ref, bl.at[core, chip], bs, br, (v, (j + 2 * t) % 16)).start()

    pltpu.make_async_copy(b_ref, bl.at[core, chip], br).start()

    relay(left)
    relay(right)

    def regroup(k, e):
        for yh in range(2):
            for q in range(4):
                rows = tt[2 * e + yh, q * 32 + k * 8:q * 32 + k * 8 + 8, :]
                s[0, k, e * 4 + q, pl.ds(yh * 8, 8), :] = rows[:, :128]
                s[1, k, e * 4 + q, pl.ds(yh * 8, 8), :] = rows[:, 128:256]
                s[k % 2, k, e * 4 + q, pl.ds(16 + yh * 8, 8), :] = rows[:, 256:]

    def whole(k, c):
        return jnp.logical_and(c == k % 2, x % 2 == k // 2)

    def to_planes(k, e):
        for c in range(2):
            def along_z(part):
                @pl.loop(0, 4)
                def _(w):
                    zl = e * 4 + (z + w) % 4
                    zz = core * 8 + zl
                    itself = jnp.logical_and(zz == z, c == core)

                    @pl.when(itself)
                    def _():
                        pltpu.make_async_copy(s.at[c, k, zl, part], r.at[k, z, part], zr.at[k]).start()

                    @pl.when(jnp.logical_not(itself))
                    def _():
                        remote(s.at[c, k, zl, part], r.at[k, z, part], zs.at[k, c], zr.at[k],
                               (y_lo * 16 + zz, chip * 2 + c)).start()

            @pl.when(whole(k, c))
            def _():
                along_z(pl.ds(0, 32))

            @pl.when(jnp.logical_not(whole(k, c)))
            def _():
                along_z(pl.ds(0, 16))

    def at(block, count=1):
        return pl.ds(pl.multiple_of(block * 16, 16), count * 16)

    def piece(k):
        return pl.ds(k * 8, 8)

    def turn(k, first, dst):
        for zz in range(16):
            rf[pl.ds(zz * 16, 16), :] = r[k, zz, pl.ds(first, 16), :].astype(F32)
        for i in range(16):
            dst[i // 8, i % 8] = rf[pl.ds(i, 16, stride=16), :].astype(BF)

    def main(k, xx, first=0, count=4):
        return tm.at[piece(k), at(xx * 4 + first, count), :]

    def pooled(k, xx):
        return gx.at[k // 2, :, :, xx // 2]

    def along_y(k):
        @pl.when(share != k)
        def _():
            arrived(r.at[k, :, pl.ds(0, 16)], zr.at[k])

        @pl.when(share == k)
        def _():
            arrived(r.at[k], zr.at[k])

        turn(k, 0, g.at[k])
        for dy in (1, 3, 2):
            half = y_lo if dy == 2 else 1 - y_lo
            remote(g.at[k, half], main(k, x, y, 1), ys.at[k], yr.at[k], dev((y + dy) % 4, x)).start()
        tm[piece(k), at(x * 4 + y), :] = g[k, y_lo]

        @pl.when(share == k)
        def _():
            turn(k, 16, gh)
            gx[k // 2, :, :, x // 2] = gh[...]
            for way, device in enumerate((to_right, to_left)):
                remote(pooled(k, x), pooled(k, x), xhs.at[way], xhr.at[way], device).start()

    def along_x(k):
        arrived(main(k, x, 0, 3), yr.at[k])
        both_ways(lambda part: main(k, x, 2 * part, 2), xs.at[k], xr.at[k])

        @pl.when(jnp.logical_and(core == k % 2, x % 2 != k // 2))
        def _():
            for way, (frm, device) in enumerate(((left, to_right), (right, to_left))):
                arrived(pooled(k, frm), xhr.at[way])
                blk = gx.at[k // 2, way, :, frm // 2]
                remote(blk, blk, fhs.at[way], fhr.at[way], device).start()

    def pass_on(k):
        for way, (frm, device) in enumerate(((left, to_right), (right, to_left))):
            blk = main(k, frm, 2 * way, 2)
            arrived(blk, xr.at[k, way, 0])
            remote(blk, blk, fs.at[k, way], fr.at[k, way], device).start()

        @pl.when(core == k % 2)
        def _():
            @pl.when(share == k)
            def _():
                for way in range(2):
                    arrived(gx.at[k // 2, way, :, far // 2], fhr.at[way])

            for dy in (1, 3, 2):
                half = y_lo if dy == 2 else 1 - y_lo
                remote(gx.at[k // 2, half], tq.at[piece(k), :, y], yhs.at[k // 2], yhr.at[k // 2], dev((y + dy) % 4, x)).start()
            tq[piece(k), :, y] = gx[k // 2, y_lo]

    def sides(k):
        for way, frm in enumerate((left, right)):
            arrived(main(k, frm, 2 - 2 * way, 2), xr.at[k, way, 1])

    mine_at = pl.ds(pl.multiple_of(core * 256, 256), 256)
    theirs_at = pl.ds(pl.multiple_of((1 - core) * 256, 256), 256)
    pool_at = pl.ds(512, 128)

    def to_s(k):
        arrived(main(k, far, 0, 2), fr.at[k, 0])
        arrived(main(k, far, 2, 2), fr.at[k, 1])
        terms = jnp.concatenate([tm[k * 8 + n] for n in range(8)], axis=1)
        ho[k] = lax.dot_general(kp[1 - core], terms, NT, preferred_element_type=F32).astype(BF)
        remote(ho.at[k], hb.at[k, :, mine_at], hs.at[k], hr.at[k], other).start()

        @pl.when(core == k % 2)
        def _():
            arrived(tq.at[piece(k), :, pl.ds(0, 3)], yhr.at[k // 2])
            terms = jnp.concatenate([tq[k * 8 + n].reshape(128, 128) for n in range(8)], axis=1)
            hq[k] = lax.dot_general(kp[1 - core], terms, NT, preferred_element_type=F32).astype(BF)
            remote(hq.at[k], hb.at[k, :, pool_at], qs.at[k], qr.at[k], other).start()
            hb[k, :, pool_at] = lax.dot_general(kp[core], terms, NT, preferred_element_type=F32).astype(BF)

        terms = jnp.concatenate([tm[k * 8 + n] for n in range(8)], axis=1)
        hb[k, :, mine_at] = lax.dot_general(kp[core], terms, NT, preferred_element_type=F32).astype(BF)

    def to_m(k):
        arrived(hb.at[k, :, theirs_at], hr.at[k])

        @pl.when(core != k % 2)
        def _():
            arrived(hb.at[k, :, pool_at], qr.at[k])

        @pl.loop(0, 4)
        def _(q):
            cols = pl.ds(pl.multiple_of(q * 256, 256), 256)
            out = jnp.dot(hb[k], cp[:, cols], preferred_element_type=F32)
            o_ref[:, pl.ds(k * 8, 8), cols] = out.reshape(64, 8, 256).astype(BF)

    near = x // 2
    regroup(0, near)
    to_planes(0, near)
    for way in range(2):
        arrived(cl.at[far, y_lo, pl.ds(way * 8, 8)], fcr.at[way, 0])
        arrived(cl.at[far, 1 - y_lo, pl.ds(way * 8, 8)], fcr.at[way, 1])
    relay(far)

    regroup(0, 1 - near)
    to_planes(0, 1 - near)
    arrived(bl.at[core], br)
    remote(bl.at[core], bl.at[core], bks, bkr, other).start()
    for k in (1, 2):
        for e in range(2):
            regroup(k, e)
            to_planes(k, e)

    arrived(bl.at[1 - core], bkr)
    block = jnp.concatenate([bl[q % 2, q // 2].astype(F32) for q in range(16)], axis=0).astype(BF)
    pt[...] = lax.dot_general(hot[...].astype(BF), block, NT, preferred_element_type=F32).astype(BF)
    spread = lax.broadcasted_iota(jnp.int32, (512, 64), 0) // 8 == lax.broadcasted_iota(jnp.int32, (512, 64), 1)
    place = lax.broadcasted_iota(jnp.int32, (512, 128), 0) % 8
    for e in range(2):
        panel = jnp.dot(jnp.where(spread, 1.0, 0.0).astype(BF), pt[e * 64:(e + 1) * 64], preferred_element_type=F32)
        for n in range(8):
            kp[e, :, pl.ds(n * 128, 128)] = jnp.where(place == n, panel, 0.0).astype(BF)

    along_y(0)
    for e in range(2):
        regroup(3, e)
        to_planes(3, e)
    along_x(0)

    def coeff_half(e, c):
        return cp.at[:, pl.ds(pl.multiple_of(e * 512 + c * 256, 256), 256)]

    for e in range(2):
        remote(coeff_half(e, core), coeff_half(e, core), kcs.at[e], kcr.at[e], other).start()

    along_y(1)
    along_x(1)
    pass_on(0)
    along_y(2)
    sides(0)
    along_x(2)
    pass_on(1)
    along_y(3)
    sides(1)
    to_s(0)
    along_x(3)
    pass_on(2)
    sides(2)
    for e in range(2):
        arrived(coeff_half(e, 1 - core), kcr.at[e])
    to_m(0)
    to_s(1)
    pass_on(3)
    sides(3)
    to_m(1)
    to_s(2)
    to_s(3)
    to_m(2)
    to_m(3)

    @pl.loop(0, 15)
    def _(w):
        left_for(c_ref.at[:, lanes], zcs.at[w])

    left_for(dl.at[pl.ds(0, 2), core, pl.ds(0, 7)], ds)
    left_for(dl.at[2, core, pl.ds(0, 7)], des)
    left_for(dl.at[:, core], dks)
    left_for(bl.at[core, pl.ds(0, 7)], bs)
    left_for(bl.at[core], bks)
    for e in range(2):
        left_for(cl.at[x, y_lo, pl.ds(0, 8)], ycs.at[e])
        for half in range(2):
            left_for(cl.at[x, 0], xcs.at[e, half])
            left_for(cl.at[x, 0, pl.ds(0, 8)], fcs.at[e, half])
        left_for(cp.at[:, pl.ds(e * 256, 256)], kcs.at[e])
    for e in range(2):
        left_for(tq.at[pl.ds(0, 8), :, pl.ds(0, 3)], yhs.at[e])
        left_for(gx.at[0, :, :, 0], xhs.at[e])
        left_for(gx.at[0, 0, :, 0], fhs.at[e])
    for k in range(STEPS):
        for c in range(2):
            itself = jnp.logical_and(z // 8 == core, c == core)
            for count, few in ((7, itself), (8, jnp.logical_not(itself))):
                @pl.when(jnp.logical_and(few, whole(k, c)))
                def _():
                    left_for(s.at[c, k, pl.ds(0, count)], zs.at[k, c])

                @pl.when(jnp.logical_and(few, jnp.logical_not(whole(k, c))))
                def _():
                    left_for(s.at[c, k, pl.ds(0, count), pl.ds(0, 16)], zs.at[k, c])

        left_for(main(k, x, 0, 3), ys.at[k])
        for e in range(2):
            for half in range(2):
                left_for(main(k, x, 0, 2), xs.at[k, e, half])
            left_for(main(k, x, 0, 2), fs.at[k, e])
        left_for(ho.at[k], hs.at[k])

        @pl.when(core == k % 2)
        def _():
            left_for(hq.at[k], qs.at[k])


def shards(density, virt_coeff, block_coeff, ao_order):
    hbm = pl.BlockSpec(memory_space=pltpu.HBM)
    dma = pltpu.SemaphoreType.DMA
    one, two, four = dma, dma((2,)), dma((4,))
    return pl.pallas_call(
        exchange,
        out_shape=pltpu.VMEM((64, 32, 1024), BF),
        in_specs=[hbm] * 4,
        out_specs=pl.BlockSpec(memory_space=pltpu.VMEM),
        scratch_shapes=[
            pltpu.SMEM((1024,), jnp.int32),
            pltpu.VMEM((3, 2, 8, 40, 128), BF),
            pltpu.VMEM((4, 2, 16, 20, 128), BF),
            pltpu.VMEM((2, 8, 8, 1024), BF),
            pltpu.VMEM((128, 1024), F32),
            pltpu.VMEM((128, 128), BF),
            pltpu.VMEM((2, 512, 1024), BF),
            pltpu.VMEM((3, 640, 128), F32),
            pltpu.VMEM((640, 384), BF),
            pltpu.VMEM((32, 24, 128), F32),
            pltpu.VMEM((640, 1024), BF),
            pltpu.VMEM((4, 128, 384), BF),
            pltpu.VMEM((2, STEPS, 8, 32, 128), BF),
            pltpu.VMEM((STEPS, 16, 32, 128), BF),
            pltpu.VMEM((256, 128), F32),
            pltpu.VMEM((STEPS, 2, 8, 16, 128), BF),
            pltpu.VMEM((2, 8, 16, 128), BF),
            pltpu.VMEM((2, 2, 8, 2, 16, 128), BF),
            pltpu.VMEM((32, 256, 128), BF),
            pltpu.VMEM((32, 2, 4, 16, 128), BF),
            pltpu.VMEM((STEPS, 512, 640), BF),
            pltpu.VMEM((STEPS, 512, 256), BF),
            pltpu.VMEM((STEPS, 512, 128), BF),
            one,
            one, one, one, one, one, one,
            one, one, one, one,
            dma((16,)), one, two, one, dma((2, 2)), dma((2, 2)), dma((2, 2)), dma((2, 2)), two, two,
            dma((4, 2)), four, four, four, dma((4, 2, 2)), dma((4, 2, 2)), dma((4, 2)), dma((4, 2)), four, four,
            two, two, two, two, two, two, four, four,
        ],
        compiler_params=pltpu.CompilerParams(
            collective_id=0, has_side_effects=True, vmem_limit_bytes=56 * 1024 * 1024
        ),
    )(ao_order, density, virt_coeff, block_coeff)


def solution(mesh):
    return jax.shard_map(
        shards,
        mesh=mesh,
        in_specs=(P("virt", "ao", None), P("virt", None), P("ao", None), P()),
        out_specs=P("ao", "virt", None),
        check_vma=False,
    )
```

```python
import jax
import jax.numpy as jnp
from jax import lax
from jax.experimental import pallas as pl
from jax.experimental.pallas import tpu as pltpu
from jax.sharding import PartitionSpec as P

MESH = pl.DeviceIdType.MESH
BF = jnp.bfloat16
F32 = jnp.float32
TN = (((0,), (0,)), ((), ()))
NT = (((1,), (1,)), ((), ()))
STEPS = 4
BLOCKS = [(y % 2, (y // 2) * 8 + x * 2 + c) for c in range(2) for x in range(4) for y in range(4)]
BLOCKS += [(y % 2, 16 + (y // 2) * 2 + h) for h in range(2) for y in range(4)]


def exchange(
    order_hbm, d_ref, c_ref, b_ref, o_ref,
    order, dl, cl, bl, hot, pt, kp, df, dp, cf, cp, tt, s, r, rf, g, gh, gx, tm, tq, hb, ho, hq,
    order_sem, ds, dr, des, der, dks, dkr, bs, br, bks, bkr, zcs, zcr, ycs, ycr, xcs, xcr, fcs, fcr, kcs, kcr,
    zs, zr, ys, yr, xs, xr, fs, fr, hs, hr, yhs, yhr, xhs, xhr, fhs, fhr, qs, qr,
):
    v, j = lax.axis_index("virt"), lax.axis_index("ao")
    y_lo, z = v // 16, v % 16
    core, x, y_hi = j % 2, (j // 2) % 4, j // 8
    y = 2 * y_hi + y_lo
    share = j % 4
    right, left, far = (x + 1) % 4, (x + 3) % 4, (x + 2) % 4
    chip = j // 2

    def lanes_of(yh, e):
        return pl.ds(pl.multiple_of(yh * 512 + core * 256 + e * 128, 128), 128)

    lanes = lanes_of(x % 2, x // 2)

    def dev(yy, xx):
        return (yy % 2) * 16 + z, (yy // 2) * 8 + xx * 2 + core

    other = (v, j + 1 - 2 * core)
    to_right, to_left = dev(y, right), dev(y, left)

    def remote(src, dst, send, recv, device):
        return pltpu.make_async_remote_copy(
            src_ref=src, dst_ref=dst, send_sem=send, recv_sem=recv, device_id=device, device_id_type=MESH
        )

    def arrived(ref, sem):
        remote(ref, ref, sem, sem, other).wait_recv()

    def left_for(ref, sem):
        remote(ref, ref, sem, sem, other).wait_send()

    order_copy = pltpu.make_async_copy(order_hbm, order, order_sem)
    order_copy.start()

    barrier = pltpu.get_barrier_semaphore()

    def to_and_fro(w):
        return (w + 1) // 2 * (1 - 2 * (w % 2))

    @pl.loop(0, 15)
    def _(w):
        zv = y_lo * 16 + (z + 8 + to_and_fro(w)) % 16
        pl.semaphore_signal(barrier, inc=1, device_id=(zv, j), device_id_type=MESH)

        @pl.when(z // 8 != core)
        def _():
            pl.semaphore_signal(barrier, inc=1, device_id=(zv, j + 1 - 2 * core), device_id_type=MESH)

    for dy in (1, 3):
        pl.semaphore_signal(barrier, inc=1, device_id=dev((y + dy) % 4, x), device_id_type=MESH)

    pl.semaphore_signal(barrier, inc=1, device_id=other, device_id_type=MESH)

    @pl.loop(1, 8)
    def _(t):
        pl.semaphore_signal(barrier, inc=1, device_id=(v, (j + 2 * t) % 16), device_id_type=MESH)

    pl.semaphore_wait(barrier, 32 + (z // 8 + core) % 2)

    @pl.loop(0, 15)
    def _(w):
        zv = y_lo * 16 + (z + 8 + to_and_fro(w)) % 16
        remote(c_ref.at[:, lanes], cl.at[x, y_lo, z], zcs.at[w], zcr, (zv, j)).start()

    pltpu.make_async_copy(c_ref.at[:, lanes], cl.at[x, y_lo, z], zcr).start()

    @pl.loop(1, 8)
    def _(t):
        jj = (j + 2 * t) % 16
        remote(d_ref.at[pl.ds(jj // 2 * 2, 2)], dl.at[pl.ds(0, 2), core, chip], ds, dr, (v, jj)).start()
        remote(d_ref.at[16 + jj // 4], dl.at[2, core, chip], des, der, (v, jj)).start()

    pltpu.make_async_copy(d_ref.at[pl.ds(chip * 2, 2)], dl.at[pl.ds(0, 2), core, chip], dr).start()
    pltpu.make_async_copy(d_ref.at[16 + j // 4], dl.at[2, core, chip], der).start()

    order_copy.wait()
    column = lax.broadcasted_iota(jnp.int32, (1, 1024), 1)

    @pl.loop(0, 128)
    def _(k):
        hot[pl.ds(k, 1), :] = jnp.where(column == order[chip * 128 + k], 1.0, 0.0).astype(F32)

    def coeff_x(part, yl):
        blk = cl.at[x, yl]
        remote(blk, blk, xcs.at[0, part], xcr.at[0, part], to_right).start()
        remote(blk, blk, xcs.at[1, part], xcr.at[1, part], to_left).start()

    def coeff_on(part, yl):
        for way, (frm, device) in enumerate(((left, to_right), (right, to_left))):
            arrived(cl.at[frm, yl], xcr.at[way, part])
            blk = cl.at[frm, yl, pl.ds(way * 8, 8)]
            remote(blk, blk, fcs.at[way, part], fcr.at[way, part], device).start()

    arrived(cl.at[x, y_lo], zcr)
    for e, dy in enumerate((3, 1)):
        blk = cl.at[x, y_lo, pl.ds(e * 8, 8)]
        remote(blk, blk, ycs.at[e], ycr, dev((y + dy) % 4, x)).start()
    coeff_x(0, y_lo)

    arrived(dl.at[pl.ds(0, 2), core], dr)
    arrived(dl.at[2, core], der)
    remote(dl.at[:, core], dl.at[:, core], dks, dkr, other).start()

    arrived(cl.at[x, 1 - y_lo], ycr)
    coeff_x(1, 1 - y_lo)
    coeff_on(0, y_lo)

    arrived(dl.at[:, 1 - core], dkr)
    for u in range(3):
        for jj in range(16):
            df[u, pl.ds(jj * 40, 40), :] = dl[u, jj % 2, jj // 2].astype(F32)
        for q, (yl, i) in enumerate(BLOCKS):
            dp[pl.ds(q * 16, 16), pl.ds(u * 128, 128)] = df[u, pl.ds(yl * 320 + i, 16, stride=20), :].astype(BF)

    def both_ways(blocks, send, recv):
        for half in range(2):
            for way, device in enumerate((to_right, to_left)):
                blk = blocks(half ^ way)
                remote(blk, blk, send.at[way, half], recv.at[way, half], device).start()

    def widen(xx, yl):
        for zz in range(16):
            cf[yl * 16 + zz, pl.ds(0, 20), :] = cl[xx, yl, zz].astype(F32)

    def relay(xx):
        widen(xx, 0)
        widen(xx, 1)
        turn_coeff(xx)

    def turn_coeff(xx):
        flat = cf.reshape(32 * 24, 128)
        to = lanes_of(xx % 2, xx // 2)
        for q, (yl, i) in enumerate(BLOCKS):
            cp[pl.ds(q * 16, 16), to] = flat[pl.ds(yl * 384 + i, 16, stride=24), :].astype(BF)
        tt[xx] = lax.dot_general(cp[:, to], dp[...], TN, preferred_element_type=F32).astype(BF)

    relay(x)
    coeff_on(1, 1 - y_lo)

    @pl.loop(1, 8)
    def _(t):
        remote(b_ref, bl.at[core, chip], bs, br, (v, (j + 2 * t) % 16)).start()

    pltpu.make_async_copy(b_ref, bl.at[core, chip], br).start()

    relay(left)
    relay(right)

    def regroup(k, e):
        for yh in range(2):
            for q in range(4):
                rows = tt[2 * e + yh, q * 32 + k * 8:q * 32 + k * 8 + 8, :]
                s[0, k, e * 4 + q, pl.ds(yh * 8, 8), :] = rows[:, :128]
                s[1, k, e * 4 + q, pl.ds(yh * 8, 8), :] = rows[:, 128:256]
                s[k % 2, k, e * 4 + q, pl.ds(16 + yh * 8, 8), :] = rows[:, 256:]

    def whole(k, c):
        return jnp.logical_and(c == k % 2, x % 2 == k // 2)

    def to_planes(k, e):
        for c in range(2):
            def along_z(part):
                @pl.loop(0, 4)
                def _(w):
                    zl = e * 4 + (z + w) % 4
                    zz = core * 8 + zl
                    itself = jnp.logical_and(zz == z, c == core)

                    @pl.when(itself)
                    def _():
                        pltpu.make_async_copy(s.at[c, k, zl, part], r.at[k, z, part], zr.at[k]).start()

                    @pl.when(jnp.logical_not(itself))
                    def _():
                        remote(s.at[c, k, zl, part], r.at[k, z, part], zs.at[k, c], zr.at[k],
                               (y_lo * 16 + zz, chip * 2 + c)).start()

            @pl.when(whole(k, c))
            def _():
                along_z(pl.ds(0, 32))

            @pl.when(jnp.logical_not(whole(k, c)))
            def _():
                along_z(pl.ds(0, 16))

    def at(block, count=1):
        return pl.ds(pl.multiple_of(block * 16, 16), count * 16)

    def piece(k):
        return pl.ds(k * 8, 8)

    def turn(k, first, dst):
        for zz in range(16):
            rf[pl.ds(zz * 16, 16), :] = r[k, zz, pl.ds(first, 16), :].astype(F32)
        for i in range(16):
            dst[i // 8, i % 8] = rf[pl.ds(i, 16, stride=16), :].astype(BF)

    def main(k, xx, first=0, count=4):
        return tm.at[piece(k), at(xx * 4 + first, count), :]

    def pooled(k, xx):
        return gx.at[k // 2, :, :, xx // 2]

    def along_y(k):
        @pl.when(share != k)
        def _():
            arrived(r.at[k, :, pl.ds(0, 16)], zr.at[k])

        @pl.when(share == k)
        def _():
            arrived(r.at[k], zr.at[k])

        turn(k, 0, g.at[k])
        for dy in (2, 1, 3):
            half = y_lo if dy == 2 else 1 - y_lo
            remote(g.at[k, half], main(k, x, y, 1), ys.at[k], yr.at[k], dev((y + dy) % 4, x)).start()
        tm[piece(k), at(x * 4 + y), :] = g[k, y_lo]

        @pl.when(share == k)
        def _():
            turn(k, 16, gh)
            gx[k // 2, :, :, x // 2] = gh[...]
            for way, device in enumerate((to_right, to_left)):
                remote(pooled(k, x), pooled(k, x), xhs.at[way], xhr.at[way], device).start()

    def along_x(k):
        arrived(main(k, x, 0, 3), yr.at[k])
        both_ways(lambda part: main(k, x, 2 * part, 2), xs.at[k], xr.at[k])

        @pl.when(jnp.logical_and(core == k % 2, x % 2 != k // 2))
        def _():
            for way, (frm, device) in enumerate(((left, to_right), (right, to_left))):
                arrived(pooled(k, frm), xhr.at[way])
                blk = gx.at[k // 2, way, :, frm // 2]
                remote(blk, blk, fhs.at[way], fhr.at[way], device).start()

    def pass_on(k):
        for way, (frm, device) in enumerate(((left, to_right), (right, to_left))):
            blk = main(k, frm, 2 * way, 2)
            arrived(blk, xr.at[k, way, 0])
            remote(blk, blk, fs.at[k, way], fr.at[k, way], device).start()

        @pl.when(core == k % 2)
        def _():
            @pl.when(share == k)
            def _():
                for way in range(2):
                    arrived(gx.at[k // 2, way, :, far // 2], fhr.at[way])

            for dy in (2, 1, 3):
                half = y_lo if dy == 2 else 1 - y_lo
                remote(gx.at[k // 2, half], tq.at[piece(k), :, y], yhs.at[k // 2], yhr.at[k // 2], dev((y + dy) % 4, x)).start()
            tq[piece(k), :, y] = gx[k // 2, y_lo]

    def sides(k):
        for way, frm in enumerate((left, right)):
            arrived(main(k, frm, 2 - 2 * way, 2), xr.at[k, way, 1])

    mine_at = pl.ds(pl.multiple_of(core * 256, 256), 256)
    theirs_at = pl.ds(pl.multiple_of((1 - core) * 256, 256), 256)
    pool_at = pl.ds(512, 128)

    def to_other_s(k):
        arrived(main(k, far, 0, 2), fr.at[k, 0])
        arrived(main(k, far, 2, 2), fr.at[k, 1])
        terms = jnp.concatenate([tm[k * 8 + n] for n in range(8)], axis=1)
        ho[k] = lax.dot_general(kp[1 - core], terms, NT, preferred_element_type=F32).astype(BF)
        remote(ho.at[k], hb.at[k, :, mine_at], hs.at[k], hr.at[k], other).start()

        @pl.when(core == k % 2)
        def _():
            arrived(tq.at[piece(k), :, pl.ds(0, 3)], yhr.at[k // 2])
            terms = jnp.concatenate([tq[k * 8 + n].reshape(128, 128) for n in range(8)], axis=1)
            hq[k] = lax.dot_general(kp[1 - core], terms, NT, preferred_element_type=F32).astype(BF)
            remote(hq.at[k], hb.at[k, :, pool_at], qs.at[k], qr.at[k], other).start()

    def to_own_s(k):
        @pl.when(core == k % 2)
        def _():
            terms = jnp.concatenate([tq[k * 8 + n].reshape(128, 128) for n in range(8)], axis=1)
            hb[k, :, pool_at] = lax.dot_general(kp[core], terms, NT, preferred_element_type=F32).astype(BF)

        terms = jnp.concatenate([tm[k * 8 + n] for n in range(8)], axis=1)
        hb[k, :, mine_at] = lax.dot_general(kp[core], terms, NT, preferred_element_type=F32).astype(BF)

    def to_m(k):
        arrived(hb.at[k, :, theirs_at], hr.at[k])

        @pl.when(core != k % 2)
        def _():
            arrived(hb.at[k, :, pool_at], qr.at[k])

        @pl.loop(0, 4)
        def _(q):
            cols = pl.ds(pl.multiple_of(q * 256, 256), 256)
            out = jnp.dot(hb[k], cp[:, cols], preferred_element_type=F32)
            o_ref[:, pl.ds(k * 8, 8), cols] = out.reshape(64, 8, 256).astype(BF)

    near = x // 2
    regroup(0, near)
    to_planes(0, near)
    for part, yl in enumerate((y_lo, 1 - y_lo)):
        for way in range(2):
            arrived(cl.at[far, yl, pl.ds(way * 8, 8)], fcr.at[way, part])
        widen(far, yl)
    turn_coeff(far)

    regroup(0, 1 - near)
    to_planes(0, 1 - near)
    arrived(bl.at[core], br)
    remote(bl.at[core], bl.at[core], bks, bkr, other).start()
    for k in (1, 2):
        for e in range(2):
            regroup(k, e)
            to_planes(k, e)

    arrived(bl.at[1 - core], bkr)
    block = jnp.concatenate([bl[q % 2, q // 2].astype(F32) for q in range(16)], axis=0).astype(BF)
    pt[...] = lax.dot_general(hot[...].astype(BF), block, NT, preferred_element_type=F32).astype(BF)
    spread = lax.broadcasted_iota(jnp.int32, (512, 64), 0) // 8 == lax.broadcasted_iota(jnp.int32, (512, 64), 1)
    place = lax.broadcasted_iota(jnp.int32, (512, 128), 0) % 8
    for e in range(2):
        panel = jnp.dot(jnp.where(spread, 1.0, 0.0).astype(BF), pt[e * 64:(e + 1) * 64], preferred_element_type=F32)
        for n in range(8):
            kp[e, :, pl.ds(n * 128, 128)] = jnp.where(place == n, panel, 0.0).astype(BF)

    along_y(0)
    for e in range(2):
        regroup(3, e)
        to_planes(3, e)
    along_x(0)

    def coeff_half(e, c):
        return cp.at[:, pl.ds(pl.multiple_of(e * 512 + c * 256, 256), 256)]

    for e in range(2):
        remote(coeff_half(e, core), coeff_half(e, core), kcs.at[e], kcr.at[e], other).start()

    along_y(1)
    along_x(1)
    pass_on(0)
    along_y(2)
    sides(0)
    along_x(2)
    pass_on(1)
    along_y(3)
    sides(1)
    to_other_s(0)
    to_own_s(0)
    along_x(3)
    pass_on(2)
    sides(2)
    for e in range(2):
        arrived(coeff_half(e, 1 - core), kcr.at[e])
    to_m(0)
    to_other_s(1)
    to_own_s(1)
    pass_on(3)
    sides(3)
    to_m(1)
    to_other_s(2)
    to_other_s(3)
    to_own_s(2)
    to_own_s(3)
    to_m(2)
    to_m(3)

    @pl.loop(0, 15)
    def _(w):
        left_for(c_ref.at[:, lanes], zcs.at[w])

    left_for(dl.at[pl.ds(0, 2), core, pl.ds(0, 7)], ds)
    left_for(dl.at[2, core, pl.ds(0, 7)], des)
    left_for(dl.at[:, core], dks)
    left_for(bl.at[core, pl.ds(0, 7)], bs)
    left_for(bl.at[core], bks)
    for e in range(2):
        left_for(cl.at[x, y_lo, pl.ds(0, 8)], ycs.at[e])
        for half in range(2):
            left_for(cl.at[x, 0], xcs.at[e, half])
            left_for(cl.at[x, 0, pl.ds(0, 8)], fcs.at[e, half])
        left_for(cp.at[:, pl.ds(e * 256, 256)], kcs.at[e])
    for e in range(2):
        left_for(tq.at[pl.ds(0, 8), :, pl.ds(0, 3)], yhs.at[e])
        left_for(gx.at[0, :, :, 0], xhs.at[e])
        left_for(gx.at[0, 0, :, 0], fhs.at[e])
    for k in range(STEPS):
        for c in range(2):
            itself = jnp.logical_and(z // 8 == core, c == core)
            for count, few in ((7, itself), (8, jnp.logical_not(itself))):
                @pl.when(jnp.logical_and(few, whole(k, c)))
                def _():
                    left_for(s.at[c, k, pl.ds(0, count)], zs.at[k, c])

                @pl.when(jnp.logical_and(few, jnp.logical_not(whole(k, c))))
                def _():
                    left_for(s.at[c, k, pl.ds(0, count), pl.ds(0, 16)], zs.at[k, c])

        left_for(main(k, x, 0, 3), ys.at[k])
        for e in range(2):
            for half in range(2):
                left_for(main(k, x, 0, 2), xs.at[k, e, half])
            left_for(main(k, x, 0, 2), fs.at[k, e])
        left_for(ho.at[k], hs.at[k])

        @pl.when(core == k % 2)
        def _():
            left_for(hq.at[k], qs.at[k])


def shards(density, virt_coeff, block_coeff, ao_order):
    hbm = pl.BlockSpec(memory_space=pltpu.HBM)
    dma = pltpu.SemaphoreType.DMA
    one, two, four = dma, dma((2,)), dma((4,))
    return pl.pallas_call(
        exchange,
        out_shape=pltpu.VMEM((64, 32, 1024), BF),
        in_specs=[hbm] * 4,
        out_specs=pl.BlockSpec(memory_space=pltpu.VMEM),
        scratch_shapes=[
            pltpu.SMEM((1024,), jnp.int32),
            pltpu.VMEM((3, 2, 8, 40, 128), BF),
            pltpu.VMEM((4, 2, 16, 20, 128), BF),
            pltpu.VMEM((2, 8, 8, 1024), BF),
            pltpu.VMEM((128, 1024), F32),
            pltpu.VMEM((128, 128), BF),
            pltpu.VMEM((2, 512, 1024), BF),
            pltpu.VMEM((3, 640, 128), F32),
            pltpu.VMEM((640, 384), BF),
            pltpu.VMEM((32, 24, 128), F32),
            pltpu.VMEM((640, 1024), BF),
            pltpu.VMEM((4, 128, 384), BF),
            pltpu.VMEM((2, STEPS, 8, 32, 128), BF),
            pltpu.VMEM((STEPS, 16, 32, 128), BF),
            pltpu.VMEM((256, 128), F32),
            pltpu.VMEM((STEPS, 2, 8, 16, 128), BF),
            pltpu.VMEM((2, 8, 16, 128), BF),
            pltpu.VMEM((2, 2, 8, 2, 16, 128), BF),
            pltpu.VMEM((32, 256, 128), BF),
            pltpu.VMEM((32, 2, 4, 16, 128), BF),
            pltpu.VMEM((STEPS, 512, 640), BF),
            pltpu.VMEM((STEPS, 512, 256), BF),
            pltpu.VMEM((STEPS, 512, 128), BF),
            one,
            one, one, one, one, one, one,
            one, one, one, one,
            dma((16,)), one, two, one, dma((2, 2)), dma((2, 2)), dma((2, 2)), dma((2, 2)), two, two,
            dma((4, 2)), four, four, four, dma((4, 2, 2)), dma((4, 2, 2)), dma((4, 2)), dma((4, 2)), four, four,
            two, two, two, two, two, two, four, four,
        ],
        compiler_params=pltpu.CompilerParams(
            collective_id=0, has_side_effects=True, vmem_limit_bytes=56 * 1024 * 1024
        ),
    )(ao_order, density, virt_coeff, block_coeff)


def solution(mesh):
    return jax.shard_map(
        shards,
        mesh=mesh,
        in_specs=(P("virt", "ao", None), P("virt", None), P("ao", None), P()),
        out_specs=P("ao", "virt", None),
        check_vma=False,
    )
```

```python
import jax
import jax.numpy as jnp
from jax import lax
from jax.experimental import pallas as pl
from jax.experimental.pallas import tpu as pltpu
from jax.sharding import PartitionSpec as P

MESH = pl.DeviceIdType.MESH
BF = jnp.bfloat16
F32 = jnp.float32
TN = (((0,), (0,)), ((), ()))
NT = (((1,), (1,)), ((), ()))
STEPS = 4
BLOCKS = [(y % 2, (y // 2) * 8 + x * 2 + c) for c in range(2) for x in range(4) for y in range(4)]
BLOCKS += [(y % 2, 16 + (y // 2) * 2 + h) for h in range(2) for y in range(4)]


def exchange(
    order_hbm, d_ref, c_ref, b_ref, o_ref,
    order, dl, cl, bl, hot, pt, kp, df, dp, cf, cp, tt, s, r, rf, g, gh, gx, tm, tq, hb, ho, hq,
    order_sem, ds, dr, des, der, dks, dkr, bs, br, bks, bkr, zcs, zcr, ycs, ycr, xcs, xcr, fcs, fcr, kcs, kcr,
    zs, zr, ys, yr, xs, xr, fs, fr, hs, hr, yhs, yhr, xhs, xhr, fhs, fhr, qs, qr,
):
    v, j = lax.axis_index("virt"), lax.axis_index("ao")
    y_lo, z = v // 16, v % 16
    core, x, y_hi = j % 2, (j // 2) % 4, j // 8
    y = 2 * y_hi + y_lo
    share = j % 4
    right, left, far = (x + 1) % 4, (x + 3) % 4, (x + 2) % 4
    chip = j // 2

    def lanes_of(yh, e):
        return pl.ds(pl.multiple_of(yh * 512 + core * 256 + e * 128, 128), 128)

    lanes = lanes_of(x % 2, x // 2)

    def dev(yy, xx):
        return (yy % 2) * 16 + z, (yy // 2) * 8 + xx * 2 + core

    other = (v, j + 1 - 2 * core)
    to_right, to_left = dev(y, right), dev(y, left)

    def remote(src, dst, send, recv, device):
        return pltpu.make_async_remote_copy(
            src_ref=src, dst_ref=dst, send_sem=send, recv_sem=recv, device_id=device, device_id_type=MESH
        )

    def arrived(ref, sem):
        remote(ref, ref, sem, sem, other).wait_recv()

    def left_for(ref, sem):
        remote(ref, ref, sem, sem, other).wait_send()

    order_copy = pltpu.make_async_copy(order_hbm, order, order_sem)
    order_copy.start()

    barrier = pltpu.get_barrier_semaphore()

    def to_and_fro(w):
        return (w + 1) // 2 * (1 - 2 * (w % 2))

    @pl.loop(0, 15)
    def _(w):
        zv = y_lo * 16 + (z + 8 + to_and_fro(w)) % 16
        pl.semaphore_signal(barrier, inc=1, device_id=(zv, j), device_id_type=MESH)

        @pl.when(z // 8 != core)
        def _():
            pl.semaphore_signal(barrier, inc=1, device_id=(zv, j + 1 - 2 * core), device_id_type=MESH)

    for dy in (1, 3):
        pl.semaphore_signal(barrier, inc=1, device_id=dev((y + dy) % 4, x), device_id_type=MESH)

    pl.semaphore_signal(barrier, inc=1, device_id=other, device_id_type=MESH)

    @pl.loop(1, 8)
    def _(t):
        pl.semaphore_signal(barrier, inc=1, device_id=(v, (j + 2 * t) % 16), device_id_type=MESH)

    pl.semaphore_wait(barrier, 32 + (z // 8 + core) % 2)

    @pl.loop(0, 15)
    def _(w):
        zv = y_lo * 16 + (z + 8 + to_and_fro(w)) % 16
        remote(c_ref.at[:, lanes], cl.at[x, y_lo, z], zcs.at[w], zcr, (zv, j)).start()

    pltpu.make_async_copy(c_ref.at[:, lanes], cl.at[x, y_lo, z], zcr).start()

    @pl.loop(1, 8)
    def _(t):
        jj = (j + 2 * t) % 16
        remote(d_ref.at[pl.ds(jj // 2 * 2, 2)], dl.at[pl.ds(0, 2), core, chip], ds, dr, (v, jj)).start()
        remote(d_ref.at[16 + jj // 4], dl.at[2, core, chip], des, der, (v, jj)).start()

    pltpu.make_async_copy(d_ref.at[pl.ds(chip * 2, 2)], dl.at[pl.ds(0, 2), core, chip], dr).start()
    pltpu.make_async_copy(d_ref.at[16 + j // 4], dl.at[2, core, chip], der).start()

    order_copy.wait()
    column = lax.broadcasted_iota(jnp.int32, (1, 1024), 1)

    @pl.loop(0, 128)
    def _(k):
        hot[pl.ds(k, 1), :] = jnp.where(column == order[chip * 128 + k], 1.0, 0.0).astype(F32)

    def coeff_x(part, yl):
        blk = cl.at[x, yl]
        remote(blk, blk, xcs.at[0, part], xcr.at[0, part], to_right).start()
        remote(blk, blk, xcs.at[1, part], xcr.at[1, part], to_left).start()

    def coeff_on(part, yl):
        for way, (frm, device) in enumerate(((left, to_right), (right, to_left))):
            arrived(cl.at[frm, yl], xcr.at[way, part])
            blk = cl.at[frm, yl, pl.ds(way * 8, 8)]
            remote(blk, blk, fcs.at[way, part], fcr.at[way, part], device).start()

    arrived(cl.at[x, y_lo], zcr)
    for e, dy in enumerate((3, 1)):
        blk = cl.at[x, y_lo, pl.ds(e * 8, 8)]
        remote(blk, blk, ycs.at[e], ycr, dev((y + dy) % 4, x)).start()
    coeff_x(0, y_lo)

    arrived(dl.at[pl.ds(0, 2), core], dr)
    arrived(dl.at[2, core], der)
    remote(dl.at[:, core], dl.at[:, core], dks, dkr, other).start()

    arrived(cl.at[x, 1 - y_lo], ycr)
    coeff_x(1, 1 - y_lo)
    coeff_on(0, y_lo)

    arrived(dl.at[:, 1 - core], dkr)
    for u in range(3):
        for jj in range(16):
            df[u, pl.ds(jj * 40, 40), :] = dl[u, jj % 2, jj // 2].astype(F32)
        for q, (yl, i) in enumerate(BLOCKS):
            dp[pl.ds(q * 16, 16), pl.ds(u * 128, 128)] = df[u, pl.ds(yl * 320 + i, 16, stride=20), :].astype(BF)

    def both_ways(blocks, send, recv):
        for half in range(2):
            for way, device in enumerate((to_right, to_left)):
                blk = blocks(half ^ way)
                remote(blk, blk, send.at[way, half], recv.at[way, half], device).start()

    def widen(xx, yl, slot):
        for zz in range(16):
            cf[slot, yl * 16 + zz, pl.ds(0, 20), :] = cl[xx, yl, zz].astype(F32)

    def turn_coeff(xx, slot):
        flat = cf.at[slot].reshape(32 * 24, 128)
        to = lanes_of(xx % 2, xx // 2)
        for q, (yl, i) in enumerate(BLOCKS):
            cp[pl.ds(q * 16, 16), to] = flat[pl.ds(yl * 384 + i, 16, stride=24), :].astype(BF)
        tt[xx] = lax.dot_general(cp[:, to], dp[...], TN, preferred_element_type=F32).astype(BF)

    widen(x, 0, 0)
    widen(x, 1, 0)
    turn_coeff(x, 0)
    widen(left, y_lo, 0)
    widen(right, y_lo, 1)
    coeff_on(1, 1 - y_lo)

    @pl.loop(1, 8)
    def _(t):
        remote(b_ref, bl.at[core, chip], bs, br, (v, (j + 2 * t) % 16)).start()

    pltpu.make_async_copy(b_ref, bl.at[core, chip], br).start()

    for slot, xx in enumerate((left, right)):
        widen(xx, 1 - y_lo, slot)
        turn_coeff(xx, slot)

    def regroup(k, e):
        for yh in range(2):
            for q in range(4):
                rows = tt[2 * e + yh, q * 32 + k * 8:q * 32 + k * 8 + 8, :]
                s[0, k, e * 4 + q, pl.ds(yh * 8, 8), :] = rows[:, :128]
                s[1, k, e * 4 + q, pl.ds(yh * 8, 8), :] = rows[:, 128:256]
                s[k % 2, k, e * 4 + q, pl.ds(16 + yh * 8, 8), :] = rows[:, 256:]

    def whole(k, c):
        return jnp.logical_and(c == k % 2, x % 2 == k // 2)

    def to_planes(k, e):
        for c in range(2):
            def along_z(part):
                @pl.loop(0, 4)
                def _(w):
                    zl = e * 4 + (z + w) % 4
                    zz = core * 8 + zl
                    itself = jnp.logical_and(zz == z, c == core)

                    @pl.when(itself)
                    def _():
                        pltpu.make_async_copy(s.at[c, k, zl, part], r.at[k, z, part], zr.at[k]).start()

                    @pl.when(jnp.logical_not(itself))
                    def _():
                        remote(s.at[c, k, zl, part], r.at[k, z, part], zs.at[k, c], zr.at[k],
                               (y_lo * 16 + zz, chip * 2 + c)).start()

            @pl.when(whole(k, c))
            def _():
                along_z(pl.ds(0, 32))

            @pl.when(jnp.logical_not(whole(k, c)))
            def _():
                along_z(pl.ds(0, 16))

    def at(block, count=1):
        return pl.ds(pl.multiple_of(block * 16, 16), count * 16)

    def piece(k):
        return pl.ds(k * 8, 8)

    def turn(k, first, dst):
        for zz in range(16):
            rf[pl.ds(zz * 16, 16), :] = r[k, zz, pl.ds(first, 16), :].astype(F32)
        for i in range(16):
            dst[i // 8, i % 8] = rf[pl.ds(i, 16, stride=16), :].astype(BF)

    def main(k, xx, first=0, count=4):
        return tm.at[piece(k), at(xx * 4 + first, count), :]

    def pooled(k, xx):
        return gx.at[k // 2, :, :, xx // 2]

    def along_y(k):
        @pl.when(share != k)
        def _():
            arrived(r.at[k, :, pl.ds(0, 16)], zr.at[k])

        @pl.when(share == k)
        def _():
            arrived(r.at[k], zr.at[k])

        turn(k, 0, g.at[k])
        for dy in (2, 1, 3):
            half = y_lo if dy == 2 else 1 - y_lo
            remote(g.at[k, half], main(k, x, y, 1), ys.at[k], yr.at[k], dev((y + dy) % 4, x)).start()
        tm[piece(k), at(x * 4 + y), :] = g[k, y_lo]

        @pl.when(share == k)
        def _():
            turn(k, 16, gh)
            gx[k // 2, :, :, x // 2] = gh[...]
            for way, device in enumerate((to_right, to_left)):
                remote(pooled(k, x), pooled(k, x), xhs.at[way], xhr.at[way], device).start()

    def along_x(k):
        arrived(main(k, x, 0, 3), yr.at[k])
        both_ways(lambda part: main(k, x, 2 * part, 2), xs.at[k], xr.at[k])

        @pl.when(jnp.logical_and(core == k % 2, x % 2 != k // 2))
        def _():
            for way, (frm, device) in enumerate(((left, to_right), (right, to_left))):
                arrived(pooled(k, frm), xhr.at[way])
                blk = gx.at[k // 2, way, :, frm // 2]
                remote(blk, blk, fhs.at[way], fhr.at[way], device).start()

    def pass_on(k):
        for way, (frm, device) in enumerate(((left, to_right), (right, to_left))):
            blk = main(k, frm, 2 * way, 2)
            arrived(blk, xr.at[k, way, 0])
            remote(blk, blk, fs.at[k, way], fr.at[k, way], device).start()

        @pl.when(core == k % 2)
        def _():
            @pl.when(share == k)
            def _():
                for way in range(2):
                    arrived(gx.at[k // 2, way, :, far // 2], fhr.at[way])

            for dy in (2, 1, 3):
                half = y_lo if dy == 2 else 1 - y_lo
                remote(gx.at[k // 2, half], tq.at[piece(k), :, y], yhs.at[k // 2], yhr.at[k // 2], dev((y + dy) % 4, x)).start()
            tq[piece(k), :, y] = gx[k // 2, y_lo]

    def sides(k):
        for way, frm in enumerate((left, right)):
            arrived(main(k, frm, 2 - 2 * way, 2), xr.at[k, way, 1])

    mine_at = pl.ds(pl.multiple_of(core * 256, 256), 256)
    theirs_at = pl.ds(pl.multiple_of((1 - core) * 256, 256), 256)
    pool_at = pl.ds(512, 128)

    def to_other_s(k):
        arrived(main(k, far, 0, 2), fr.at[k, 0])
        arrived(main(k, far, 2, 2), fr.at[k, 1])
        terms = jnp.concatenate([tm[k * 8 + n] for n in range(8)], axis=1)
        ho[k] = lax.dot_general(kp[1 - core], terms, NT, preferred_element_type=F32).astype(BF)
        remote(ho.at[k], hb.at[k, :, mine_at], hs.at[k], hr.at[k], other).start()

        @pl.when(core == k % 2)
        def _():
            arrived(tq.at[piece(k), :, pl.ds(0, 3)], yhr.at[k // 2])
            terms = jnp.concatenate([tq[k * 8 + n].reshape(128, 128) for n in range(8)], axis=1)
            hq[k] = lax.dot_general(kp[1 - core], terms, NT, preferred_element_type=F32).astype(BF)
            remote(hq.at[k], hb.at[k, :, pool_at], qs.at[k], qr.at[k], other).start()

    def to_own_s(k):
        @pl.when(core == k % 2)
        def _():
            terms = jnp.concatenate([tq[k * 8 + n].reshape(128, 128) for n in range(8)], axis=1)
            hb[k, :, pool_at] = lax.dot_general(kp[core], terms, NT, preferred_element_type=F32).astype(BF)

        terms = jnp.concatenate([tm[k * 8 + n] for n in range(8)], axis=1)
        hb[k, :, mine_at] = lax.dot_general(kp[core], terms, NT, preferred_element_type=F32).astype(BF)

    def to_m(k):
        arrived(hb.at[k, :, theirs_at], hr.at[k])

        @pl.when(core != k % 2)
        def _():
            arrived(hb.at[k, :, pool_at], qr.at[k])

        @pl.loop(0, 4)
        def _(q):
            cols = pl.ds(pl.multiple_of(q * 256, 256), 256)
            out = jnp.dot(hb[k], cp[:, cols], preferred_element_type=F32)
            o_ref[:, pl.ds(k * 8, 8), cols] = out.reshape(64, 8, 256).astype(BF)

    near = x // 2
    regroup(0, near)
    to_planes(0, near)
    for part, yl in enumerate((y_lo, 1 - y_lo)):
        for way in range(2):
            arrived(cl.at[far, yl, pl.ds(way * 8, 8)], fcr.at[way, part])
        widen(far, yl, 0)
    turn_coeff(far, 0)

    regroup(0, 1 - near)
    to_planes(0, 1 - near)
    arrived(bl.at[core], br)
    remote(bl.at[core], bl.at[core], bks, bkr, other).start()
    for k in (1, 2):
        for e in range(2):
            regroup(k, e)
            to_planes(k, e)

    arrived(bl.at[1 - core], bkr)
    block = jnp.concatenate([bl[q % 2, q // 2].astype(F32) for q in range(16)], axis=0).astype(BF)
    pt[...] = lax.dot_general(hot[...].astype(BF), block, NT, preferred_element_type=F32).astype(BF)
    spread = lax.broadcasted_iota(jnp.int32, (512, 64), 0) // 8 == lax.broadcasted_iota(jnp.int32, (512, 64), 1)
    place = lax.broadcasted_iota(jnp.int32, (512, 128), 0) % 8
    for e in range(2):
        panel = jnp.dot(jnp.where(spread, 1.0, 0.0).astype(BF), pt[e * 64:(e + 1) * 64], preferred_element_type=F32)
        for n in range(8):
            kp[e, :, pl.ds(n * 128, 128)] = jnp.where(place == n, panel, 0.0).astype(BF)

    along_y(0)
    for e in range(2):
        regroup(3, e)
        to_planes(3, e)
    along_x(0)

    def coeff_half(e, c):
        return cp.at[:, pl.ds(pl.multiple_of(e * 512 + c * 256, 256), 256)]

    for e in range(2):
        remote(coeff_half(e, core), coeff_half(e, core), kcs.at[e], kcr.at[e], other).start()

    along_y(1)
    along_x(1)
    pass_on(0)
    along_y(2)
    sides(0)
    along_x(2)
    pass_on(1)
    along_y(3)
    sides(1)
    to_other_s(0)
    to_own_s(0)
    along_x(3)
    pass_on(2)
    sides(2)
    for e in range(2):
        arrived(coeff_half(e, 1 - core), kcr.at[e])
    to_m(0)
    to_other_s(1)
    to_own_s(1)
    pass_on(3)
    sides(3)
    to_m(1)
    to_other_s(2)
    to_other_s(3)
    to_own_s(2)
    to_own_s(3)
    to_m(2)
    to_m(3)

    @pl.loop(0, 15)
    def _(w):
        left_for(c_ref.at[:, lanes], zcs.at[w])

    left_for(dl.at[pl.ds(0, 2), core, pl.ds(0, 7)], ds)
    left_for(dl.at[2, core, pl.ds(0, 7)], des)
    left_for(dl.at[:, core], dks)
    left_for(bl.at[core, pl.ds(0, 7)], bs)
    left_for(bl.at[core], bks)
    for e in range(2):
        left_for(cl.at[x, y_lo, pl.ds(0, 8)], ycs.at[e])
        for half in range(2):
            left_for(cl.at[x, 0], xcs.at[e, half])
            left_for(cl.at[x, 0, pl.ds(0, 8)], fcs.at[e, half])
        left_for(cp.at[:, pl.ds(e * 256, 256)], kcs.at[e])
    for e in range(2):
        left_for(tq.at[pl.ds(0, 8), :, pl.ds(0, 3)], yhs.at[e])
        left_for(gx.at[0, :, :, 0], xhs.at[e])
        left_for(gx.at[0, 0, :, 0], fhs.at[e])
    for k in range(STEPS):
        for c in range(2):
            itself = jnp.logical_and(z // 8 == core, c == core)
            for count, few in ((7, itself), (8, jnp.logical_not(itself))):
                @pl.when(jnp.logical_and(few, whole(k, c)))
                def _():
                    left_for(s.at[c, k, pl.ds(0, count)], zs.at[k, c])

                @pl.when(jnp.logical_and(few, jnp.logical_not(whole(k, c))))
                def _():
                    left_for(s.at[c, k, pl.ds(0, count), pl.ds(0, 16)], zs.at[k, c])

        left_for(main(k, x, 0, 3), ys.at[k])
        for e in range(2):
            for half in range(2):
                left_for(main(k, x, 0, 2), xs.at[k, e, half])
            left_for(main(k, x, 0, 2), fs.at[k, e])
        left_for(ho.at[k], hs.at[k])

        @pl.when(core == k % 2)
        def _():
            left_for(hq.at[k], qs.at[k])


def shards(density, virt_coeff, block_coeff, ao_order):
    hbm = pl.BlockSpec(memory_space=pltpu.HBM)
    dma = pltpu.SemaphoreType.DMA
    one, two, four = dma, dma((2,)), dma((4,))
    return pl.pallas_call(
        exchange,
        out_shape=pltpu.VMEM((64, 32, 1024), BF),
        in_specs=[hbm] * 4,
        out_specs=pl.BlockSpec(memory_space=pltpu.VMEM),
        scratch_shapes=[
            pltpu.SMEM((1024,), jnp.int32),
            pltpu.VMEM((3, 2, 8, 40, 128), BF),
            pltpu.VMEM((4, 2, 16, 20, 128), BF),
            pltpu.VMEM((2, 8, 8, 1024), BF),
            pltpu.VMEM((128, 1024), F32),
            pltpu.VMEM((128, 128), BF),
            pltpu.VMEM((2, 512, 1024), BF),
            pltpu.VMEM((3, 640, 128), F32),
            pltpu.VMEM((640, 384), BF),
            pltpu.VMEM((2, 32, 24, 128), F32),
            pltpu.VMEM((640, 1024), BF),
            pltpu.VMEM((4, 128, 384), BF),
            pltpu.VMEM((2, STEPS, 8, 32, 128), BF),
            pltpu.VMEM((STEPS, 16, 32, 128), BF),
            pltpu.VMEM((256, 128), F32),
            pltpu.VMEM((STEPS, 2, 8, 16, 128), BF),
            pltpu.VMEM((2, 8, 16, 128), BF),
            pltpu.VMEM((2, 2, 8, 2, 16, 128), BF),
            pltpu.VMEM((32, 256, 128), BF),
            pltpu.VMEM((32, 2, 4, 16, 128), BF),
            pltpu.VMEM((STEPS, 512, 640), BF),
            pltpu.VMEM((STEPS, 512, 256), BF),
            pltpu.VMEM((STEPS, 512, 128), BF),
            one,
            one, one, one, one, one, one,
            one, one, one, one,
            dma((16,)), one, two, one, dma((2, 2)), dma((2, 2)), dma((2, 2)), dma((2, 2)), two, two,
            dma((4, 2)), four, four, four, dma((4, 2, 2)), dma((4, 2, 2)), dma((4, 2)), dma((4, 2)), four, four,
            two, two, two, two, two, two, four, four,
        ],
        compiler_params=pltpu.CompilerParams(
            collective_id=0, has_side_effects=True, vmem_limit_bytes=56 * 1024 * 1024
        ),
    )(ao_order, density, virt_coeff, block_coeff)


def solution(mesh):
    return jax.shard_map(
        shards,
        mesh=mesh,
        in_specs=(P("virt", "ao", None), P("virt", None), P("ao", None), P()),
        out_specs=P("ao", "virt", None),
        check_vma=False,
    )
```
